256 devices in a mesh: dom: 16 (over z, core), st: 16 (over x, y).
Axes of the slice: x: 4, y: 4, z: 8, core: 2. Of those that a mesh axis runs over, the one named last changes fastest.
Arguments:
- inv_sqrt_blocks: bfloat16 [1024, 8, 128, 128], P('dom'), may hold values from -0.1875 to 0.1875
- waves: bfloat16 [512, 131072], P('st', 'dom'), may hold values from -0.59765625 to 0.59765625
- occupation: float32 [512], P('st'), may hold values from 0 to 2
- block_ref: int32 [1024, 8], P('dom'), may hold values from 0 to 127, as said below
- row_count: int32 [1024], P('dom'), may hold values from 2 to 8
- send_list: int32 [16, 4, 16], P('dom'), may hold values from 0 to 63
Outputs:
- density: float32 [1024, 8, 128, 128], P('dom', None, 'st')
The draws below stay inside these ranges and needn't reach their ends.
Inputs may be any that keep to these rules, and one draw needn't show every extreme that they name: `block_ref`: slot 0 names the row's own block, slot 1 another block of the same domain, slots 2 and on codes 64 and above of blocks received from neighbouring domains.
All inputs are finite; a program needn't handle non-finite values.
Results may differ from the reference program's by a relative error of at most 0.0037.
Values may be sent and summed in bfloat16 or wider, within the bound.
No kernel may reach another device: no remote copies, remote signals or barrier semaphores. Data moves between devices by JAX's collectives and lax.ppermute only.
A program may use at most 192 MiB of HBM per device.

```python
import jax
import jax.numpy as jnp
from jax import lax

BLOCK = 128
K = 8
NEIGH = 4
STATES = 512
NB_DEV = 64
MAXSEND = 16
DOMAINS = 16
RECV = 64
NBLK = 1024


def draw_block_ref(key, part):
    rows = jnp.arange(NBLK, dtype=jnp.int32)
    local = rows % NB_DEV
    domain = rows // NB_DEV
    offset = jax.random.randint(jax.random.fold_in(key, 1), (NBLK,), 1, NB_DEV)
    second = (local + offset) % NB_DEV
    scores = jax.random.randint(jax.random.fold_in(key, 2), (DOMAINS, RECV), 0, 4096) * RECV + jnp.arange(RECV, dtype=jnp.int32)[None, :]
    order = jnp.argsort(scores, axis=1).astype(jnp.int32)
    position = (local[:, None] * (K - 2) + jnp.arange(K - 2, dtype=jnp.int32)[None, :]) % RECV
    remote = NB_DEV + order[domain[:, None], position]
    return jnp.concatenate([local[:, None], second[:, None], remote], axis=1).astype(jnp.int32)


def place_ends(values, own_key, low, top_value):
    longest = values.shape.index(max(values.shape))
    spots = []
    for shift in (0, 1):
        where = [jax.random.randint(jax.random.fold_in(own_key, axis), (), 0, length) for axis, length in enumerate(values.shape)]
        where[longest] = (where[longest] + shift) % values.shape[longest]
        spots.append(tuple(where))
    return values.at[spots[0]].set(low).at[spots[1]].set(top_value)


def steps_of(own_key, dims, cuts, smallest, high):
    def one(dim, blocks):
        draws = jax.random.uniform(jax.random.fold_in(jax.random.fold_in(own_key, 6), dim), (blocks,), jnp.float32, smallest / len(cuts), high / len(cuts))
        return jnp.repeat(jnp.exp(draws), dims[dim] // blocks).reshape((-1,) + (1,) * (len(dims) - dim - 1))

    loudness = one(*cuts[0])
    for cut in cuts[1:]:
        loudness = loudness * one(*cut)
    return loudness


def bell_draw(key, shape, scale, reach, split=(), kind=jnp.bfloat16):
    drawn = scale * jax.random.normal(key, shape, jnp.float32)
    if split:
        drawn = drawn * steps_of(key, shape, split, -0.22, 0.18)
    return jnp.clip(drawn, -reach, reach).astype(kind)


def setup_inputs(seed: int = 0) -> dict:
    streams_of = jax.random.split(jax.random.key(seed), 7)
    return {
        "inv_sqrt_blocks": bell_draw(streams_of[0], (NBLK, K, BLOCK, BLOCK), (K * BLOCK) ** -0.5, 0.1875, ((0, 16),)),
        "waves": bell_draw(streams_of[1], (STATES, NBLK * BLOCK), 0.1, 0.59765625, ((0, 16), (1, 16))),
        "occupation": jnp.clip(2.0 * jax.random.uniform(streams_of[2], (STATES,), jnp.float32) ** steps_of(streams_of[2], (STATES,), ((0, 16),), -0.2, 0.2), 0.0, 2.0),
        "block_ref": draw_block_ref(jax.random.fold_in(streams_of[6], 71), 0),
        "row_count": place_ends(jax.random.randint(streams_of[4], (NBLK,), 2, K + 1), jax.random.fold_in(streams_of[4], 1), 2, K).astype(jnp.int32),
        "send_list": place_ends(jax.random.randint(streams_of[5], (DOMAINS, NEIGH, MAXSEND), 0, NB_DEV), jax.random.fold_in(streams_of[5], 1), 0, NB_DEV - 1).astype(jnp.int32),
    }


neighbour_offsets = (-2, -1, 1, 2)

def column_blocks(block_ref, send_list):
    offsets = jnp.array(neighbour_offsets, dtype=jnp.int32)
    domain = (jnp.arange(NBLK, dtype=jnp.int32) // NB_DEV)[:, None]
    remote = jnp.maximum(block_ref - NB_DEV, 0)
    neighbour = remote // MAXSEND
    position = remote % MAXSEND
    source = (domain - offsets[neighbour] + DOMAINS) % DOMAINS
    far = source * NB_DEV + send_list[source, neighbour, position]
    return jnp.where(block_ref < NB_DEV, domain * NB_DEV + block_ref, far).astype(jnp.int32)

def reference(inv_sqrt_blocks, waves, occupation, block_ref, row_count, send_list):
    column = column_blocks(block_ref, send_list)
    live = jnp.arange(K, dtype=jnp.int32)[None, :] < row_count[:, None]
    blocked = waves.reshape(STATES, NBLK, BLOCK)

    def coef_domain(domain):
        first = (domain * NB_DEV).astype(jnp.int32)
        cols = lax.dynamic_slice(column, (first, jnp.int32(0)), (NB_DEV, K))
        alive = lax.dynamic_slice(live, (first, jnp.int32(0)), (NB_DEV, K))
        blocks = lax.dynamic_slice(inv_sqrt_blocks, (first, jnp.int32(0), jnp.int32(0), jnp.int32(0)), (NB_DEV, K, BLOCK, BLOCK))
        operand = blocked[:, cols].astype(jnp.float32) * alive[None, :, :, None].astype(jnp.float32)
        return jnp.einsum('sikc,ikrc->sir', operand, blocks.astype(jnp.float32)).astype(jnp.bfloat16)
    coef_parts = lax.map(coef_domain, jnp.arange(DOMAINS, dtype=jnp.int32))
    coef = jnp.transpose(coef_parts, (1, 0, 2, 3)).reshape(STATES, NBLK, BLOCK)
    weighted = (occupation[:, None, None] * coef.astype(jnp.float32)).astype(jnp.bfloat16)

    def density_domain(domain):
        first = (domain * NB_DEV).astype(jnp.int32)
        cols = lax.dynamic_slice(column, (first, jnp.int32(0)), (NB_DEV, K))
        alive = lax.dynamic_slice(live, (first, jnp.int32(0)), (NB_DEV, K))
        rows_here = lax.dynamic_slice_in_dim(weighted, first, NB_DEV, 1).astype(jnp.float32)
        partner = coef[:, cols].astype(jnp.float32)
        dens = jnp.einsum('sir,sikc->ikrc', rows_here, partner)
        return dens * alive[:, :, None, None].astype(jnp.float32)
    dens_parts = lax.map(density_domain, jnp.arange(DOMAINS, dtype=jnp.int32))
    return dens_parts.reshape(NBLK, K, BLOCK, BLOCK)
```

```python
import jax
import jax.numpy as jnp
from jax import lax
from jax.experimental import pallas as pl
from jax.experimental.pallas import tpu as pltpu
from jax.sharding import PartitionSpec as P

OFFSETS = (-2, -1, 1, 2)
SIDE = 4
BF16, F32 = jnp.bfloat16, jnp.float32
VMEM_LIMIT = 48 * 1024 * 1024


def params(**more):
    return pltpu.CompilerParams(vmem_limit_bytes=VMEM_LIMIT, **more)


def cost(flops, moved):
    return pl.CostEstimate(flops=flops, bytes_accessed=moved, transcendentals=0)


def along_dom(value, by):
    return lax.ppermute(value, "dom", [(i, (i + by) % 16) for i in range(16)])


def along_x(value, by):
    pairs = [(SIDE * x + y, SIDE * ((x + by) % SIDE) + y) for x in range(SIDE) for y in range(SIDE)]
    return lax.ppermute(value, "st", pairs)


def along_y(value, by):
    pairs = [(SIDE * x + y, SIDE * x + (y + by) % SIDE) for x in range(SIDE) for y in range(SIDE)]
    return lax.ppermute(value, "st", pairs)


def pick_waves(waves, send_list):
    def kernel(send_ref, waves_ref, *outs):
        for n in range(4):
            for j in range(16):
                block = send_ref[n, j]
                outs[n][j] = waves_ref[:, pl.ds(pl.multiple_of(block * 128, 128), 128)]

    piece = jax.ShapeDtypeStruct((16, 32, 128), BF16)
    return pl.pallas_call(
        kernel,
        out_shape=[piece] * 4,
        in_specs=[
            pl.BlockSpec(memory_space=pltpu.SMEM),
            pl.BlockSpec(memory_space=pltpu.VMEM),
        ],
        out_specs=[pl.BlockSpec(memory_space=pltpu.VMEM)] * 4,
        compiler_params=params(),
        name="pick_waves",
    )(send_list, waves)


NT = (((1,), (1,)), ((), ()))
ROWS = 16


def coef_own(inv_sqrt_blocks, waves, block_ref):
    def kernel(ref_ref, blocks_ref, waves_ref, out_ref):
        step = pl.program_id(0)
        for b in range(ROWS):
            i = step * ROWS + b
            operand = jnp.concatenate(
                [
                    waves_ref[:, pl.ds(pl.multiple_of(ref_ref[i, k] * 128, 128), 128)]
                    for k in range(2)
                ],
                axis=1,
            )
            factor = jnp.concatenate([blocks_ref[b, 0], blocks_ref[b, 1]], axis=1)
            out_ref[b] = lax.dot_general(operand, factor, NT, preferred_element_type=F32)

    return pl.pallas_call(
        kernel,
        grid=(64 // ROWS,),
        out_shape=jax.ShapeDtypeStruct((64, 32, 128), F32),
        in_specs=[
            pl.BlockSpec(memory_space=pltpu.SMEM),
            pl.BlockSpec((ROWS, 2, 128, 128), lambda i: (i, 0, 0, 0)),
            pl.BlockSpec((32, 8192), lambda i: (0, 0)),
        ],
        out_specs=pl.BlockSpec((ROWS, 32, 128), lambda i: (i, 0, 0)),
        compiler_params=params(),
        cost_estimate=cost(2 * 64 * 2 * 32 * 128 * 128, 6 * 1024 * 1024),
        name="coef_own",
    )(block_ref, inv_sqrt_blocks, waves)


def coef_all(inv_sqrt_blocks, first, pieces, block_ref, row_count, send_list, occupation):
    def kernel(
        ref_ref, count_ref, send_ref, blocks_ref, first_ref, occ_ref,
        p0, p1, p2, p3, coef_ref, o0, o1, o2, o3, table, total,
    ):
        step, pair = pl.program_id(0), pl.program_id(1)

        @pl.when((step == 0) & (pair == 0))
        def _():
            for n, piece in enumerate((p0, p1, p2, p3)):
                table[16 * n : 16 * n + 16] = piece[...]
            lane = lax.broadcasted_iota(jnp.int32, (32, 128), 1)
            occ = jnp.broadcast_to(occ_ref[...], (32, 128))
            high = occ.astype(BF16).astype(F32)
            middle = (occ - high).astype(BF16).astype(F32)
            low = occ - high - middle
            parts = jnp.where(lane == 0, high, jnp.where(lane == 1, middle, low))
            coef_ref[64] = jnp.where(lane < 3, parts, 0.0).astype(BF16)

        for b in range(ROWS):
            i = step * ROWS + b
            operands = []
            for k in range(2):
                slot = 2 + 2 * pair + k
                code = jnp.clip(ref_ref[i, slot] - 64, 0, 63)
                block = table[code]
                operands.append(jnp.where(slot < count_ref[0, i], block, jnp.zeros_like(block)))
            operand = jnp.concatenate(operands, axis=1)
            factor = jnp.concatenate([blocks_ref[b, 0], blocks_ref[b, 1]], axis=1)
            term = lax.dot_general(operand, factor, NT, preferred_element_type=F32)

            @pl.when(pair == 0)
            def _():
                total[b] = first_ref[b] + term

            @pl.when(pair == 1)
            def _():
                total[b] = total[b] + term

            @pl.when(pair == 2)
            def _():
                coef_ref[i] = (total[b] + term).astype(BF16)

        @pl.when((step == 64 // ROWS - 1) & (pair == 2))
        def _():
            for n, out in enumerate((o0, o1, o2, o3)):
                for j in range(16):
                    out[j] = coef_ref[send_ref[n, j]]

    piece = jax.ShapeDtypeStruct((16, 32, 128), BF16)
    whole = pl.BlockSpec((16, 32, 128), lambda i, k: (0, 0, 0))
    smem = pl.BlockSpec(memory_space=pltpu.SMEM)
    return pl.pallas_call(
        kernel,
        grid=(64 // ROWS, 3),
        out_shape=[jax.ShapeDtypeStruct((65, 32, 128), BF16)] + [piece] * 4,
        in_specs=[
            smem,
            smem,
            smem,
            pl.BlockSpec((ROWS, 2, 128, 128), lambda i, k: (i, k + 1, 0, 0)),
            pl.BlockSpec((ROWS, 32, 128), lambda i, k: (i, 0, 0)),
            pl.BlockSpec((32, 1), lambda i, k: (0, 0)),
        ]
        + [whole] * 4,
        out_specs=[pl.BlockSpec((65, 32, 128), lambda i, k: (0, 0, 0))] + [whole] * 4,
        scratch_shapes=[pltpu.VMEM((64, 32, 128), BF16), pltpu.VMEM((ROWS, 32, 128), F32)],
        compiler_params=params(),
        cost_estimate=cost(2 * 64 * 6 * 32 * 128 * 128, 14 * 1024 * 1024),
        name="coef_all",
    )(block_ref, row_count, send_list, inv_sqrt_blocks, first, occupation, *pieces)


def gathered(value):
    lower_y, lower_x = along_y(value, 1), along_x(value, 1)
    higher_y, higher_x = along_y(value, -1), along_x(value, -1)
    far_y = along_y(lower_y[:32], 1), along_y(higher_y[32:], -1)
    far_x = along_x(lower_x[:32], 1), along_x(higher_x[32:], -1)
    return (lower_y, higher_y, *far_y), (lower_x, higher_x, *far_x)


HALF = jax.ShapeDtypeStruct((4, 32, 16, 128), BF16)
KEPT = jax.ShapeDtypeStruct((4, 32, 16, 128), F32)
PARTS = [KEPT, HALF, HALF, HALF]


def product(weighted, low, high):
    both = jnp.dot(weighted, jnp.concatenate([low, high], axis=1), preferred_element_type=F32)
    for t in range(4):
        rows = both[8 * t : 8 * t + 8]
        yield jnp.concatenate([rows[:, :128], rows[:, 128:]], axis=0)


def density_own(here, coef, gathered_y, gathered_x, block_ref):
    def kernel(here_ref, ref_ref, own, ly, hy, fy0, fy1, lx, hx, fx0, fx1, w_ref, *rest):
        outs, (oy, ox, turned) = rest[:8], rest[8:]
        x, y = here_ref[0], here_ref[1]
        oy[0:32], oy[32:65] = fy0[...], fy1[...]
        ox[0:32], ox[32:65] = fx0[...], fx1[...]
        for v, sources in enumerate(((own, ly, hy, oy), (own, lx, hx, ox))):

            def block_of(c, sources=sources):
                return jnp.concatenate([s[c] for s in sources], axis=0)

            split = block_of(64).astype(F32)
            occ = split[:, 0:1] + split[:, 1:2] + split[:, 2:3]

            def row(i, carry, v=v, occ=occ, block_of=block_of):
                mine = block_of(32 * v + i)
                weighted = (occ * mine.astype(F32)).astype(BF16).astype(F32)
                turned[i % 2] = weighted.T
                groups = []
                for t in range(4):
                    group = SIDE * lax.rem(x + t, SIDE) + y if v == 0 else SIDE * x + lax.rem(y + t, SIDE)
                    groups.append(turned[i % 2, pl.ds(pl.multiple_of(group * 8, 8), 8)])
                lhs = jnp.concatenate(groups, axis=0).astype(BF16)
                w_ref[32 * v + i] = lhs
                other = block_of(jnp.clip(ref_ref[32 * v + i, 1], 0, 63))
                own_block = block_of(jnp.clip(ref_ref[32 * v + i, 0], 0, 63))
                for t, part in enumerate(product(lhs, own_block, other)):
                    outs[4 * v + t][0, i] = part.astype(outs[4 * v + t].dtype)
                return carry

            lax.fori_loop(0, 32, row, 0, unroll=4)

    smem, vmem = pl.BlockSpec(memory_space=pltpu.SMEM), pl.BlockSpec(memory_space=pltpu.VMEM)
    full = pl.BlockSpec((65, 32, 128), lambda i: (0, 0, 0))
    lower = pl.BlockSpec((32, 32, 128), lambda i: (0, 0, 0))
    upper = pl.BlockSpec((33, 32, 128), lambda i: (0, 0, 0))
    return pl.pallas_call(
        kernel,
        grid=(1,),
        out_shape=[jax.ShapeDtypeStruct((64, 32, 128), BF16)] + PARTS * 2,
        in_specs=[smem, smem, full] + [full, full, lower, upper] * 2,
        out_specs=[pl.BlockSpec((64, 32, 128), lambda i: (0, 0, 0))]
        + [pl.BlockSpec((1, 32, 16, 128), lambda i: (0, 0, 0, 0))] * 8,
        scratch_shapes=[
            pltpu.VMEM((65, 32, 128), BF16),
            pltpu.VMEM((65, 32, 128), BF16),
            pltpu.VMEM((2, 128, 128), F32),
        ],
        compiler_params=params(),
        cost_estimate=cost(2 * 64 * 2 * 128 * 32 * 128, 7 * 1024 * 1024),
        name="density_own",
    )(here, block_ref, coef, *gathered_y, *gathered_x)


def density_rest(weighted, halo, halo_y, halo_x, block_ref, begun):
    def kernel(ref_ref, w_ref, own, ly, hy, fy0, fy1, lx, hx, fx0, fx1, *rest):
        outs, (oy, ox) = rest[8:16], rest[16:]
        pair = pl.program_id(0)

        @pl.when(pair == 0)
        def _():
            oy[0:32], oy[32:64] = fy0[...], fy1[...]
            ox[0:32], ox[32:64] = fx0[...], fx1[...]

        for v, sources in enumerate(((own, ly, hy, oy), (own, lx, hx, ox))):

            def block_of(i, slot, sources=sources):
                c = jnp.clip(ref_ref[i, slot] - 64, 0, 63)
                return jnp.concatenate([s[c] for s in sources], axis=0)

            def row(i, carry, v=v, block_of=block_of):
                first = block_of(32 * v + i, 2 + 2 * pair)
                second = block_of(32 * v + i, 3 + 2 * pair)
                for t, part in enumerate(product(w_ref[32 * v + i], first, second)):
                    outs[4 * v + t][0, i] = part.astype(outs[4 * v + t].dtype)
                return carry

            lax.fori_loop(0, 32, row, 0, unroll=8)

    smem = pl.BlockSpec(memory_space=pltpu.SMEM)
    full = pl.BlockSpec((64, 32, 128), lambda i: (0, 0, 0))
    lower = pl.BlockSpec((32, 32, 128), lambda i: (0, 0, 0))
    return pl.pallas_call(
        kernel,
        grid=(3,),
        out_shape=PARTS * 2,
        in_specs=[smem, full, full] + [full, full, lower, lower] * 2 + [pl.BlockSpec(memory_space=pl.ANY)] * 8,
        out_specs=[pl.BlockSpec((1, 32, 16, 128), lambda i: (i + 1, 0, 0, 0))] * 8,
        scratch_shapes=[pltpu.VMEM((64, 32, 128), BF16), pltpu.VMEM((64, 32, 128), BF16)],
        input_output_aliases={11 + n: n for n in range(8)},
        compiler_params=params(),
        cost_estimate=cost(2 * 64 * 6 * 128 * 32 * 128, 10 * 1024 * 1024),
        name="density_rest",
    )(block_ref, weighted, halo, *halo_y, *halo_x, *begun)


def finish(parts, row_count):
    rows = 8

    def kernel(count_ref, *refs):
        ins, out_ref = refs[:8], refs[8]
        step = pl.program_id(0)
        for v in range(2):

            @pl.when(step // (32 // rows) == v)
            def _():
                for pair in range(4):
                    value = ins[4 * v][pair]
                    for t in range(1, 4):
                        value = value + ins[4 * v + t][pair].astype(F32)
                    for b in range(rows):
                        count = count_ref[0, step * rows + b]
                        for k in range(2):
                            part = value[b, 8 * k : 8 * k + 8]
                            out_ref[b, 2 * pair + k] = jnp.where(2 * pair + k < count, part, jnp.zeros_like(part))

    per = 32 // rows
    low = pl.BlockSpec((4, rows, 16, 128), lambda i: (0, jnp.minimum(i, per - 1), 0, 0))
    high = pl.BlockSpec((4, rows, 16, 128), lambda i: (0, jnp.maximum(i - per, 0), 0, 0))
    return pl.pallas_call(
        kernel,
        grid=(64 // rows,),
        out_shape=jax.ShapeDtypeStruct((64, 8, 8, 128), F32),
        in_specs=[pl.BlockSpec(memory_space=pltpu.SMEM)] + [low] * 4 + [high] * 4,
        out_specs=pl.BlockSpec((rows, 8, 8, 128), lambda i: (i, 0, 0, 0)),
        compiler_params=params(),
        cost_estimate=cost(0, 7 * 1024 * 1024),
        name="finish",
    )(row_count, *parts)


def body(inv_sqrt_blocks, waves, occupation, block_ref, row_count, send_list):
    send = send_list[0]
    count = row_count.reshape(1, 64)
    st = lax.axis_index("st")
    here = jnp.stack([st // SIDE, st % SIDE]).astype(jnp.int32)

    picked = pick_waves(waves, send)
    pieces = [along_dom(p, offset) for p, offset in zip(picked, OFFSETS)]
    first = coef_own(inv_sqrt_blocks, waves, block_ref)
    coef, *outgoing = coef_all(
        inv_sqrt_blocks, first, pieces, block_ref, count, send, occupation.reshape(32, 1)
    )
    own_y, own_x = gathered(coef)
    halo = jnp.concatenate([along_dom(p, offset) for p, offset in zip(outgoing, OFFSETS)], axis=0)
    halo_y, halo_x = gathered(halo)
    weighted, *begun = density_own(here, coef, own_y, own_x, block_ref)
    parts = density_rest(weighted, halo, halo_y, halo_x, block_ref, begun)
    arrived = []
    for v, along in enumerate((along_x, along_y)):
        arrived.append(parts[4 * v])
        arrived += [along(parts[4 * v + t], t) for t in range(1, 4)]
    return finish(arrived, count)


def solution(mesh):
    in_specs = (
        P("dom", None, None, None),
        P("st", "dom"),
        P("st"),
        P("dom", None),
        P("dom"),
        P("dom", None, None),
    )
    out_specs = P("dom", None, "st", None)
    return jax.shard_map(body, mesh=mesh, in_specs=in_specs, out_specs=out_specs, check_vma=False)
```

```python
import jax
import jax.numpy as jnp
from jax import lax
from jax.experimental import pallas as pl
from jax.experimental.pallas import tpu as pltpu
from jax.sharding import PartitionSpec as P

OFFSETS = (-2, -1, 1, 2)
SIDE = 4
BF16, F32 = jnp.bfloat16, jnp.float32
VMEM_LIMIT = 32 * 1024 * 1024


def params(**more):
    return pltpu.CompilerParams(vmem_limit_bytes=VMEM_LIMIT, **more)


def cost(flops, moved):
    return pl.CostEstimate(flops=flops, bytes_accessed=moved, transcendentals=0)


def along_dom(value, by):
    return lax.ppermute(value, "dom", [(i, (i + by) % 16) for i in range(16)])


def along_x(value, by):
    pairs = [(SIDE * x + y, SIDE * ((x + by) % SIDE) + y) for x in range(SIDE) for y in range(SIDE)]
    return lax.ppermute(value, "st", pairs)


def along_y(value, by):
    pairs = [(SIDE * x + y, SIDE * x + (y + by) % SIDE) for x in range(SIDE) for y in range(SIDE)]
    return lax.ppermute(value, "st", pairs)


def pick_waves(waves, send_list):
    def kernel(send_ref, waves_ref, *outs):
        for n in range(4):
            for j in range(16):
                block = send_ref[n, j]
                outs[n][j] = waves_ref[:, pl.ds(pl.multiple_of(block * 128, 128), 128)]

    piece = jax.ShapeDtypeStruct((16, 32, 128), BF16)
    return pl.pallas_call(
        kernel,
        out_shape=[piece] * 4,
        in_specs=[
            pl.BlockSpec(memory_space=pltpu.SMEM),
            pl.BlockSpec(memory_space=pltpu.VMEM),
        ],
        out_specs=[pl.BlockSpec(memory_space=pltpu.VMEM)] * 4,
        compiler_params=params(),
        name="pick_waves",
    )(send_list, waves)


NT = (((1,), (1,)), ((), ()))
ROWS = 16
OWN_ROWS = 32


def coef_own(inv_sqrt_blocks, waves, block_ref):
    def kernel(ref_ref, blocks_ref, waves_ref, out_ref):
        step = pl.program_id(0)
        for b in range(OWN_ROWS):
            i = step * OWN_ROWS + b
            operand = jnp.concatenate(
                [
                    waves_ref[:, pl.ds(pl.multiple_of(ref_ref[i, k] * 128, 128), 128)]
                    for k in range(2)
                ],
                axis=1,
            )
            factor = jnp.concatenate([blocks_ref[b, 0], blocks_ref[b, 1]], axis=1)
            out_ref[b] = lax.dot_general(operand, factor, NT, preferred_element_type=F32)

    return pl.pallas_call(
        kernel,
        grid=(64 // OWN_ROWS,),
        out_shape=jax.ShapeDtypeStruct((64, 32, 128), F32),
        in_specs=[
            pl.BlockSpec(memory_space=pltpu.SMEM),
            pl.BlockSpec((OWN_ROWS, 2, 128, 128), lambda i: (i, 0, 0, 0)),
            pl.BlockSpec((32, 8192), lambda i: (0, 0)),
        ],
        out_specs=pl.BlockSpec((OWN_ROWS, 32, 128), lambda i: (i, 0, 0)),
        compiler_params=params(),
        cost_estimate=cost(2 * 64 * 2 * 32 * 128 * 128, 6 * 1024 * 1024),
        name="coef_own",
    )(block_ref, inv_sqrt_blocks, waves)


def coef_all(inv_sqrt_blocks, first, pieces, block_ref, row_count, send_list, occupation):
    def kernel(
        ref_ref, count_ref, send_ref, blocks_1, blocks_2, blocks_3, first_ref, occ_ref,
        p0, p1, p2, p3, coef_ref, o0, o1, o2, o3, table,
    ):
        step = pl.program_id(0)

        @pl.when(step == 0)
        def _():
            for n, piece in enumerate((p0, p1, p2, p3)):
                table[16 * n : 16 * n + 16] = piece[...]
            lane = lax.broadcasted_iota(jnp.int32, (32, 128), 1)
            occ = jnp.broadcast_to(occ_ref[...], (32, 128))
            high = occ.astype(BF16).astype(F32)
            middle = (occ - high).astype(BF16).astype(F32)
            low = occ - high - middle
            parts = jnp.where(lane == 0, high, jnp.where(lane == 1, middle, low))
            coef_ref[64] = jnp.where(lane < 3, parts, 0.0).astype(BF16)

        for b in range(ROWS):
            i = step * ROWS + b
            operands, factors = [], []
            for slot in range(2, 8):
                block = table[jnp.clip(ref_ref[i, slot] - 64, 0, 63)]
                operands.append(jnp.where(slot < count_ref[0, i], block, jnp.zeros_like(block)))
                factors.append((blocks_1, blocks_2, blocks_3)[slot // 2 - 1][b, slot % 2])
            term = lax.dot_general(
                jnp.concatenate(factors, axis=1),
                jnp.concatenate(operands, axis=1),
                NT,
                preferred_element_type=F32,
            )
            coef_ref[i] = (first_ref[b] + term.T).astype(BF16)

        @pl.when(step == 64 // ROWS - 1)
        def _():
            for n, out in enumerate((o0, o1, o2, o3)):
                for j in range(16):
                    out[j] = coef_ref[send_ref[n, j]]

    piece = jax.ShapeDtypeStruct((16, 32, 128), BF16)
    whole = pl.BlockSpec((16, 32, 128), lambda i: (0, 0, 0))
    smem = pl.BlockSpec(memory_space=pltpu.SMEM)
    return pl.pallas_call(
        kernel,
        grid=(64 // ROWS,),
        out_shape=[jax.ShapeDtypeStruct((65, 32, 128), BF16)] + [piece] * 4,
        in_specs=[smem, smem, smem]
        + [pl.BlockSpec((ROWS, 2, 128, 128), lambda i, k=k: (i, k, 0, 0)) for k in (1, 2, 3)]
        + [
            pl.BlockSpec((ROWS, 32, 128), lambda i: (i, 0, 0)),
            pl.BlockSpec((32, 1), lambda i: (0, 0)),
        ]
        + [whole] * 4,
        out_specs=[pl.BlockSpec((65, 32, 128), lambda i: (0, 0, 0))] + [whole] * 4,
        scratch_shapes=[pltpu.VMEM((64, 32, 128), BF16)],
        compiler_params=params(),
        cost_estimate=cost(2 * 64 * 6 * 32 * 128 * 128, 14 * 1024 * 1024),
        name="coef_all",
    )(
        block_ref, row_count, send_list, inv_sqrt_blocks, inv_sqrt_blocks, inv_sqrt_blocks,
        first, occupation, *pieces,
    )


def from_beside(value):
    return along_y(value, 1), along_y(value, -1), along_x(value, 1), along_x(value, -1)


def from_far(beside):
    lower_y, higher_y, lower_x, higher_x = beside
    far_y = along_y(lower_y[:32], 1), along_y(higher_y[32:], -1)
    far_x = along_x(lower_x[:32], 1), along_x(higher_x[32:], -1)
    return (lower_y, higher_y, *far_y), (lower_x, higher_x, *far_x)


def unite(table, pieces):
    own, lower, higher, far_0, far_1 = pieces
    for n, piece in enumerate((own, lower, higher)):
        table[:, 32 * n : 32 * n + 32] = piece[...]
    table[0:32, 96:128] = far_0[...]
    table[32 : table.shape[0], 96:128] = far_1[...]


HALF = jax.ShapeDtypeStruct((4, 32, 16, 128), BF16)
KEPT = jax.ShapeDtypeStruct((4, 32, 16, 128), F32)
PARTS = [KEPT, HALF, HALF, HALF]


def product(weighted, low, high):
    both = jnp.dot(weighted, jnp.concatenate([low, high], axis=1), preferred_element_type=F32)
    for t in range(4):
        rows = both[8 * t : 8 * t + 8]
        yield jnp.concatenate([rows[:, :128], rows[:, 128:]], axis=0)


def density_own(here, coef, gathered_y, gathered_x, block_ref):
    def kernel(here_ref, ref_ref, own, ly, hy, fy0, fy1, lx, hx, fx0, fx1, w_ref, *rest):
        outs, tables, turned = rest[:8], rest[8:10], rest[10]
        x, y = here_ref[0], here_ref[1]
        for v, pieces in enumerate(((own, ly, hy, fy0, fy1), (own, lx, hx, fx0, fx1))):
            table = tables[v]
            unite(table, pieces)
            split = table[64].astype(F32)
            occ = split[:, 0:1] + split[:, 1:2] + split[:, 2:3]

            for i in range(32):
                mine = table[32 * v + i]
                weighted = (occ * mine.astype(F32)).astype(BF16).astype(F32)
                turned[32 * v + i] = weighted.T

            for i in range(32):
                groups = []
                for t in range(4):
                    group = SIDE * lax.rem(x + t, SIDE) + y if v == 0 else SIDE * x + lax.rem(y + t, SIDE)
                    groups.append(turned[32 * v + i, pl.ds(pl.multiple_of(group * 8, 8), 8)])
                lhs = jnp.concatenate(groups, axis=0).astype(BF16)
                w_ref[32 * v + i] = lhs
                both = [table[jnp.clip(ref_ref[32 * v + i, k], 0, 63)] for k in range(2)]
                for t, part in enumerate(product(lhs, *both)):
                    outs[4 * v + t][0, i] = part.astype(outs[4 * v + t].dtype)

    smem, vmem = pl.BlockSpec(memory_space=pltpu.SMEM), pl.BlockSpec(memory_space=pltpu.VMEM)
    full = pl.BlockSpec((65, 32, 128), lambda i: (0, 0, 0))
    lower = pl.BlockSpec((32, 32, 128), lambda i: (0, 0, 0))
    upper = pl.BlockSpec((33, 32, 128), lambda i: (0, 0, 0))
    return pl.pallas_call(
        kernel,
        grid=(1,),
        out_shape=[jax.ShapeDtypeStruct((64, 32, 128), BF16)] + PARTS * 2,
        in_specs=[smem, smem, full] + [full, full, lower, upper] * 2,
        out_specs=[pl.BlockSpec((64, 32, 128), lambda i: (0, 0, 0))]
        + [pl.BlockSpec((1, 32, 16, 128), lambda i: (0, 0, 0, 0))] * 8,
        scratch_shapes=[
            pltpu.VMEM((65, 128, 128), BF16),
            pltpu.VMEM((65, 128, 128), BF16),
            pltpu.VMEM((64, 128, 128), F32),
        ],
        compiler_params=params(),
        cost_estimate=cost(2 * 64 * 2 * 128 * 32 * 128, 7 * 1024 * 1024),
        name="density_own",
    )(here, block_ref, coef, *gathered_y, *gathered_x)


def density_rest(weighted, halo, halo_y, halo_x, block_ref, begun):
    def kernel(ref_ref, w_ref, own, ly, hy, fy0, fy1, lx, hx, fx0, fx1, *rest):
        outs, tables = rest[8:16], rest[16:]
        pair = pl.program_id(0)

        @pl.when(pair == 0)
        def _():
            unite(tables[0], (own, ly, hy, fy0, fy1))
            unite(tables[1], (own, lx, hx, fx0, fx1))

        for v, table in enumerate(tables):
            for i in range(32):
                codes = [ref_ref[32 * v + i, 2 + 2 * pair + k] - 64 for k in range(2)]
                both = [table[jnp.clip(code, 0, 63)] for code in codes]
                for t, part in enumerate(product(w_ref[32 * v + i], *both)):
                    outs[4 * v + t][0, i] = part.astype(outs[4 * v + t].dtype)

    smem = pl.BlockSpec(memory_space=pltpu.SMEM)
    full = pl.BlockSpec((64, 32, 128), lambda i: (0, 0, 0))
    lower = pl.BlockSpec((32, 32, 128), lambda i: (0, 0, 0))
    return pl.pallas_call(
        kernel,
        grid=(3,),
        out_shape=PARTS * 2,
        in_specs=[smem, full, full] + [full, full, lower, lower] * 2 + [pl.BlockSpec(memory_space=pl.ANY)] * 8,
        out_specs=[pl.BlockSpec((1, 32, 16, 128), lambda i: (i + 1, 0, 0, 0))] * 8,
        scratch_shapes=[pltpu.VMEM((64, 128, 128), BF16)] * 2,
        input_output_aliases={11 + n: n for n in range(8)},
        compiler_params=params(),
        cost_estimate=cost(2 * 64 * 6 * 128 * 32 * 128, 10 * 1024 * 1024),
        name="density_rest",
    )(block_ref, weighted, halo, *halo_y, *halo_x, *begun)


def finish(parts, row_count):
    rows = 16

    def kernel(count_ref, *refs):
        ins, out_ref = refs[:8], refs[8]
        step = pl.program_id(0)
        for v in range(2):

            @pl.when(step // (32 // rows) == v)
            def _():
                for pair in range(4):
                    value = ins[4 * v][pair]
                    for t in range(1, 4):
                        value = value + ins[4 * v + t][pair].astype(F32)
                    for b in range(rows):
                        count = count_ref[0, step * rows + b]
                        for k in range(2):
                            part = value[b, 8 * k : 8 * k + 8]
                            out_ref[b, 2 * pair + k] = jnp.where(2 * pair + k < count, part, jnp.zeros_like(part))

    per = 32 // rows
    low = pl.BlockSpec((4, rows, 16, 128), lambda i: (0, jnp.minimum(i, per - 1), 0, 0))
    high = pl.BlockSpec((4, rows, 16, 128), lambda i: (0, jnp.maximum(i - per, 0), 0, 0))
    return pl.pallas_call(
        kernel,
        grid=(64 // rows,),
        out_shape=jax.ShapeDtypeStruct((64, 8, 8, 128), F32),
        in_specs=[pl.BlockSpec(memory_space=pltpu.SMEM)] + [low] * 4 + [high] * 4,
        out_specs=pl.BlockSpec((rows, 8, 8, 128), lambda i: (i, 0, 0, 0)),
        compiler_params=params(),
        cost_estimate=cost(0, 7 * 1024 * 1024),
        name="finish",
    )(row_count, *parts)


def body(inv_sqrt_blocks, waves, occupation, block_ref, row_count, send_list):
    send = send_list[0]
    count = row_count.reshape(1, 64)
    st = lax.axis_index("st")
    here = jnp.stack([st // SIDE, st % SIDE]).astype(jnp.int32)

    picked = pick_waves(waves, send)
    pieces = [along_dom(p, offset) for p, offset in zip(picked, OFFSETS)]
    first = coef_own(inv_sqrt_blocks, waves, block_ref)
    coef, *outgoing = coef_all(
        inv_sqrt_blocks, first, pieces, block_ref, count, send, occupation.reshape(32, 1)
    )
    beside = from_beside(coef)
    halos = [along_dom(p, offset) for p, offset in zip(outgoing[:2], OFFSETS)]
    *beside, third, fourth = lax.optimization_barrier((*beside, *outgoing[2:]))
    halos += [along_dom(p, offset) for p, offset in zip((third, fourth), OFFSETS[2:])]
    own_y, own_x = from_far(beside)
    halo = jnp.concatenate(halos, axis=0)
    halo_y, halo_x = from_far(from_beside(halo))
    weighted, *begun = density_own(here, coef, own_y, own_x, block_ref)
    parts = density_rest(weighted, halo, halo_y, halo_x, block_ref, begun)
    arrived = []
    for v, along in enumerate((along_x, along_y)):
        arrived.append(parts[4 * v])
        arrived += [along(parts[4 * v + t], t) for t in range(1, 4)]
    return finish(arrived, count)


def solution(mesh):
    in_specs = (
        P("dom", None, None, None),
        P("st", "dom"),
        P("st"),
        P("dom", None),
        P("dom"),
        P("dom", None, None),
    )
    out_specs = P("dom", None, "st", None)
    return jax.shard_map(body, mesh=mesh, in_specs=in_specs, out_specs=out_specs, check_vma=False)
```

```python
import jax
import jax.numpy as jnp
from jax import lax
from jax.experimental import pallas as pl
from jax.experimental.pallas import tpu as pltpu
from jax.sharding import PartitionSpec as P

LIST = 144
PAIRS = 32 + LIST // 2
OFFSETS = (-2, -1, 1, 2)
SIDE = 4
BF16, F32 = jnp.bfloat16, jnp.float32
VMEM_LIMIT = 32 * 1024 * 1024


def params(**more):
    return pltpu.CompilerParams(vmem_limit_bytes=VMEM_LIMIT, **more)


def cost(flops, moved):
    return pl.CostEstimate(flops=flops, bytes_accessed=moved, transcendentals=0)


def along_dom(value, by):
    return lax.ppermute(value, "dom", [(i, (i + by) % 16) for i in range(16)])


def along_x(value, by):
    pairs = [(SIDE * x + y, SIDE * ((x + by) % SIDE) + y) for x in range(SIDE) for y in range(SIDE)]
    return lax.ppermute(value, "st", pairs)


def along_y(value, by):
    pairs = [(SIDE * x + y, SIDE * x + (y + by) % SIDE) for x in range(SIDE) for y in range(SIDE)]
    return lax.ppermute(value, "st", pairs)


def pick_waves(waves, send_list):
    def kernel(send_ref, waves_ref, *outs):
        for n in range(4):
            for j in range(16):
                block = send_ref[n, j]
                outs[n][j] = waves_ref[:, pl.ds(pl.multiple_of(block * 128, 128), 128)]

    piece = jax.ShapeDtypeStruct((16, 32, 128), BF16)
    return pl.pallas_call(
        kernel,
        out_shape=[piece] * 4,
        in_specs=[
            pl.BlockSpec(memory_space=pltpu.SMEM),
            pl.BlockSpec(memory_space=pltpu.VMEM),
        ],
        out_specs=[pl.BlockSpec(memory_space=pltpu.VMEM)] * 4,
        compiler_params=params(),
        name="pick_waves",
    )(send_list, waves)


NT = (((1,), (1,)), ((), ()))
ROWS = 16
OWN_ROWS = 32


def coef_own(inv_sqrt_blocks, waves, block_ref):
    def kernel(ref_ref, blocks_ref, waves_ref, out_ref):
        step = pl.program_id(0)
        for b in range(OWN_ROWS):
            i = step * OWN_ROWS + b
            operand = jnp.concatenate(
                [
                    waves_ref[:, pl.ds(pl.multiple_of(ref_ref[i, k] * 128, 128), 128)]
                    for k in range(2)
                ],
                axis=1,
            )
            factor = jnp.concatenate([blocks_ref[b, 0], blocks_ref[b, 1]], axis=1)
            out_ref[b] = lax.dot_general(operand, factor, NT, preferred_element_type=F32)

    return pl.pallas_call(
        kernel,
        grid=(64 // OWN_ROWS,),
        out_shape=jax.ShapeDtypeStruct((64, 32, 128), F32),
        in_specs=[
            pl.BlockSpec(memory_space=pltpu.SMEM),
            pl.BlockSpec((OWN_ROWS, 2, 128, 128), lambda i: (i, 0, 0, 0)),
            pl.BlockSpec((32, 8192), lambda i: (0, 0)),
        ],
        out_specs=pl.BlockSpec((OWN_ROWS, 32, 128), lambda i: (i, 0, 0)),
        compiler_params=params(),
        cost_estimate=cost(2 * 64 * 2 * 32 * 128 * 128, 6 * 1024 * 1024),
        name="coef_own",
    )(block_ref, inv_sqrt_blocks, waves)


def coef_all(inv_sqrt_blocks, first, pieces, block_ref, row_count, send_list, occupation):
    def kernel(
        ref_ref, count_ref, send_ref, blocks_1, blocks_2, blocks_3, first_ref, occ_ref,
        p0, p1, p2, p3, coef_ref, o0, o1, o2, o3, table,
    ):
        step = pl.program_id(0)

        @pl.when(step == 0)
        def _():
            for n, piece in enumerate((p0, p1, p2, p3)):
                table[16 * n : 16 * n + 16] = piece[...]
            lane = lax.broadcasted_iota(jnp.int32, (32, 128), 1)
            occ = jnp.broadcast_to(occ_ref[...], (32, 128))
            high = occ.astype(BF16).astype(F32)
            middle = (occ - high).astype(BF16).astype(F32)
            low = occ - high - middle
            parts = jnp.where(lane == 0, high, jnp.where(lane == 1, middle, low))
            coef_ref[64] = jnp.where(lane < 3, parts, 0.0).astype(BF16)

        for b in range(ROWS):
            i = step * ROWS + b
            operands, factors = [], []
            for slot in range(2, 8):
                block = table[jnp.clip(ref_ref[i, slot] - 64, 0, 63)]
                operands.append(jnp.where(slot < count_ref[0, i], block, jnp.zeros_like(block)))
                factors.append((blocks_1, blocks_2, blocks_3)[slot // 2 - 1][b, slot % 2])
            term = lax.dot_general(
                jnp.concatenate(factors, axis=1),
                jnp.concatenate(operands, axis=1),
                NT,
                preferred_element_type=F32,
            )
            coef_ref[i] = (first_ref[b] + term.T).astype(BF16)

        @pl.when(step == 64 // ROWS - 1)
        def _():
            for n, out in enumerate((o0, o1, o2, o3)):
                for j in range(16):
                    out[j] = coef_ref[send_ref[n, j]]

    piece = jax.ShapeDtypeStruct((16, 32, 128), BF16)
    whole = pl.BlockSpec((16, 32, 128), lambda i: (0, 0, 0))
    smem = pl.BlockSpec(memory_space=pltpu.SMEM)
    return pl.pallas_call(
        kernel,
        grid=(64 // ROWS,),
        out_shape=[jax.ShapeDtypeStruct((65, 32, 128), BF16)] + [piece] * 4,
        in_specs=[smem, smem, smem]
        + [pl.BlockSpec((ROWS, 2, 128, 128), lambda i, k=k: (i, k, 0, 0)) for k in (1, 2, 3)]
        + [
            pl.BlockSpec((ROWS, 32, 128), lambda i: (i, 0, 0)),
            pl.BlockSpec((32, 1), lambda i: (0, 0)),
        ]
        + [whole] * 4,
        out_specs=[pl.BlockSpec((65, 32, 128), lambda i: (0, 0, 0))] + [whole] * 4,
        scratch_shapes=[pltpu.VMEM((64, 32, 128), BF16)],
        compiler_params=params(),
        cost_estimate=cost(2 * 64 * 6 * 32 * 128 * 128, 14 * 1024 * 1024),
        name="coef_all",
    )(
        block_ref, row_count, send_list, inv_sqrt_blocks, inv_sqrt_blocks, inv_sqrt_blocks,
        first, occupation, *pieces,
    )


def from_beside(value):
    return along_y(value, 1), along_y(value, -1), along_x(value, 1), along_x(value, -1)


def from_far(beside):
    lower_y, higher_y, lower_x, higher_x = beside
    far_y = along_y(lower_y[:32], 1), along_y(higher_y[32:], -1)
    far_x = along_x(lower_x[:32], 1), along_x(higher_x[32:], -1)
    return (lower_y, higher_y, *far_y), (lower_x, higher_x, *far_x)


def unite(table, pieces):
    own, lower, higher, far_0, far_1 = pieces
    for n, piece in enumerate((own, lower, higher)):
        table[:, 32 * n : 32 * n + 32] = piece[...]
    table[0:32, 96:128] = far_0[...]
    table[32 : table.shape[0], 96:128] = far_1[...]


HALF = jax.ShapeDtypeStruct((4, 32, 16, 128), BF16)
KEPT = jax.ShapeDtypeStruct((4, 32, 16, 128), F32)
PARTS = [KEPT, HALF, HALF, HALF]


def product(weighted, low, high):
    both = jnp.dot(weighted, jnp.concatenate([low, high], axis=1), preferred_element_type=F32)
    for t in range(4):
        rows = both[8 * t : 8 * t + 8]
        yield jnp.concatenate([rows[:, :128], rows[:, 128:]], axis=0)


def density_own(here, coef, gathered_y, gathered_x, block_ref):
    def kernel(here_ref, ref_ref, own, ly, hy, fy0, fy1, lx, hx, fx0, fx1, w_ref, *rest):
        outs, tables, turned = rest[:8], rest[8:10], rest[10]
        x, y = here_ref[0], here_ref[1]
        for v, pieces in enumerate(((own, ly, hy, fy0, fy1), (own, lx, hx, fx0, fx1))):
            table = tables[v]
            unite(table, pieces)
            split = table[64].astype(F32)
            occ = split[:, 0:1] + split[:, 1:2] + split[:, 2:3]

            for i in range(32):
                mine = table[32 * v + i]
                weighted = (occ * mine.astype(F32)).astype(BF16).astype(F32)
                turned[32 * v + i] = weighted.T

            for i in range(32):
                groups = []
                for t in range(4):
                    group = SIDE * lax.rem(x + t, SIDE) + y if v == 0 else SIDE * x + lax.rem(y + t, SIDE)
                    groups.append(turned[32 * v + i, pl.ds(pl.multiple_of(group * 8, 8), 8)])
                lhs = jnp.concatenate(groups, axis=0).astype(BF16)
                w_ref[32 * v + i] = lhs
                both = [table[jnp.clip(ref_ref[32 * v + i, k], 0, 63)] for k in range(2)]
                for t, part in enumerate(product(lhs, *both)):
                    outs[4 * v + t][0, i] = part.astype(outs[4 * v + t].dtype)

    smem, vmem = pl.BlockSpec(memory_space=pltpu.SMEM), pl.BlockSpec(memory_space=pltpu.VMEM)
    full = pl.BlockSpec((65, 32, 128), lambda i: (0, 0, 0))
    lower = pl.BlockSpec((32, 32, 128), lambda i: (0, 0, 0))
    upper = pl.BlockSpec((33, 32, 128), lambda i: (0, 0, 0))
    return pl.pallas_call(
        kernel,
        grid=(1,),
        out_shape=[jax.ShapeDtypeStruct((64, 32, 128), BF16)] + PARTS * 2,
        in_specs=[smem, smem, full] + [full, full, lower, upper] * 2,
        out_specs=[pl.BlockSpec((64, 32, 128), lambda i: (0, 0, 0))]
        + [pl.BlockSpec((1, 32, 16, 128), lambda i: (0, 0, 0, 0))] * 8,
        scratch_shapes=[
            pltpu.VMEM((65, 128, 128), BF16),
            pltpu.VMEM((65, 128, 128), BF16),
            pltpu.VMEM((64, 128, 128), F32),
        ],
        compiler_params=params(),
        cost_estimate=cost(2 * 64 * 2 * 128 * 32 * 128, 7 * 1024 * 1024),
        name="density_own",
    )(here, block_ref, coef, *gathered_y, *gathered_x)


def density_rest(weighted, halo, halo_y, halo_x, block_ref, begun):
    def kernel(ref_ref, w_ref, own, ly, hy, fy0, fy1, lx, hx, fx0, fx1, *rest):
        outs, tables = rest[8:16], rest[16:]
        pair = pl.program_id(0)

        @pl.when(pair == 0)
        def _():
            unite(tables[0], (own, ly, hy, fy0, fy1))
            unite(tables[1], (own, lx, hx, fx0, fx1))

        for v, table in enumerate(tables):
            for i in range(32):
                codes = [ref_ref[32 * v + i, 2 + 2 * pair + k] - 64 for k in range(2)]
                both = [table[jnp.clip(code, 0, 63)] for code in codes]
                for t, part in enumerate(product(w_ref[32 * v + i], *both)):
                    outs[4 * v + t][0, i] = part.astype(outs[4 * v + t].dtype)

    smem = pl.BlockSpec(memory_space=pltpu.SMEM)
    full = pl.BlockSpec((64, 32, 128), lambda i: (0, 0, 0))
    lower = pl.BlockSpec((32, 32, 128), lambda i: (0, 0, 0))
    return pl.pallas_call(
        kernel,
        grid=(3,),
        out_shape=PARTS * 2,
        in_specs=[smem, full, full] + [full, full, lower, lower] * 2 + [pl.BlockSpec(memory_space=pl.ANY)] * 8,
        out_specs=[pl.BlockSpec((1, 32, 16, 128), lambda i: (i + 1, 0, 0, 0))] * 8,
        scratch_shapes=[pltpu.VMEM((64, 128, 128), BF16)] * 2,
        input_output_aliases={11 + n: n for n in range(8)},
        compiler_params=params(),
        cost_estimate=cost(2 * 64 * 6 * 128 * 32 * 128, 10 * 1024 * 1024),
        name="density_rest",
    )(block_ref, weighted, halo, *halo_y, *halo_x, *begun)


def finish(parts, row_count):
    rows = 16

    def kernel(count_ref, *refs):
        ins, out_ref = refs[:8], refs[8]
        step = pl.program_id(0)
        for v in range(2):

            @pl.when(step // (32 // rows) == v)
            def _():
                for pair in range(4):
                    value = ins[4 * v][pair]
                    for t in range(1, 4):
                        value = value + ins[4 * v + t][pair].astype(F32)
                    for b in range(rows):
                        count = count_ref[0, step * rows + b]
                        for k in range(2):
                            part = value[b, 8 * k : 8 * k + 8]
                            out_ref[b, 2 * pair + k] = jnp.where(2 * pair + k < count, part, jnp.zeros_like(part))

    per = 32 // rows
    low = pl.BlockSpec((4, rows, 16, 128), lambda i: (0, jnp.minimum(i, per - 1), 0, 0))
    high = pl.BlockSpec((4, rows, 16, 128), lambda i: (0, jnp.maximum(i - per, 0), 0, 0))
    return pl.pallas_call(
        kernel,
        grid=(64 // rows,),
        out_shape=jax.ShapeDtypeStruct((64, 8, 8, 128), F32),
        in_specs=[pl.BlockSpec(memory_space=pltpu.SMEM)] + [low] * 4 + [high] * 4,
        out_specs=pl.BlockSpec((rows, 8, 8, 128), lambda i: (i, 0, 0, 0)),
        compiler_params=params(),
        cost_estimate=cost(0, 7 * 1024 * 1024),
        name="finish",
    )(row_count, *parts)


def plan(block_ref, row_count):
    room, none = 2 * PAIRS, 4 * PAIRS

    def kernel(ref_ref, count_ref, entry_ref, place_ref, over_ref):
        def clear(p, carry):
            entry_ref[0, p] = 0
            entry_ref[1, p] = 0
            return carry

        lax.fori_loop(0, LIST + 1, clear, 0, unroll=5)

        def row(i, lengths):
            count = count_ref[0, i]
            for k in range(2, 8):
                block = jnp.clip(ref_ref[i, k] - 64, 0, 63)
                which = block // 32
                long = jnp.where(which == 0, lengths[0], lengths[1])
                p = jnp.minimum(long, LIST)
                alive = (k < count).astype(jnp.int32)
                entry_ref[which, p] = i * 64 + block
                placed = (k < count) & (p < LIST)
                place_ref[i, k] = jnp.where(placed, which * room + 64 + p, none)
                lengths = (lengths[0] + alive * (1 - which), lengths[1] + alive * which)
            return lengths

        lengths = lax.fori_loop(0, 64, row, (jnp.int32(0), jnp.int32(0)), unroll=2)
        over_ref[0, 0] = (jnp.maximum(*lengths) > LIST).astype(jnp.int32)

    smem = pl.BlockSpec(memory_space=pltpu.SMEM)
    return pl.pallas_call(
        kernel,
        out_shape=[
            jax.ShapeDtypeStruct((2, LIST + 1), jnp.int32),
            jax.ShapeDtypeStruct((64, 8), jnp.int32),
            jax.ShapeDtypeStruct((1, 1), jnp.int32),
        ],
        in_specs=[smem, smem],
        out_specs=[smem] * 3,
        compiler_params=params(),
        cost_estimate=cost(0, 1024 * 1024),
        name="plan",
    )(block_ref, row_count)


def targets(here_ref, v):
    x, y = here_ref[0], here_ref[1]
    for t in range(4):
        yield SIDE * lax.rem(x + t, SIDE) + y if v == 0 else SIDE * x + lax.rem(y + t, SIDE)


def weigh(v, here, shards, block_ref):
    def kernel(here_ref, ref_ref, own, lower, higher, far, w_ref, *rest):
        outs, table, turned = rest[:4], rest[4], rest[5]
        for n, piece in enumerate((own, lower, higher, far)):
            table[:, 32 * n : 32 * n + 32] = piece[...]
        split = table[64].astype(F32)
        occ = split[:, 0:1] + split[:, 1:2] + split[:, 2:3]
        for i in range(64):
            turned[i] = (occ * table[i].astype(F32)).astype(BF16).astype(F32).T
        starts = [pl.multiple_of(group * 8, 8) for group in targets(here_ref, v)]
        for i in range(64):
            groups = [turned[i, pl.ds(start, 8)] for start in starts]
            w_ref[i] = jnp.concatenate(groups, axis=0).astype(BF16)
        for i in range(32):
            both = [table[jnp.clip(ref_ref[32 * v + i, k], 0, 63)] for k in range(2)]
            for t, part in enumerate(product(w_ref[32 * v + i], *both)):
                outs[t][i] = part.astype(outs[t].dtype)

    smem, vmem = pl.BlockSpec(memory_space=pltpu.SMEM), pl.BlockSpec(memory_space=pltpu.VMEM)
    part = (32, 16, 128)
    return pl.pallas_call(
        kernel,
        out_shape=[jax.ShapeDtypeStruct((64, 32, 128), BF16), jax.ShapeDtypeStruct(part, F32)]
        + [jax.ShapeDtypeStruct(part, BF16)] * 3,
        in_specs=[smem, smem] + [vmem] * 4,
        out_specs=[vmem] * 5,
        scratch_shapes=[pltpu.VMEM((65, 128, 128), BF16), pltpu.VMEM((64, 128, 128), F32)],
        compiler_params=params(),
        cost_estimate=cost(64 * 2 * 128 * 32 * 128, 4 * 1024 * 1024),
        name=f"weigh_{v}",
    )(here, block_ref, *shards)


def density_list(v, entries, weighted, shards, begun):
    def kernel(entry_ref, w_ref, own, lower, higher, far, *rest):
        begun_refs, outs, table = rest[:4], rest[4:8], rest[8]
        for n, piece in enumerate((own, lower, higher, far)):
            table[:, 32 * n : 32 * n + 32] = piece[...]
        for begun_ref, out in zip(begun_refs, outs):
            out[0:32] = begun_ref[...]
        for p in range(0, LIST, 2):
            halves = []
            for q in range(2):
                entry = entry_ref[v, p + q]
                weight, block = w_ref[lax.shift_right_logical(entry, 6)], table[entry & 31]
                halves.append(jnp.dot(weight, block, preferred_element_type=F32))
            for t, out in enumerate(outs):
                pair = jnp.concatenate([half[8 * t : 8 * t + 8] for half in halves], axis=0)
                out[32 + p // 2] = pair.astype(out.dtype)

    smem, vmem = pl.BlockSpec(memory_space=pltpu.SMEM), pl.BlockSpec(memory_space=pltpu.VMEM)
    part = (PAIRS, 16, 128)
    return pl.pallas_call(
        kernel,
        out_shape=[jax.ShapeDtypeStruct(part, F32)] + [jax.ShapeDtypeStruct(part, BF16)] * 3,
        in_specs=[smem] + [vmem] * 9,
        out_specs=[vmem] * 4,
        scratch_shapes=[pltpu.VMEM((32, 128, 128), BF16)],
        compiler_params=params(),
        cost_estimate=cost(LIST * 2 * 128 * 32 * 128, 4 * 1024 * 1024),
        name=f"density_list_{v}",
    )(entries, weighted, *shards, *begun)


def gather_up(parts, places):
    def kernel(place_ref, *refs):
        ins, out_ref, sums = refs[:8], refs[8], refs[9]
        for v in range(2):
            value = ins[4 * v][...]
            for t in range(1, 4):
                value = value + ins[4 * v + t][...].astype(F32)
            sums[2 * PAIRS * v : 2 * PAIRS * v + 2 * PAIRS] = value.reshape(2 * PAIRS, 8, 128)
        sums[4 * PAIRS] = jnp.zeros((8, 128), F32)
        for i in range(64):
            for k in range(2):
                out_ref[i, k] = sums[2 * PAIRS * (i // 32) + 2 * (i % 32) + k]
            for k in range(2, 8):
                out_ref[i, k] = sums[place_ref[i, k]]

    smem, vmem = pl.BlockSpec(memory_space=pltpu.SMEM), pl.BlockSpec(memory_space=pltpu.VMEM)
    return pl.pallas_call(
        kernel,
        out_shape=jax.ShapeDtypeStruct((64, 8, 8, 128), F32),
        in_specs=[smem] + [vmem] * 8,
        out_specs=vmem,
        scratch_shapes=[pltpu.VMEM((4 * PAIRS + 1, 8, 128), F32)],
        compiler_params=params(),
        cost_estimate=cost(0, 7 * 1024 * 1024),
        name="gather_up",
    )(places, *parts)


def scattered(parts_x, parts_y):
    arrived = []
    for parts, along in ((parts_x, along_x), (parts_y, along_y)):
        arrived.append(parts[0])
        arrived += [along(parts[t], t) for t in range(1, 4)]
    return arrived


def any_way(coef, halo, here, block_ref, count):
    own_y, own_x = from_far(from_beside(coef))
    halo_y, halo_x = from_far(from_beside(halo))
    weighted, *begun = density_own(here, coef, own_y, own_x, block_ref)
    parts = density_rest(weighted, halo, halo_y, halo_x, block_ref, begun)
    return finish(scattered(parts[:4], parts[4:]), count)


def body(inv_sqrt_blocks, waves, occupation, block_ref, row_count, send_list):
    send = send_list[0]
    count = row_count.reshape(1, 64)
    st = lax.axis_index("st")
    here = jnp.stack([st // SIDE, st % SIDE]).astype(jnp.int32)

    picked = pick_waves(waves, send)
    pieces = [along_dom(p, offset) for p, offset in zip(picked, OFFSETS)]
    first = coef_own(inv_sqrt_blocks, waves, block_ref)
    entries, places, over = plan(block_ref, count)
    coef, *outgoing = coef_all(
        inv_sqrt_blocks, first, pieces, block_ref, count, send, occupation.reshape(32, 1)
    )
    own_y = [coef] + [along_y(coef, by) for by in (1, -1, 2)]
    own_x = [coef] + [along_x(coef, by) for by in (1, -1, 2)]
    halos = [along_dom(p, offset) for p, offset in zip(outgoing, OFFSETS)]
    half_y = jnp.concatenate(halos[:2], axis=0)
    half_x = jnp.concatenate(halos[2:], axis=0)
    halo_y = [half_y] + [along_y(half_y, by) for by in (1, -1, 2)]
    halo_x = [half_x] + [along_x(half_x, by) for by in (1, -1, 2)]
    weighted_y, *begun_y = weigh(0, here, own_y, block_ref)
    weighted_x, *begun_x = weigh(1, here, own_x, block_ref)
    parts_x = density_list(0, entries, weighted_y, halo_y, begun_y)
    parts_y = density_list(1, entries, weighted_x, halo_x, begun_x)
    density = gather_up(scattered(parts_x, parts_y), places)

    def again(density, coef, halo, *rest):
        return any_way(coef, halo, *rest)

    def keep(density, *rest):
        return density

    halo = jnp.concatenate([half_y, half_x], axis=0)
    return lax.cond(over[0, 0] > 0, again, keep, density, coef, halo, here, block_ref, count)


def solution(mesh):
    in_specs = (
        P("dom", None, None, None),
        P("st", "dom"),
        P("st"),
        P("dom", None),
        P("dom"),
        P("dom", None, None),
    )
    out_specs = P("dom", None, "st", None)
    return jax.shard_map(body, mesh=mesh, in_specs=in_specs, out_specs=out_specs, check_vma=False)
```

```python
import jax
import jax.numpy as jnp
from jax import lax
from jax.experimental import pallas as pl
from jax.experimental.pallas import tpu as pltpu
from jax.sharding import PartitionSpec as P

LIST = 144
PAIRS = 32 + LIST // 2
OFFSETS = (-2, -1, 1, 2)
SIDE = 4
BF16, F32 = jnp.bfloat16, jnp.float32


def params(mib=32):
    return pltpu.CompilerParams(vmem_limit_bytes=mib * 1024 * 1024)


def cost(flops, moved):
    return pl.CostEstimate(flops=flops, bytes_accessed=moved, transcendentals=0)


def along_dom(value, by):
    return lax.ppermute(value, "dom", [(i, (i + by) % 16) for i in range(16)])


def along_x(value, by):
    pairs = [(SIDE * x + y, SIDE * ((x + by) % SIDE) + y) for x in range(SIDE) for y in range(SIDE)]
    return lax.ppermute(value, "st", pairs)


def along_y(value, by):
    pairs = [(SIDE * x + y, SIDE * x + (y + by) % SIDE) for x in range(SIDE) for y in range(SIDE)]
    return lax.ppermute(value, "st", pairs)


def pick_waves(waves, send_list):
    def kernel(send_ref, waves_ref, *outs):
        for n in range(4):
            for j in range(16):
                block = send_ref[n, j]
                outs[n][j] = waves_ref[:, pl.ds(pl.multiple_of(block * 128, 128), 128)]

    piece = jax.ShapeDtypeStruct((16, 32, 128), BF16)
    return pl.pallas_call(
        kernel,
        out_shape=[piece] * 4,
        in_specs=[
            pl.BlockSpec(memory_space=pltpu.SMEM),
            pl.BlockSpec(memory_space=pltpu.VMEM),
        ],
        out_specs=[pl.BlockSpec(memory_space=pltpu.VMEM)] * 4,
        compiler_params=params(16),
        name="pick_waves",
    )(send_list, waves)


NT = (((1,), (1,)), ((), ()))
ROWS = 16
OWN_ROWS = 32


def coef_own(inv_sqrt_blocks, waves, block_ref):
    def kernel(ref_ref, blocks_ref, waves_ref, out_ref):
        step = pl.program_id(0)
        for b in range(OWN_ROWS):
            i = step * OWN_ROWS + b
            operand = jnp.concatenate(
                [
                    waves_ref[:, pl.ds(pl.multiple_of(ref_ref[i, k] * 128, 128), 128)]
                    for k in range(2)
                ],
                axis=1,
            )
            factor = jnp.concatenate([blocks_ref[b, 0], blocks_ref[b, 1]], axis=1)
            out_ref[b] = lax.dot_general(operand, factor, NT, preferred_element_type=F32)

    return pl.pallas_call(
        kernel,
        grid=(64 // OWN_ROWS,),
        out_shape=jax.ShapeDtypeStruct((64, 32, 128), F32),
        in_specs=[
            pl.BlockSpec(memory_space=pltpu.SMEM),
            pl.BlockSpec((OWN_ROWS, 2, 128, 128), lambda i: (i, 0, 0, 0)),
            pl.BlockSpec((32, 8192), lambda i: (0, 0)),
        ],
        out_specs=pl.BlockSpec((OWN_ROWS, 32, 128), lambda i: (i, 0, 0)),
        compiler_params=params(48),
        cost_estimate=cost(2 * 64 * 2 * 32 * 128 * 128, 6 * 1024 * 1024),
        name="coef_own",
    )(block_ref, inv_sqrt_blocks, waves)


def coef_all(inv_sqrt_blocks, first, pieces, block_ref, row_count, send_list, occupation):
    def kernel(
        ref_ref, count_ref, send_ref, blocks_1, blocks_2, blocks_3, first_ref, occ_ref,
        p0, p1, p2, p3, coef_ref, o0, o1, o2, o3, table,
    ):
        step = pl.program_id(0)

        @pl.when(step == 0)
        def _():
            for n, piece in enumerate((p0, p1, p2, p3)):
                table[16 * n : 16 * n + 16] = piece[...]
            lane = lax.broadcasted_iota(jnp.int32, (32, 128), 1)
            occ = jnp.broadcast_to(occ_ref[...], (32, 128))
            high = occ.astype(BF16).astype(F32)
            middle = (occ - high).astype(BF16).astype(F32)
            low = occ - high - middle
            parts = jnp.where(lane == 0, high, jnp.where(lane == 1, middle, low))
            coef_ref[64] = jnp.where(lane < 3, parts, 0.0).astype(BF16)

        for b in range(ROWS):
            i = step * ROWS + b
            operands, factors = [], []
            for slot in range(2, 8):
                block = table[jnp.clip(ref_ref[i, slot] - 64, 0, 63)]
                operands.append(jnp.where(slot < count_ref[0, i], block, jnp.zeros_like(block)))
                factors.append((blocks_1, blocks_2, blocks_3)[slot // 2 - 1][b, slot % 2])
            term = lax.dot_general(
                jnp.concatenate(factors, axis=1),
                jnp.concatenate(operands, axis=1),
                NT,
                preferred_element_type=F32,
            )
            coef_ref[i] = (first_ref[b] + term.T).astype(BF16)

        @pl.when(step == 64 // ROWS - 1)
        def _():
            for n, out in enumerate((o0, o1, o2, o3)):
                for j in range(16):
                    out[j] = coef_ref[send_ref[n, j]]

    piece = jax.ShapeDtypeStruct((16, 32, 128), BF16)
    whole = pl.BlockSpec((16, 32, 128), lambda i: (0, 0, 0))
    smem = pl.BlockSpec(memory_space=pltpu.SMEM)
    return pl.pallas_call(
        kernel,
        grid=(64 // ROWS,),
        out_shape=[jax.ShapeDtypeStruct((65, 32, 128), BF16)] + [piece] * 4,
        in_specs=[smem, smem, smem]
        + [pl.BlockSpec((ROWS, 2, 128, 128), lambda i, k=k: (i, k, 0, 0)) for k in (1, 2, 3)]
        + [
            pl.BlockSpec((ROWS, 32, 128), lambda i: (i, 0, 0)),
            pl.BlockSpec((32, 1), lambda i: (0, 0)),
        ]
        + [whole] * 4,
        out_specs=[pl.BlockSpec((65, 32, 128), lambda i: (0, 0, 0))] + [whole] * 4,
        scratch_shapes=[pltpu.VMEM((64, 32, 128), BF16)],
        compiler_params=params(48),
        cost_estimate=cost(2 * 64 * 6 * 32 * 128 * 128, 14 * 1024 * 1024),
        name="coef_all",
    )(
        block_ref, row_count, send_list, inv_sqrt_blocks, inv_sqrt_blocks, inv_sqrt_blocks,
        first, occupation, *pieces,
    )


def from_beside(value):
    return along_y(value, 1), along_y(value, -1), along_x(value, 1), along_x(value, -1)


def from_far(beside):
    lower_y, higher_y, lower_x, higher_x = beside
    far_y = along_y(lower_y[:32], 1), along_y(higher_y[32:], -1)
    far_x = along_x(lower_x[:32], 1), along_x(higher_x[32:], -1)
    return (lower_y, higher_y, *far_y), (lower_x, higher_x, *far_x)


def unite(table, pieces):
    own, lower, higher, far_0, far_1 = pieces
    for n, piece in enumerate((own, lower, higher)):
        table[:, 32 * n : 32 * n + 32] = piece[...]
    table[0:32, 96:128] = far_0[...]
    table[32 : table.shape[0], 96:128] = far_1[...]


HALF = jax.ShapeDtypeStruct((4, 32, 16, 128), BF16)
KEPT = jax.ShapeDtypeStruct((4, 32, 16, 128), F32)
PARTS = [KEPT, HALF, HALF, HALF]


def product(weighted, low, high):
    both = jnp.dot(weighted, jnp.concatenate([low, high], axis=1), preferred_element_type=F32)
    for t in range(4):
        rows = both[8 * t : 8 * t + 8]
        yield jnp.concatenate([rows[:, :128], rows[:, 128:]], axis=0)


def density_own(here, coef, gathered_y, gathered_x, block_ref):
    def kernel(here_ref, ref_ref, own, ly, hy, fy0, fy1, lx, hx, fx0, fx1, w_ref, *rest):
        outs, tables, turned = rest[:8], rest[8:10], rest[10]
        x, y = here_ref[0], here_ref[1]
        for v, pieces in enumerate(((own, ly, hy, fy0, fy1), (own, lx, hx, fx0, fx1))):
            table = tables[v]
            unite(table, pieces)
            split = table[64].astype(F32)
            occ = split[:, 0:1] + split[:, 1:2] + split[:, 2:3]

            for i in range(32):
                mine = table[32 * v + i]
                weighted = (occ * mine.astype(F32)).astype(BF16).astype(F32)
                turned[32 * v + i] = weighted.T

            for i in range(32):
                groups = []
                for t in range(4):
                    group = SIDE * lax.rem(x + t, SIDE) + y if v == 0 else SIDE * x + lax.rem(y + t, SIDE)
                    groups.append(turned[32 * v + i, pl.ds(pl.multiple_of(group * 8, 8), 8)])
                lhs = jnp.concatenate(groups, axis=0).astype(BF16)
                w_ref[32 * v + i] = lhs
                both = [table[jnp.clip(ref_ref[32 * v + i, k], 0, 63)] for k in range(2)]
                for t, part in enumerate(product(lhs, *both)):
                    outs[4 * v + t][0, i] = part.astype(outs[4 * v + t].dtype)

    smem, vmem = pl.BlockSpec(memory_space=pltpu.SMEM), pl.BlockSpec(memory_space=pltpu.VMEM)
    full = pl.BlockSpec((65, 32, 128), lambda i: (0, 0, 0))
    lower = pl.BlockSpec((32, 32, 128), lambda i: (0, 0, 0))
    upper = pl.BlockSpec((33, 32, 128), lambda i: (0, 0, 0))
    return pl.pallas_call(
        kernel,
        grid=(1,),
        out_shape=[jax.ShapeDtypeStruct((64, 32, 128), BF16)] + PARTS * 2,
        in_specs=[smem, smem, full] + [full, full, lower, upper] * 2,
        out_specs=[pl.BlockSpec((64, 32, 128), lambda i: (0, 0, 0))]
        + [pl.BlockSpec((1, 32, 16, 128), lambda i: (0, 0, 0, 0))] * 8,
        scratch_shapes=[
            pltpu.VMEM((65, 128, 128), BF16),
            pltpu.VMEM((65, 128, 128), BF16),
            pltpu.VMEM((64, 128, 128), F32),
        ],
        compiler_params=params(),
        cost_estimate=cost(2 * 64 * 2 * 128 * 32 * 128, 7 * 1024 * 1024),
        name="density_own",
    )(here, block_ref, coef, *gathered_y, *gathered_x)


def density_rest(weighted, halo, halo_y, halo_x, block_ref, begun):
    def kernel(ref_ref, w_ref, own, ly, hy, fy0, fy1, lx, hx, fx0, fx1, *rest):
        outs, tables = rest[8:16], rest[16:]
        pair = pl.program_id(0)

        @pl.when(pair == 0)
        def _():
            unite(tables[0], (own, ly, hy, fy0, fy1))
            unite(tables[1], (own, lx, hx, fx0, fx1))

        for v, table in enumerate(tables):
            for i in range(32):
                codes = [ref_ref[32 * v + i, 2 + 2 * pair + k] - 64 for k in range(2)]
                both = [table[jnp.clip(code, 0, 63)] for code in codes]
                for t, part in enumerate(product(w_ref[32 * v + i], *both)):
                    outs[4 * v + t][0, i] = part.astype(outs[4 * v + t].dtype)

    smem = pl.BlockSpec(memory_space=pltpu.SMEM)
    full = pl.BlockSpec((64, 32, 128), lambda i: (0, 0, 0))
    lower = pl.BlockSpec((32, 32, 128), lambda i: (0, 0, 0))
    return pl.pallas_call(
        kernel,
        grid=(3,),
        out_shape=PARTS * 2,
        in_specs=[smem, full, full] + [full, full, lower, lower] * 2 + [pl.BlockSpec(memory_space=pl.ANY)] * 8,
        out_specs=[pl.BlockSpec((1, 32, 16, 128), lambda i: (i + 1, 0, 0, 0))] * 8,
        scratch_shapes=[pltpu.VMEM((64, 128, 128), BF16)] * 2,
        input_output_aliases={11 + n: n for n in range(8)},
        compiler_params=params(),
        cost_estimate=cost(2 * 64 * 6 * 128 * 32 * 128, 10 * 1024 * 1024),
        name="density_rest",
    )(block_ref, weighted, halo, *halo_y, *halo_x, *begun)


def finish(parts, row_count):
    rows = 16

    def kernel(count_ref, *refs):
        ins, out_ref = refs[:8], refs[8]
        step = pl.program_id(0)
        for v in range(2):

            @pl.when(step // (32 // rows) == v)
            def _():
                for pair in range(4):
                    value = ins[4 * v][pair]
                    for t in range(1, 4):
                        value = value + ins[4 * v + t][pair].astype(F32)
                    for b in range(rows):
                        count = count_ref[0, step * rows + b]
                        for k in range(2):
                            part = value[b, 8 * k : 8 * k + 8]
                            out_ref[b, 2 * pair + k] = jnp.where(2 * pair + k < count, part, jnp.zeros_like(part))

    per = 32 // rows
    low = pl.BlockSpec((4, rows, 16, 128), lambda i: (0, jnp.minimum(i, per - 1), 0, 0))
    high = pl.BlockSpec((4, rows, 16, 128), lambda i: (0, jnp.maximum(i - per, 0), 0, 0))
    return pl.pallas_call(
        kernel,
        grid=(64 // rows,),
        out_shape=jax.ShapeDtypeStruct((64, 8, 8, 128), F32),
        in_specs=[pl.BlockSpec(memory_space=pltpu.SMEM)] + [low] * 4 + [high] * 4,
        out_specs=pl.BlockSpec((rows, 8, 8, 128), lambda i: (i, 0, 0, 0)),
        compiler_params=params(),
        cost_estimate=cost(0, 7 * 1024 * 1024),
        name="finish",
    )(row_count, *parts)


def plan(block_ref, row_count):
    room, none = 2 * PAIRS, 4 * PAIRS

    def kernel(ref_ref, count_ref, entry_ref, place_ref, over_ref):
        def clear(p, carry):
            entry_ref[0, p] = 0
            entry_ref[1, p] = 0
            return carry

        lax.fori_loop(0, LIST + 1, clear, 0, unroll=5)

        def row(i, lengths):
            count = count_ref[0, i]
            for k in range(2, 8):
                block = jnp.clip(ref_ref[i, k] - 64, 0, 63)
                which = block // 32
                long = jnp.where(which == 0, lengths[0], lengths[1])
                p = jnp.minimum(long, LIST)
                alive = (k < count).astype(jnp.int32)
                entry_ref[which, p] = i * 64 + block
                placed = (k < count) & (p < LIST)
                place_ref[i, k] = jnp.where(placed, which * room + 64 + p, none)
                lengths = (lengths[0] + alive * (1 - which), lengths[1] + alive * which)
            return lengths

        lengths = lax.fori_loop(0, 64, row, (jnp.int32(0), jnp.int32(0)), unroll=2)
        over_ref[0, 0] = (jnp.maximum(*lengths) > LIST).astype(jnp.int32)

    smem = pl.BlockSpec(memory_space=pltpu.SMEM)
    return pl.pallas_call(
        kernel,
        out_shape=[
            jax.ShapeDtypeStruct((2, LIST + 1), jnp.int32),
            jax.ShapeDtypeStruct((64, 8), jnp.int32),
            jax.ShapeDtypeStruct((1, 1), jnp.int32),
        ],
        in_specs=[smem, smem],
        out_specs=[smem] * 3,
        compiler_params=params(16),
        cost_estimate=cost(0, 24 * 1024 * 1024),
        name="plan",
    )(block_ref, row_count)


def targets(here_ref, v):
    x, y = here_ref[0], here_ref[1]
    for t in range(4):
        yield SIDE * lax.rem(x + t, SIDE) + y if v == 0 else SIDE * x + lax.rem(y + t, SIDE)


def weigh(v, here, shards, block_ref):
    def kernel(here_ref, ref_ref, own, lower, higher, far_0, far_1, w_ref, *rest):
        outs, table, turned = rest[:4], rest[4], rest[5]
        unite(table, (own, lower, higher, far_0, far_1))
        split = table[64].astype(F32)
        occ = split[:, 0:1] + split[:, 1:2] + split[:, 2:3]
        for i in range(64):
            turned[i] = (occ * table[i].astype(F32)).astype(BF16).astype(F32).T
        starts = [pl.multiple_of(group * 8, 8) for group in targets(here_ref, v)]
        for i in range(64):
            groups = [turned[i, pl.ds(start, 8)] for start in starts]
            w_ref[i] = jnp.concatenate(groups, axis=0).astype(BF16)
        for i in range(32):
            both = [table[jnp.clip(ref_ref[32 * v + i, k], 0, 63)] for k in range(2)]
            for t, part in enumerate(product(w_ref[32 * v + i], *both)):
                outs[t][i] = part.astype(outs[t].dtype)

    smem, vmem = pl.BlockSpec(memory_space=pltpu.SMEM), pl.BlockSpec(memory_space=pltpu.VMEM)
    part = (32, 16, 128)
    return pl.pallas_call(
        kernel,
        out_shape=[jax.ShapeDtypeStruct((64, 32, 128), BF16), jax.ShapeDtypeStruct(part, F32)]
        + [jax.ShapeDtypeStruct(part, BF16)] * 3,
        in_specs=[smem, smem] + [vmem] * 5,
        out_specs=[vmem] * 5,
        scratch_shapes=[pltpu.VMEM((65, 128, 128), BF16), pltpu.VMEM((64, 128, 128), F32)],
        compiler_params=params(16),
        cost_estimate=cost(64 * 2 * 128 * 32 * 128, 4 * 1024 * 1024),
        name=f"weigh_{v}",
    )(here, block_ref, *shards)


def density_list(v, entries, weighted, shards, begun):
    def kernel(entry_ref, w_ref, own, lower, higher, far, *rest):
        begun_refs, outs, table = rest[:4], rest[4:8], rest[8]
        for n, piece in enumerate((own, lower, higher, far)):
            table[:, 32 * n : 32 * n + 32] = piece[...]
        for begun_ref, out in zip(begun_refs, outs):
            out[0:32] = begun_ref[...]
        for p in range(0, LIST, 2):
            halves = []
            for q in range(2):
                entry = entry_ref[v, p + q]
                weight, block = w_ref[lax.shift_right_logical(entry, 6)], table[entry & 31]
                halves.append(jnp.dot(weight, block, preferred_element_type=F32))
            for t, out in enumerate(outs):
                pair = jnp.concatenate([half[8 * t : 8 * t + 8] for half in halves], axis=0)
                out[32 + p // 2] = pair.astype(out.dtype)

    smem, vmem = pl.BlockSpec(memory_space=pltpu.SMEM), pl.BlockSpec(memory_space=pltpu.VMEM)
    part = (PAIRS, 16, 128)
    return pl.pallas_call(
        kernel,
        out_shape=[jax.ShapeDtypeStruct(part, F32)] + [jax.ShapeDtypeStruct(part, BF16)] * 3,
        in_specs=[smem] + [vmem] * 9,
        out_specs=[vmem] * 4,
        scratch_shapes=[pltpu.VMEM((32, 128, 128), BF16)],
        compiler_params=params(16),
        cost_estimate=cost(LIST * 2 * 128 * 32 * 128, 4 * 1024 * 1024),
        name=f"density_list_{v}",
    )(entries, weighted, *shards, *begun)


def gather_up(parts, places):
    def kernel(place_ref, *refs):
        ins, out_ref, sums = refs[:8], refs[8], refs[9]
        for v in range(2):
            value = ins[4 * v][...]
            for t in range(1, 4):
                value = value + ins[4 * v + t][...].astype(F32)
            sums[2 * PAIRS * v : 2 * PAIRS * v + 2 * PAIRS] = value.reshape(2 * PAIRS, 8, 128)
        sums[4 * PAIRS] = jnp.zeros((8, 128), F32)
        for i in range(64):
            for k in range(2):
                out_ref[i, k] = sums[2 * PAIRS * (i // 32) + 2 * (i % 32) + k]
            for k in range(2, 8):
                out_ref[i, k] = sums[place_ref[i, k]]

    smem, vmem = pl.BlockSpec(memory_space=pltpu.SMEM), pl.BlockSpec(memory_space=pltpu.VMEM)
    return pl.pallas_call(
        kernel,
        out_shape=jax.ShapeDtypeStruct((64, 8, 8, 128), F32),
        in_specs=[smem] + [vmem] * 8,
        out_specs=vmem,
        scratch_shapes=[pltpu.VMEM((4 * PAIRS + 1, 8, 128), F32)],
        compiler_params=params(16),
        cost_estimate=cost(0, 7 * 1024 * 1024),
        name="gather_up",
    )(places, *parts)


def scattered(parts_x, parts_y):
    arrived = []
    for parts, along in ((parts_x, along_x), (parts_y, along_y)):
        arrived.append(parts[0])
        arrived += [along(parts[t], t) for t in range(1, 4)]
    return arrived


def any_way(coef, halo, here, block_ref, count):
    own_y, own_x = from_far(from_beside(coef))
    halo_y, halo_x = from_far(from_beside(halo))
    weighted, *begun = density_own(here, coef, own_y, own_x, block_ref)
    parts = density_rest(weighted, halo, halo_y, halo_x, block_ref, begun)
    return finish(scattered(parts[:4], parts[4:]), count)


def body(inv_sqrt_blocks, waves, occupation, block_ref, row_count, send_list):
    send = send_list[0]
    count = row_count.reshape(1, 64)
    st = lax.axis_index("st")
    here = jnp.stack([st // SIDE, st % SIDE]).astype(jnp.int32)

    picked = pick_waves(waves, send)
    pieces = [along_dom(p, offset) for p, offset in zip(picked, OFFSETS)]
    first = coef_own(inv_sqrt_blocks, waves, block_ref)
    entries, places, over = plan(block_ref, count)
    coef, *outgoing = coef_all(
        inv_sqrt_blocks, first, pieces, block_ref, count, send, occupation.reshape(32, 1)
    )
    beside = from_beside(coef)
    halos = [along_dom(p, offset) for p, offset in zip(outgoing, OFFSETS)]
    *beside, h0, h1, h2, h3 = lax.optimization_barrier((*beside, *halos))
    far_y, far_x = from_far(beside)
    own_y, own_x = [coef, *far_y], [coef, *far_x]
    half_y = jnp.concatenate([h0, h1], axis=0)
    half_x = jnp.concatenate([h2, h3], axis=0)
    half_y, half_x, *far = lax.optimization_barrier((half_y, half_x, *far_y, *far_x))
    own_y, own_x = [coef, *far[:4]], [coef, *far[4:]]
    halo_y = [half_y] + [along_y(half_y, by) for by in (1, -1, 2)]
    halo_x = [half_x] + [along_x(half_x, by) for by in (1, -1, 2)]
    weighted_y, *begun_y = weigh(0, here, own_y, block_ref)
    weighted_x, *begun_x = weigh(1, here, own_x, block_ref)
    *shards, entries, weighted_y, weighted_x = lax.optimization_barrier(
        (*halo_y[1:], *halo_x[1:], entries, weighted_y, weighted_x)
    )
    halo_y, halo_x = [half_y, *shards[:3]], [half_x, *shards[3:]]
    parts_x = density_list(0, entries, weighted_y, halo_y, begun_y)
    parts_y = density_list(1, entries, weighted_x, halo_x, begun_x)
    density = gather_up(scattered(parts_x, parts_y), places)

    def again(density, coef, halo, *rest):
        return any_way(coef, halo, *rest)

    def keep(density, *rest):
        return density

    halo = jnp.concatenate([half_y, half_x], axis=0)
    return lax.cond(over[0, 0] > 0, again, keep, density, coef, halo, here, block_ref, count)


def solution(mesh):
    in_specs = (
        P("dom", None, None, None),
        P("st", "dom"),
        P("st"),
        P("dom", None),
        P("dom"),
        P("dom", None, None),
    )
    out_specs = P("dom", None, "st", None)
    return jax.shard_map(body, mesh=mesh, in_specs=in_specs, out_specs=out_specs, check_vma=False)
```

```python
import jax
import jax.numpy as jnp
from jax import lax
from jax.experimental import pallas as pl
from jax.experimental.pallas import tpu as pltpu
from jax.sharding import PartitionSpec as P

LIST = 144
PAIRS = 32 + LIST // 2
OFFSETS = (-2, -1, 1, 2)
SIDE = 4
BF16, F32 = jnp.bfloat16, jnp.float32


def params(mib=32):
    return pltpu.CompilerParams(vmem_limit_bytes=mib * 1024 * 1024)


def cost(flops, moved):
    return pl.CostEstimate(flops=flops, bytes_accessed=moved, transcendentals=0)


def along_dom(value, by):
    return lax.ppermute(value, "dom", [(i, (i + by) % 16) for i in range(16)])


def along_x(value, by):
    pairs = [(SIDE * x + y, SIDE * ((x + by) % SIDE) + y) for x in range(SIDE) for y in range(SIDE)]
    return lax.ppermute(value, "st", pairs)


def along_y(value, by):
    pairs = [(SIDE * x + y, SIDE * x + (y + by) % SIDE) for x in range(SIDE) for y in range(SIDE)]
    return lax.ppermute(value, "st", pairs)


def pick_waves(waves, send_list):
    def kernel(send_ref, waves_ref, *outs):
        for n in range(4):
            for j in range(16):
                block = send_ref[n, j]
                outs[n][j] = waves_ref[:, pl.ds(pl.multiple_of(block * 128, 128), 128)]

    piece = jax.ShapeDtypeStruct((16, 32, 128), BF16)
    return pl.pallas_call(
        kernel,
        out_shape=[piece] * 4,
        in_specs=[
            pl.BlockSpec(memory_space=pltpu.SMEM),
            pl.BlockSpec(memory_space=pltpu.VMEM),
        ],
        out_specs=[pl.BlockSpec(memory_space=pltpu.VMEM)] * 4,
        compiler_params=params(16),
        name="pick_waves",
    )(send_list, waves)


NT = (((1,), (1,)), ((), ()))
ROWS = 16
OWN_ROWS = 32


def coef_own(inv_sqrt_blocks, waves, block_ref):
    def kernel(ref_ref, blocks_ref, waves_ref, out_ref):
        step = pl.program_id(0)
        for b in range(OWN_ROWS):
            i = step * OWN_ROWS + b
            operand = jnp.concatenate(
                [
                    waves_ref[:, pl.ds(pl.multiple_of(ref_ref[i, k] * 128, 128), 128)]
                    for k in range(2)
                ],
                axis=1,
            )
            factor = jnp.concatenate([blocks_ref[b, 0], blocks_ref[b, 1]], axis=1)
            out_ref[b] = lax.dot_general(operand, factor, NT, preferred_element_type=F32)

    return pl.pallas_call(
        kernel,
        grid=(64 // OWN_ROWS,),
        out_shape=jax.ShapeDtypeStruct((64, 32, 128), F32),
        in_specs=[
            pl.BlockSpec(memory_space=pltpu.SMEM),
            pl.BlockSpec((OWN_ROWS, 2, 128, 128), lambda i: (i, 0, 0, 0)),
            pl.BlockSpec((32, 8192), lambda i: (0, 0)),
        ],
        out_specs=pl.BlockSpec((OWN_ROWS, 32, 128), lambda i: (i, 0, 0)),
        compiler_params=params(48),
        cost_estimate=cost(2 * 64 * 2 * 32 * 128 * 128, 6 * 1024 * 1024),
        name="coef_own",
    )(block_ref, inv_sqrt_blocks, waves)


def coef_all(inv_sqrt_blocks, first, pieces, block_ref, row_count, send_list, occupation):
    def kernel(
        ref_ref, count_ref, send_ref, blocks_1, blocks_2, blocks_3, first_ref, occ_ref,
        p0, p1, p2, p3, coef_ref, o0, o1, o2, o3, table,
    ):
        step = pl.program_id(0)

        @pl.when(step == 0)
        def _():
            for n, piece in enumerate((p0, p1, p2, p3)):
                table[16 * n : 16 * n + 16] = piece[...]
            lane = lax.broadcasted_iota(jnp.int32, (32, 128), 1)
            occ = jnp.broadcast_to(occ_ref[...], (32, 128))
            high = occ.astype(BF16).astype(F32)
            middle = (occ - high).astype(BF16).astype(F32)
            low = occ - high - middle
            parts = jnp.where(lane == 0, high, jnp.where(lane == 1, middle, low))
            coef_ref[64] = jnp.where(lane < 3, parts, 0.0).astype(BF16)

        for b in range(ROWS):
            i = step * ROWS + b
            operands, factors = [], []
            for slot in range(2, 8):
                block = table[jnp.clip(ref_ref[i, slot] - 64, 0, 63)]
                operands.append(jnp.where(slot < count_ref[0, i], block, jnp.zeros_like(block)))
                factors.append((blocks_1, blocks_2, blocks_3)[slot // 2 - 1][b, slot % 2])
            term = lax.dot_general(
                jnp.concatenate(factors, axis=1),
                jnp.concatenate(operands, axis=1),
                NT,
                preferred_element_type=F32,
            )
            coef_ref[i] = (first_ref[b] + term.T).astype(BF16)

        @pl.when(step == 64 // ROWS - 1)
        def _():
            for n, out in enumerate((o0, o1, o2, o3)):
                for j in range(16):
                    out[j] = coef_ref[send_ref[n, j]]

    piece = jax.ShapeDtypeStruct((16, 32, 128), BF16)
    whole = pl.BlockSpec((16, 32, 128), lambda i: (0, 0, 0))
    smem = pl.BlockSpec(memory_space=pltpu.SMEM)
    return pl.pallas_call(
        kernel,
        grid=(64 // ROWS,),
        out_shape=[jax.ShapeDtypeStruct((65, 32, 128), BF16)] + [piece] * 4,
        in_specs=[smem, smem, smem]
        + [pl.BlockSpec((ROWS, 2, 128, 128), lambda i, k=k: (i, k, 0, 0)) for k in (1, 2, 3)]
        + [
            pl.BlockSpec((ROWS, 32, 128), lambda i: (i, 0, 0)),
            pl.BlockSpec((32, 1), lambda i: (0, 0)),
        ]
        + [whole] * 4,
        out_specs=[pl.BlockSpec((65, 32, 128), lambda i: (0, 0, 0))] + [whole] * 4,
        scratch_shapes=[pltpu.VMEM((64, 32, 128), BF16)],
        compiler_params=params(48),
        cost_estimate=cost(2 * 64 * 6 * 32 * 128 * 128, 14 * 1024 * 1024),
        name="coef_all",
    )(
        block_ref, row_count, send_list, inv_sqrt_blocks, inv_sqrt_blocks, inv_sqrt_blocks,
        first, occupation, *pieces,
    )


def from_beside(value):
    return along_y(value, 1), along_y(value, -1), along_x(value, 1), along_x(value, -1)


def from_far(beside):
    lower_y, higher_y, lower_x, higher_x = beside
    far_y = along_y(lower_y[:32], 1), along_y(higher_y[32:], -1)
    far_x = along_x(lower_x[:32], 1), along_x(higher_x[32:], -1)
    return (lower_y, higher_y, *far_y), (lower_x, higher_x, *far_x)


def unite(table, pieces):
    own, lower, higher, far_0, far_1 = pieces
    for n, piece in enumerate((own, lower, higher)):
        table[:, 32 * n : 32 * n + 32] = piece[...]
    table[0:32, 96:128] = far_0[...]
    table[32 : table.shape[0], 96:128] = far_1[...]


HALF = jax.ShapeDtypeStruct((4, 32, 16, 128), BF16)
KEPT = jax.ShapeDtypeStruct((4, 32, 16, 128), F32)
PARTS = [KEPT, HALF, HALF, HALF]


def product(weighted, low, high):
    both = jnp.dot(weighted, jnp.concatenate([low, high], axis=1), preferred_element_type=F32)
    for t in range(4):
        rows = both[8 * t : 8 * t + 8]
        yield jnp.concatenate([rows[:, :128], rows[:, 128:]], axis=0)


def density_own(here, coef, gathered_y, gathered_x, block_ref):
    def kernel(here_ref, ref_ref, own, ly, hy, fy0, fy1, lx, hx, fx0, fx1, w_ref, *rest):
        outs, tables, turned = rest[:8], rest[8:10], rest[10]
        x, y = here_ref[0], here_ref[1]
        for v, pieces in enumerate(((own, ly, hy, fy0, fy1), (own, lx, hx, fx0, fx1))):
            table = tables[v]
            unite(table, pieces)
            split = table[64].astype(F32)
            occ = split[:, 0:1] + split[:, 1:2] + split[:, 2:3]

            for i in range(32):
                mine = table[32 * v + i]
                weighted = (occ * mine.astype(F32)).astype(BF16).astype(F32)
                turned[32 * v + i] = weighted.T

            for i in range(32):
                groups = []
                for t in range(4):
                    group = SIDE * lax.rem(x + t, SIDE) + y if v == 0 else SIDE * x + lax.rem(y + t, SIDE)
                    groups.append(turned[32 * v + i, pl.ds(pl.multiple_of(group * 8, 8), 8)])
                lhs = jnp.concatenate(groups, axis=0).astype(BF16)
                w_ref[32 * v + i] = lhs
                both = [table[jnp.clip(ref_ref[32 * v + i, k], 0, 63)] for k in range(2)]
                for t, part in enumerate(product(lhs, *both)):
                    outs[4 * v + t][0, i] = part.astype(outs[4 * v + t].dtype)

    smem, vmem = pl.BlockSpec(memory_space=pltpu.SMEM), pl.BlockSpec(memory_space=pltpu.VMEM)
    full = pl.BlockSpec((65, 32, 128), lambda i: (0, 0, 0))
    lower = pl.BlockSpec((32, 32, 128), lambda i: (0, 0, 0))
    upper = pl.BlockSpec((33, 32, 128), lambda i: (0, 0, 0))
    return pl.pallas_call(
        kernel,
        grid=(1,),
        out_shape=[jax.ShapeDtypeStruct((64, 32, 128), BF16)] + PARTS * 2,
        in_specs=[smem, smem, full] + [full, full, lower, upper] * 2,
        out_specs=[pl.BlockSpec((64, 32, 128), lambda i: (0, 0, 0))]
        + [pl.BlockSpec((1, 32, 16, 128), lambda i: (0, 0, 0, 0))] * 8,
        scratch_shapes=[
            pltpu.VMEM((65, 128, 128), BF16),
            pltpu.VMEM((65, 128, 128), BF16),
            pltpu.VMEM((64, 128, 128), F32),
        ],
        compiler_params=params(),
        cost_estimate=cost(2 * 64 * 2 * 128 * 32 * 128, 7 * 1024 * 1024),
        name="density_own",
    )(here, block_ref, coef, *gathered_y, *gathered_x)


def density_rest(weighted, halo, halo_y, halo_x, block_ref, begun):
    def kernel(ref_ref, w_ref, own, ly, hy, fy0, fy1, lx, hx, fx0, fx1, *rest):
        outs, tables = rest[8:16], rest[16:]
        pair = pl.program_id(0)

        @pl.when(pair == 0)
        def _():
            unite(tables[0], (own, ly, hy, fy0, fy1))
            unite(tables[1], (own, lx, hx, fx0, fx1))

        for v, table in enumerate(tables):
            for i in range(32):
                codes = [ref_ref[32 * v + i, 2 + 2 * pair + k] - 64 for k in range(2)]
                both = [table[jnp.clip(code, 0, 63)] for code in codes]
                for t, part in enumerate(product(w_ref[32 * v + i], *both)):
                    outs[4 * v + t][0, i] = part.astype(outs[4 * v + t].dtype)

    smem = pl.BlockSpec(memory_space=pltpu.SMEM)
    full = pl.BlockSpec((64, 32, 128), lambda i: (0, 0, 0))
    lower = pl.BlockSpec((32, 32, 128), lambda i: (0, 0, 0))
    return pl.pallas_call(
        kernel,
        grid=(3,),
        out_shape=PARTS * 2,
        in_specs=[smem, full, full] + [full, full, lower, lower] * 2 + [pl.BlockSpec(memory_space=pl.ANY)] * 8,
        out_specs=[pl.BlockSpec((1, 32, 16, 128), lambda i: (i + 1, 0, 0, 0))] * 8,
        scratch_shapes=[pltpu.VMEM((64, 128, 128), BF16)] * 2,
        input_output_aliases={11 + n: n for n in range(8)},
        compiler_params=params(),
        cost_estimate=cost(2 * 64 * 6 * 128 * 32 * 128, 10 * 1024 * 1024),
        name="density_rest",
    )(block_ref, weighted, halo, *halo_y, *halo_x, *begun)


def finish(parts, row_count):
    rows = 16

    def kernel(count_ref, *refs):
        ins, out_ref = refs[:8], refs[8]
        step = pl.program_id(0)
        for v in range(2):

            @pl.when(step // (32 // rows) == v)
            def _():
                for pair in range(4):
                    value = ins[4 * v][pair]
                    for t in range(1, 4):
                        value = value + ins[4 * v + t][pair].astype(F32)
                    for b in range(rows):
                        count = count_ref[0, step * rows + b]
                        for k in range(2):
                            part = value[b, 8 * k : 8 * k + 8]
                            out_ref[b, 2 * pair + k] = jnp.where(2 * pair + k < count, part, jnp.zeros_like(part))

    per = 32 // rows
    low = pl.BlockSpec((4, rows, 16, 128), lambda i: (0, jnp.minimum(i, per - 1), 0, 0))
    high = pl.BlockSpec((4, rows, 16, 128), lambda i: (0, jnp.maximum(i - per, 0), 0, 0))
    return pl.pallas_call(
        kernel,
        grid=(64 // rows,),
        out_shape=jax.ShapeDtypeStruct((64, 8, 8, 128), F32),
        in_specs=[pl.BlockSpec(memory_space=pltpu.SMEM)] + [low] * 4 + [high] * 4,
        out_specs=pl.BlockSpec((rows, 8, 8, 128), lambda i: (i, 0, 0, 0)),
        compiler_params=params(),
        cost_estimate=cost(0, 7 * 1024 * 1024),
        name="finish",
    )(row_count, *parts)


def plan(block_ref, row_count):
    room, none = 2 * PAIRS, 4 * PAIRS

    def kernel(ref_ref, count_ref, entry_ref, place_ref, over_ref):
        def clear(p, carry):
            entry_ref[0, p] = 0
            entry_ref[1, p] = 0
            return carry

        lax.fori_loop(0, LIST + 1, clear, 0, unroll=5)

        def row(i, lengths):
            count = count_ref[0, i]
            for k in range(2, 8):
                block = jnp.clip(ref_ref[i, k] - 64, 0, 63)
                which = block // 32
                long = jnp.where(which == 0, lengths[0], lengths[1])
                p = jnp.minimum(long, LIST)
                alive = (k < count).astype(jnp.int32)
                entry_ref[which, p] = i * 64 + block
                placed = (k < count) & (p < LIST)
                place_ref[i, k] = jnp.where(placed, which * room + 64 + p, none)
                lengths = (lengths[0] + alive * (1 - which), lengths[1] + alive * which)
            return lengths

        lengths = lax.fori_loop(0, 64, row, (jnp.int32(0), jnp.int32(0)), unroll=2)
        over_ref[0, 0] = (jnp.maximum(*lengths) > LIST).astype(jnp.int32)

    smem = pl.BlockSpec(memory_space=pltpu.SMEM)
    return pl.pallas_call(
        kernel,
        out_shape=[
            jax.ShapeDtypeStruct((2, LIST + 1), jnp.int32),
            jax.ShapeDtypeStruct((64, 8), jnp.int32),
            jax.ShapeDtypeStruct((1, 1), jnp.int32),
        ],
        in_specs=[smem, smem],
        out_specs=[smem] * 3,
        compiler_params=params(16),
        cost_estimate=cost(0, 24 * 1024 * 1024),
        name="plan",
    )(block_ref, row_count)


def targets(here_ref, v):
    x, y = here_ref[0], here_ref[1]
    for t in range(4):
        yield SIDE * lax.rem(x + t, SIDE) + y if v == 0 else SIDE * x + lax.rem(y + t, SIDE)


def weigh(v, here, shards, block_ref):
    def kernel(here_ref, ref_ref, own, lower, higher, far, w_ref, *rest):
        outs, table, turned = rest[:4], rest[4], rest[5]
        for n, piece in enumerate((own, lower, higher, far)):
            table[:, 32 * n : 32 * n + 32] = piece[...]
        split = table[64].astype(F32)
        occ = split[:, 0:1] + split[:, 1:2] + split[:, 2:3]
        for i in range(64):
            turned[i] = (occ * table[i].astype(F32)).astype(BF16).astype(F32).T
        starts = [pl.multiple_of(group * 8, 8) for group in targets(here_ref, v)]
        for i in range(64):
            groups = [turned[i, pl.ds(start, 8)] for start in starts]
            w_ref[i] = jnp.concatenate(groups, axis=0).astype(BF16)
        for i in range(32):
            both = [table[jnp.clip(ref_ref[32 * v + i, k], 0, 63)] for k in range(2)]
            for t, part in enumerate(product(w_ref[32 * v + i], *both)):
                outs[t][i] = part.astype(outs[t].dtype)

    smem, vmem = pl.BlockSpec(memory_space=pltpu.SMEM), pl.BlockSpec(memory_space=pltpu.VMEM)
    part = (32, 16, 128)
    return pl.pallas_call(
        kernel,
        out_shape=[jax.ShapeDtypeStruct((64, 32, 128), BF16), jax.ShapeDtypeStruct(part, F32)]
        + [jax.ShapeDtypeStruct(part, BF16)] * 3,
        in_specs=[smem, smem] + [vmem] * 4,
        out_specs=[vmem] * 5,
        scratch_shapes=[pltpu.VMEM((65, 128, 128), BF16), pltpu.VMEM((64, 128, 128), F32)],
        compiler_params=params(16),
        cost_estimate=cost(64 * 2 * 128 * 32 * 128, 4 * 1024 * 1024),
        name=f"weigh_{v}",
    )(here, block_ref, *shards)


def density_list(v, entries, weighted, shards, begun):
    def kernel(entry_ref, w_ref, own, lower, higher, far, *rest):
        begun_refs, outs, table = rest[:4], rest[4:8], rest[8]
        for n, piece in enumerate((own, lower, higher, far)):
            table[:, 32 * n : 32 * n + 32] = piece[...]
        for begun_ref, out in zip(begun_refs, outs):
            out[0:32] = begun_ref[...]
        for p in range(0, LIST, 2):
            halves = []
            for q in range(2):
                entry = entry_ref[v, p + q]
                weight, block = w_ref[lax.shift_right_logical(entry, 6)], table[entry & 31]
                halves.append(jnp.dot(weight, block, preferred_element_type=F32))
            for t, out in enumerate(outs):
                pair = jnp.concatenate([half[8 * t : 8 * t + 8] for half in halves], axis=0)
                out[32 + p // 2] = pair.astype(out.dtype)

    smem, vmem = pl.BlockSpec(memory_space=pltpu.SMEM), pl.BlockSpec(memory_space=pltpu.VMEM)
    part = (PAIRS, 16, 128)
    return pl.pallas_call(
        kernel,
        out_shape=[jax.ShapeDtypeStruct(part, F32)] + [jax.ShapeDtypeStruct(part, BF16)] * 3,
        in_specs=[smem] + [vmem] * 9,
        out_specs=[vmem] * 4,
        scratch_shapes=[pltpu.VMEM((32, 128, 128), BF16)],
        compiler_params=params(16),
        cost_estimate=cost(LIST * 2 * 128 * 32 * 128, 4 * 1024 * 1024),
        name=f"density_list_{v}",
    )(entries, weighted, *shards, *begun)


def gather_up(parts, places):
    def kernel(place_ref, *refs):
        ins, out_ref, sums = refs[:8], refs[8], refs[9]
        for v in range(2):
            value = ins[4 * v][...]
            for t in range(1, 4):
                value = value + ins[4 * v + t][...].astype(F32)
            sums[2 * PAIRS * v : 2 * PAIRS * v + 2 * PAIRS] = value.reshape(2 * PAIRS, 8, 128)
        sums[4 * PAIRS] = jnp.zeros((8, 128), F32)
        for i in range(64):
            for k in range(2):
                out_ref[i, k] = sums[2 * PAIRS * (i // 32) + 2 * (i % 32) + k]
            for k in range(2, 8):
                out_ref[i, k] = sums[place_ref[i, k]]

    smem, vmem = pl.BlockSpec(memory_space=pltpu.SMEM), pl.BlockSpec(memory_space=pltpu.VMEM)
    return pl.pallas_call(
        kernel,
        out_shape=jax.ShapeDtypeStruct((64, 8, 8, 128), F32),
        in_specs=[smem] + [vmem] * 8,
        out_specs=vmem,
        scratch_shapes=[pltpu.VMEM((4 * PAIRS + 1, 8, 128), F32)],
        compiler_params=params(16),
        cost_estimate=cost(0, 7 * 1024 * 1024),
        name="gather_up",
    )(places, *parts)


def scattered(parts_x, parts_y):
    arrived = []
    for parts, along in ((parts_x, along_x), (parts_y, along_y)):
        arrived.append(parts[0])
        arrived += [along(parts[t], t) for t in range(1, 4)]
    return arrived


def any_way(coef, halo, here, block_ref, count):
    own_y, own_x = from_far(from_beside(coef))
    halo_y, halo_x = from_far(from_beside(halo))
    weighted, *begun = density_own(here, coef, own_y, own_x, block_ref)
    parts = density_rest(weighted, halo, halo_y, halo_x, block_ref, begun)
    return finish(scattered(parts[:4], parts[4:]), count)


def body(inv_sqrt_blocks, waves, occupation, block_ref, row_count, send_list):
    send = send_list[0]
    count = row_count.reshape(1, 64)
    st = lax.axis_index("st")
    here = jnp.stack([st // SIDE, st % SIDE]).astype(jnp.int32)

    picked = pick_waves(waves, send)
    pieces = [along_dom(p, offset) for p, offset in zip(picked, OFFSETS)]
    first = coef_own(inv_sqrt_blocks, waves, block_ref)
    entries, places, over = plan(block_ref, count)
    coef, *outgoing = coef_all(
        inv_sqrt_blocks, first, pieces, block_ref, count, send, occupation.reshape(32, 1)
    )
    halos = [along_dom(p, offset) for p, offset in zip(outgoing, OFFSETS)]
    ready = [lax.optimization_barrier((coef, h)) for h in halos]
    own_x = [coef, along_x(ready[2][0], 1), along_x(ready[3][0], -1), along_x(coef, 2)]
    own_y = [coef, along_y(ready[1][0], 1), along_y(ready[3][0], -1), along_y(ready[0][0], 2)]
    halos = [h for _, h in ready]
    half_y, half_x, entries, *own = lax.optimization_barrier(
        (jnp.concatenate(halos[:2], axis=0), jnp.concatenate(halos[2:], axis=0), entries, *own_y[1:], *own_x[1:])
    )
    own_y, own_x = [coef, *own[:3]], [coef, *own[3:]]
    halo_y = [half_y] + [along_y(half_y, by) for by in (1, -1, 2)]
    halo_x = [half_x] + [along_x(half_x, by) for by in (1, -1, 2)]
    weighted_y, *begun_y = weigh(0, here, own_y, block_ref)
    weighted_x, *begun_x = weigh(1, here, own_x, block_ref)
    *shards, entries, weighted_y, weighted_x = lax.optimization_barrier(
        (*halo_y[1:], *halo_x[1:], entries, weighted_y, weighted_x)
    )
    halo_y, halo_x = [half_y, *shards[:3]], [half_x, *shards[3:]]
    parts_x = density_list(0, entries, weighted_y, halo_y, begun_y)
    parts_y = density_list(1, entries, weighted_x, halo_x, begun_x)
    density = gather_up(scattered(parts_x, parts_y), places)

    def again(density, coef, halo, *rest):
        return any_way(coef, halo, *rest)

    def keep(density, *rest):
        return density

    halo = jnp.concatenate([half_y, half_x], axis=0)
    return lax.cond(over[0, 0] > 0, again, keep, density, coef, halo, here, block_ref, count)


def solution(mesh):
    in_specs = (
        P("dom", None, None, None),
        P("st", "dom"),
        P("st"),
        P("dom", None),
        P("dom"),
        P("dom", None, None),
    )
    out_specs = P("dom", None, "st", None)
    return jax.shard_map(body, mesh=mesh, in_specs=in_specs, out_specs=out_specs, check_vma=False)
```

```python
import jax
import jax.numpy as jnp
from jax import lax
from jax.experimental import pallas as pl
from jax.experimental.pallas import tpu as pltpu
from jax.sharding import PartitionSpec as P

LIST = 144
PAIRS = 32 + LIST // 2
OFFSETS = (-2, -1, 1, 2)
SIDE = 4
BF16, F32 = jnp.bfloat16, jnp.float32


def params(mib=32):
    return pltpu.CompilerParams(vmem_limit_bytes=mib * 1024 * 1024)


def cost(flops, moved):
    return pl.CostEstimate(flops=flops, bytes_accessed=moved, transcendentals=0)


def along_dom(value, by):
    return lax.ppermute(value, "dom", [(i, (i + by) % 16) for i in range(16)])


def along_x(value, by):
    pairs = [(SIDE * x + y, SIDE * ((x + by) % SIDE) + y) for x in range(SIDE) for y in range(SIDE)]
    return lax.ppermute(value, "st", pairs)


def along_y(value, by):
    pairs = [(SIDE * x + y, SIDE * x + (y + by) % SIDE) for x in range(SIDE) for y in range(SIDE)]
    return lax.ppermute(value, "st", pairs)


def pick_waves(waves, send_list):
    def kernel(send_ref, waves_ref, *outs):
        for n in range(4):
            for j in range(16):
                block = send_ref[n, j]
                outs[n][j] = waves_ref[:, pl.ds(pl.multiple_of(block * 128, 128), 128)]

    piece = jax.ShapeDtypeStruct((16, 32, 128), BF16)
    return pl.pallas_call(
        kernel,
        out_shape=[piece] * 4,
        in_specs=[
            pl.BlockSpec(memory_space=pltpu.SMEM),
            pl.BlockSpec(memory_space=pltpu.VMEM),
        ],
        out_specs=[pl.BlockSpec(memory_space=pltpu.VMEM)] * 4,
        compiler_params=params(16),
        name="pick_waves",
    )(send_list, waves)


NT = (((1,), (1,)), ((), ()))
ROWS = 16
OWN_ROWS = 32


def coef_own(inv_sqrt_blocks, waves, block_ref):
    def kernel(ref_ref, blocks_ref, waves_ref, out_ref):
        step = pl.program_id(0)
        for b in range(OWN_ROWS):
            i = step * OWN_ROWS + b
            operand = jnp.concatenate(
                [
                    waves_ref[:, pl.ds(pl.multiple_of(ref_ref[i, k] * 128, 128), 128)]
                    for k in range(2)
                ],
                axis=1,
            )
            factor = jnp.concatenate([blocks_ref[b, 0], blocks_ref[b, 1]], axis=1)
            out_ref[b] = lax.dot_general(operand, factor, NT, preferred_element_type=F32)

    return pl.pallas_call(
        kernel,
        grid=(64 // OWN_ROWS,),
        out_shape=jax.ShapeDtypeStruct((64, 32, 128), F32),
        in_specs=[
            pl.BlockSpec(memory_space=pltpu.SMEM),
            pl.BlockSpec((OWN_ROWS, 2, 128, 128), lambda i: (i, 0, 0, 0)),
            pl.BlockSpec((32, 8192), lambda i: (0, 0)),
        ],
        out_specs=pl.BlockSpec((OWN_ROWS, 32, 128), lambda i: (i, 0, 0)),
        compiler_params=params(48),
        cost_estimate=cost(2 * 64 * 2 * 32 * 128 * 128, 6 * 1024 * 1024),
        name="coef_own",
    )(block_ref, inv_sqrt_blocks, waves)


def coef_all(inv_sqrt_blocks, first, pieces, block_ref, row_count, send_list, occupation):
    def kernel(
        ref_ref, count_ref, send_ref, blocks_1, blocks_2, blocks_3, first_ref, occ_ref,
        p0, p1, p2, p3, coef_ref, o0, o1, o2, o3, table,
    ):
        step = pl.program_id(0)

        @pl.when(step == 0)
        def _():
            for n, piece in enumerate((p0, p1, p2, p3)):
                table[16 * n : 16 * n + 16] = piece[...]
            lane = lax.broadcasted_iota(jnp.int32, (32, 128), 1)
            occ = jnp.broadcast_to(occ_ref[...], (32, 128))
            high = occ.astype(BF16).astype(F32)
            middle = (occ - high).astype(BF16).astype(F32)
            low = occ - high - middle
            parts = jnp.where(lane == 0, high, jnp.where(lane == 1, middle, low))
            coef_ref[64] = jnp.where(lane < 3, parts, 0.0).astype(BF16)

        for b in range(ROWS):
            i = step * ROWS + b
            operands, factors = [], []
            for slot in range(2, 8):
                block = table[jnp.clip(ref_ref[i, slot] - 64, 0, 63)]
                operands.append(jnp.where(slot < count_ref[0, i], block, jnp.zeros_like(block)))
                factors.append((blocks_1, blocks_2, blocks_3)[slot // 2 - 1][b, slot % 2])
            term = lax.dot_general(
                jnp.concatenate(factors, axis=1),
                jnp.concatenate(operands, axis=1),
                NT,
                preferred_element_type=F32,
            )
            coef_ref[i] = (first_ref[b] + term.T).astype(BF16)

        @pl.when(step == 64 // ROWS - 1)
        def _():
            for n, out in enumerate((o0, o1, o2, o3)):
                for j in range(16):
                    out[j] = coef_ref[send_ref[n, j]]

    piece = jax.ShapeDtypeStruct((16, 32, 128), BF16)
    whole = pl.BlockSpec((16, 32, 128), lambda i: (0, 0, 0))
    smem = pl.BlockSpec(memory_space=pltpu.SMEM)
    return pl.pallas_call(
        kernel,
        grid=(64 // ROWS,),
        out_shape=[jax.ShapeDtypeStruct((65, 32, 128), BF16)] + [piece] * 4,
        in_specs=[smem, smem, smem]
        + [pl.BlockSpec((ROWS, 2, 128, 128), lambda i, k=k: (i, k, 0, 0)) for k in (1, 2, 3)]
        + [
            pl.BlockSpec((ROWS, 32, 128), lambda i: (i, 0, 0)),
            pl.BlockSpec((32, 1), lambda i: (0, 0)),
        ]
        + [whole] * 4,
        out_specs=[pl.BlockSpec((65, 32, 128), lambda i: (0, 0, 0))] + [whole] * 4,
        scratch_shapes=[pltpu.VMEM((64, 32, 128), BF16)],
        compiler_params=params(48),
        cost_estimate=cost(2 * 64 * 6 * 32 * 128 * 128, 14 * 1024 * 1024),
        name="coef_all",
    )(
        block_ref, row_count, send_list, inv_sqrt_blocks, inv_sqrt_blocks, inv_sqrt_blocks,
        first, occupation, *pieces,
    )


def from_beside(value):
    return along_y(value, 1), along_y(value, -1), along_x(value, 1), along_x(value, -1)


def from_far(beside):
    lower_y, higher_y, lower_x, higher_x = beside
    far_y = along_y(lower_y[:32], 1), along_y(higher_y[32:], -1)
    far_x = along_x(lower_x[:32], 1), along_x(higher_x[32:], -1)
    return (lower_y, higher_y, *far_y), (lower_x, higher_x, *far_x)


def unite(table, pieces):
    own, lower, higher, far_0, far_1 = pieces
    for n, piece in enumerate((own, lower, higher)):
        table[:, 32 * n : 32 * n + 32] = piece[...]
    table[0:32, 96:128] = far_0[...]
    table[32 : table.shape[0], 96:128] = far_1[...]


HALF = jax.ShapeDtypeStruct((4, 32, 16, 128), BF16)
KEPT = jax.ShapeDtypeStruct((4, 32, 16, 128), F32)
PARTS = [KEPT, HALF, HALF, HALF]


def product(weighted, low, high):
    both = jnp.dot(weighted, jnp.concatenate([low, high], axis=1), preferred_element_type=F32)
    for t in range(4):
        rows = both[8 * t : 8 * t + 8]
        yield jnp.concatenate([rows[:, :128], rows[:, 128:]], axis=0)


def density_own(here, coef, gathered_y, gathered_x, block_ref):
    def kernel(here_ref, ref_ref, own, ly, hy, fy0, fy1, lx, hx, fx0, fx1, w_ref, *rest):
        outs, tables, turned = rest[:8], rest[8:10], rest[10]
        x, y = here_ref[0], here_ref[1]
        for v, pieces in enumerate(((own, ly, hy, fy0, fy1), (own, lx, hx, fx0, fx1))):
            table = tables[v]
            unite(table, pieces)
            split = table[64].astype(F32)
            occ = split[:, 0:1] + split[:, 1:2] + split[:, 2:3]

            for i in range(32):
                mine = table[32 * v + i]
                weighted = (occ * mine.astype(F32)).astype(BF16).astype(F32)
                turned[32 * v + i] = weighted.T

            for i in range(32):
                groups = []
                for t in range(4):
                    group = SIDE * lax.rem(x + t, SIDE) + y if v == 0 else SIDE * x + lax.rem(y + t, SIDE)
                    groups.append(turned[32 * v + i, pl.ds(pl.multiple_of(group * 8, 8), 8)])
                lhs = jnp.concatenate(groups, axis=0).astype(BF16)
                w_ref[32 * v + i] = lhs
                both = [table[jnp.clip(ref_ref[32 * v + i, k], 0, 63)] for k in range(2)]
                for t, part in enumerate(product(lhs, *both)):
                    outs[4 * v + t][0, i] = part.astype(outs[4 * v + t].dtype)

    smem, vmem = pl.BlockSpec(memory_space=pltpu.SMEM), pl.BlockSpec(memory_space=pltpu.VMEM)
    full = pl.BlockSpec((65, 32, 128), lambda i: (0, 0, 0))
    lower = pl.BlockSpec((32, 32, 128), lambda i: (0, 0, 0))
    upper = pl.BlockSpec((33, 32, 128), lambda i: (0, 0, 0))
    return pl.pallas_call(
        kernel,
        grid=(1,),
        out_shape=[jax.ShapeDtypeStruct((64, 32, 128), BF16)] + PARTS * 2,
        in_specs=[smem, smem, full] + [full, full, lower, upper] * 2,
        out_specs=[pl.BlockSpec((64, 32, 128), lambda i: (0, 0, 0))]
        + [pl.BlockSpec((1, 32, 16, 128), lambda i: (0, 0, 0, 0))] * 8,
        scratch_shapes=[
            pltpu.VMEM((65, 128, 128), BF16),
            pltpu.VMEM((65, 128, 128), BF16),
            pltpu.VMEM((64, 128, 128), F32),
        ],
        compiler_params=params(),
        cost_estimate=cost(2 * 64 * 2 * 128 * 32 * 128, 7 * 1024 * 1024),
        name="density_own",
    )(here, block_ref, coef, *gathered_y, *gathered_x)


def density_rest(weighted, halo, halo_y, halo_x, block_ref, begun):
    def kernel(ref_ref, w_ref, own, ly, hy, fy0, fy1, lx, hx, fx0, fx1, *rest):
        outs, tables = rest[8:16], rest[16:]
        pair = pl.program_id(0)

        @pl.when(pair == 0)
        def _():
            unite(tables[0], (own, ly, hy, fy0, fy1))
            unite(tables[1], (own, lx, hx, fx0, fx1))

        for v, table in enumerate(tables):
            for i in range(32):
                codes = [ref_ref[32 * v + i, 2 + 2 * pair + k] - 64 for k in range(2)]
                both = [table[jnp.clip(code, 0, 63)] for code in codes]
                for t, part in enumerate(product(w_ref[32 * v + i], *both)):
                    outs[4 * v + t][0, i] = part.astype(outs[4 * v + t].dtype)

    smem = pl.BlockSpec(memory_space=pltpu.SMEM)
    full = pl.BlockSpec((64, 32, 128), lambda i: (0, 0, 0))
    lower = pl.BlockSpec((32, 32, 128), lambda i: (0, 0, 0))
    return pl.pallas_call(
        kernel,
        grid=(3,),
        out_shape=PARTS * 2,
        in_specs=[smem, full, full] + [full, full, lower, lower] * 2 + [pl.BlockSpec(memory_space=pl.ANY)] * 8,
        out_specs=[pl.BlockSpec((1, 32, 16, 128), lambda i: (i + 1, 0, 0, 0))] * 8,
        scratch_shapes=[pltpu.VMEM((64, 128, 128), BF16)] * 2,
        input_output_aliases={11 + n: n for n in range(8)},
        compiler_params=params(),
        cost_estimate=cost(2 * 64 * 6 * 128 * 32 * 128, 10 * 1024 * 1024),
        name="density_rest",
    )(block_ref, weighted, halo, *halo_y, *halo_x, *begun)


def finish(parts, row_count):
    rows = 16

    def kernel(count_ref, *refs):
        ins, out_ref = refs[:8], refs[8]
        step = pl.program_id(0)
        for v in range(2):

            @pl.when(step // (32 // rows) == v)
            def _():
                for pair in range(4):
                    value = ins[4 * v][pair]
                    for t in range(1, 4):
                        value = value + ins[4 * v + t][pair].astype(F32)
                    for b in range(rows):
                        count = count_ref[0, step * rows + b]
                        for k in range(2):
                            part = value[b, 8 * k : 8 * k + 8]
                            out_ref[b, 2 * pair + k] = jnp.where(2 * pair + k < count, part, jnp.zeros_like(part))

    per = 32 // rows
    low = pl.BlockSpec((4, rows, 16, 128), lambda i: (0, jnp.minimum(i, per - 1), 0, 0))
    high = pl.BlockSpec((4, rows, 16, 128), lambda i: (0, jnp.maximum(i - per, 0), 0, 0))
    return pl.pallas_call(
        kernel,
        grid=(64 // rows,),
        out_shape=jax.ShapeDtypeStruct((64, 8, 8, 128), F32),
        in_specs=[pl.BlockSpec(memory_space=pltpu.SMEM)] + [low] * 4 + [high] * 4,
        out_specs=pl.BlockSpec((rows, 8, 8, 128), lambda i: (i, 0, 0, 0)),
        compiler_params=params(),
        cost_estimate=cost(0, 7 * 1024 * 1024),
        name="finish",
    )(row_count, *parts)


def plan(block_ref, row_count):
    room, none = 2 * PAIRS, 4 * PAIRS

    def kernel(ref_ref, count_ref, entry_ref, place_ref, over_ref):
        def clear(p, carry):
            entry_ref[0, p] = 0
            entry_ref[1, p] = 0
            return carry

        lax.fori_loop(0, LIST + 1, clear, 0, unroll=5)

        def row(i, lengths):
            count = count_ref[0, i]
            for k in range(2, 8):
                block = jnp.clip(ref_ref[i, k] - 64, 0, 63)
                which = block // 32
                long = jnp.where(which == 0, lengths[0], lengths[1])
                p = jnp.minimum(long, LIST)
                alive = (k < count).astype(jnp.int32)
                entry_ref[which, p] = i * 64 + block
                placed = (k < count) & (p < LIST)
                place_ref[i, k] = jnp.where(placed, which * room + 64 + p, none)
                lengths = (lengths[0] + alive * (1 - which), lengths[1] + alive * which)
            return lengths

        lengths = lax.fori_loop(0, 64, row, (jnp.int32(0), jnp.int32(0)), unroll=2)
        over_ref[0, 0] = (jnp.maximum(*lengths) > LIST).astype(jnp.int32)

    smem = pl.BlockSpec(memory_space=pltpu.SMEM)
    return pl.pallas_call(
        kernel,
        out_shape=[
            jax.ShapeDtypeStruct((2, LIST + 1), jnp.int32),
            jax.ShapeDtypeStruct((64, 8), jnp.int32),
            jax.ShapeDtypeStruct((1, 1), jnp.int32),
        ],
        in_specs=[smem, smem],
        out_specs=[smem] * 3,
        compiler_params=params(16),
        cost_estimate=cost(0, 24 * 1024 * 1024),
        name="plan",
    )(block_ref, row_count)


def targets(here_ref, v):
    x, y = here_ref[0], here_ref[1]
    for t in range(4):
        yield SIDE * lax.rem(x + t, SIDE) + y if v == 0 else SIDE * x + lax.rem(y + t, SIDE)


def weigh(v, here, shards, block_ref):
    def kernel(here_ref, ref_ref, own, lower, higher, far, w_ref, *rest):
        outs, table, turned = rest[:4], rest[4], rest[5]
        for n, piece in enumerate((own, lower, higher, far)):
            table[:, 32 * n : 32 * n + 32] = piece[0:65]
        split = table[64].astype(F32)
        occ = split[:, 0:1] + split[:, 1:2] + split[:, 2:3]
        for i in range(64):
            turned[i] = (occ * table[i].astype(F32)).astype(BF16).astype(F32).T
        starts = [pl.multiple_of(group * 8, 8) for group in targets(here_ref, v)]
        for i in range(64):
            groups = [turned[i, pl.ds(start, 8)] for start in starts]
            w_ref[i] = jnp.concatenate(groups, axis=0).astype(BF16)
        for i in range(32):
            both = [table[jnp.clip(ref_ref[32 * v + i, k], 0, 63)] for k in range(2)]
            for t, part in enumerate(product(w_ref[32 * v + i], *both)):
                outs[t][i] = part.astype(outs[t].dtype)

    smem, vmem = pl.BlockSpec(memory_space=pltpu.SMEM), pl.BlockSpec(memory_space=pltpu.VMEM)
    part = (32, 16, 128)
    return pl.pallas_call(
        kernel,
        out_shape=[jax.ShapeDtypeStruct((64, 32, 128), BF16), jax.ShapeDtypeStruct(part, F32)]
        + [jax.ShapeDtypeStruct(part, BF16)] * 3,
        in_specs=[smem, smem] + [vmem] * 4,
        out_specs=[vmem] * 5,
        scratch_shapes=[pltpu.VMEM((65, 128, 128), BF16), pltpu.VMEM((64, 128, 128), F32)],
        compiler_params=params(16),
        cost_estimate=cost(64 * 2 * 128 * 32 * 128, 4 * 1024 * 1024),
        name=f"weigh_{v}",
    )(here, block_ref, *shards)


def density_list(v, entries, weighted, shards, begun):
    def kernel(entry_ref, w_ref, own, lower, higher, far, *rest):
        begun_refs, outs, table = rest[:4], rest[4:8], rest[8]
        for n, piece in enumerate((own, lower, higher, far)):
            table[:, 32 * n : 32 * n + 32] = piece[piece.shape[0] - 32 :]
        for begun_ref, out in zip(begun_refs, outs):
            out[0:32] = begun_ref[...]
        for p in range(0, LIST, 2):
            halves = []
            for q in range(2):
                entry = entry_ref[v, p + q]
                weight, block = w_ref[lax.shift_right_logical(entry, 6)], table[entry & 31]
                halves.append(jnp.dot(weight, block, preferred_element_type=F32))
            for t, out in enumerate(outs):
                pair = jnp.concatenate([half[8 * t : 8 * t + 8] for half in halves], axis=0)
                out[32 + p // 2] = pair.astype(out.dtype)

    smem, vmem = pl.BlockSpec(memory_space=pltpu.SMEM), pl.BlockSpec(memory_space=pltpu.VMEM)
    part = (PAIRS, 16, 128)
    return pl.pallas_call(
        kernel,
        out_shape=[jax.ShapeDtypeStruct(part, F32)] + [jax.ShapeDtypeStruct(part, BF16)] * 3,
        in_specs=[smem] + [vmem] * 9,
        out_specs=[vmem] * 4,
        scratch_shapes=[pltpu.VMEM((32, 128, 128), BF16)],
        compiler_params=params(16),
        cost_estimate=cost(LIST * 2 * 128 * 32 * 128, 4 * 1024 * 1024),
        name=f"density_list_{v}",
    )(entries, weighted, *shards, *begun)


def gather_up(parts, places):
    def kernel(place_ref, *refs):
        ins, out_ref, sums = refs[:8], refs[8], refs[9]
        for v in range(2):
            value = ins[4 * v][...]
            for t in range(1, 4):
                value = value + ins[4 * v + t][...].astype(F32)
            sums[2 * PAIRS * v : 2 * PAIRS * v + 2 * PAIRS] = value.reshape(2 * PAIRS, 8, 128)
        sums[4 * PAIRS] = jnp.zeros((8, 128), F32)
        for i in range(64):
            for k in range(2):
                out_ref[i, k] = sums[2 * PAIRS * (i // 32) + 2 * (i % 32) + k]
            for k in range(2, 8):
                out_ref[i, k] = sums[place_ref[i, k]]

    smem, vmem = pl.BlockSpec(memory_space=pltpu.SMEM), pl.BlockSpec(memory_space=pltpu.VMEM)
    return pl.pallas_call(
        kernel,
        out_shape=jax.ShapeDtypeStruct((64, 8, 8, 128), F32),
        in_specs=[smem] + [vmem] * 8,
        out_specs=vmem,
        scratch_shapes=[pltpu.VMEM((4 * PAIRS + 1, 8, 128), F32)],
        compiler_params=params(16),
        cost_estimate=cost(0, 7 * 1024 * 1024),
        name="gather_up",
    )(places, *parts)


def scattered(parts_x, parts_y):
    arrived = []
    for parts, along in ((parts_x, along_x), (parts_y, along_y)):
        arrived.append(parts[0])
        arrived += [along(parts[t], t) for t in range(1, 4)]
    return arrived


def any_way(coef, halo, here, block_ref, count):
    own_y, own_x = from_far(from_beside(coef))
    halo_y, halo_x = from_far(from_beside(halo))
    weighted, *begun = density_own(here, coef, own_y, own_x, block_ref)
    parts = density_rest(weighted, halo, halo_y, halo_x, block_ref, begun)
    return finish(scattered(parts[:4], parts[4:]), count)


def body(inv_sqrt_blocks, waves, occupation, block_ref, row_count, send_list):
    send = send_list[0]
    count = row_count.reshape(1, 64)
    st = lax.axis_index("st")
    here = jnp.stack([st // SIDE, st % SIDE]).astype(jnp.int32)

    picked = pick_waves(waves, send)
    pieces = [along_dom(p, offset) for p, offset in zip(picked, OFFSETS)]
    first = coef_own(inv_sqrt_blocks, waves, block_ref)
    entries, places, over = plan(block_ref, count)
    coef, *outgoing = coef_all(
        inv_sqrt_blocks, first, pieces, block_ref, count, send, occupation.reshape(32, 1)
    )
    halos = [along_dom(p, offset) for p, offset in zip(outgoing[:3], OFFSETS)]
    halos[0], last = lax.optimization_barrier((halos[0], outgoing[3]))
    halos.append(along_dom(last, OFFSETS[3]))
    far_x = along_x(coef, 2)
    half_y, half_x = jnp.concatenate(halos[:2], axis=0), jnp.concatenate(halos[2:], axis=0)
    both_y, both_x = jnp.concatenate([coef, half_y], axis=0), jnp.concatenate([coef, half_x], axis=0)
    beside = [along_y(both_y, 1), along_y(both_y, -1), along_x(both_x, 1), along_x(both_x, -1)]
    far_y, half_far_x = along_y(both_y, 2), along_x(half_x, 2)
    far_x, entries, *beside = lax.optimization_barrier((far_x, entries, *beside))
    weighted_y, *begun_y = weigh(0, here, [coef, *beside[:2], far_y], block_ref)
    weighted_x, *begun_x = weigh(1, here, [coef, *beside[2:], far_x], block_ref)
    half_far_x, weighted_y, weighted_x = lax.optimization_barrier((half_far_x, weighted_y, weighted_x))
    parts_x = density_list(0, entries, weighted_y, [half_y, *beside[:2], far_y], begun_y)
    parts_y = density_list(1, entries, weighted_x, [half_x, *beside[2:], half_far_x], begun_x)
    density = gather_up(scattered(parts_x, parts_y), places)

    def again(density, coef, halo, *rest):
        return any_way(coef, halo, *rest)

    def keep(density, *rest):
        return density

    halo = jnp.concatenate([half_y, half_x], axis=0)
    return lax.cond(over[0, 0] > 0, again, keep, density, coef, halo, here, block_ref, count)


def solution(mesh):
    in_specs = (
        P("dom", None, None, None),
        P("st", "dom"),
        P("st"),
        P("dom", None),
        P("dom"),
        P("dom", None, None),
    )
    out_specs = P("dom", None, "st", None)
    return jax.shard_map(body, mesh=mesh, in_specs=in_specs, out_specs=out_specs, check_vma=False)
```

```python
import jax
import jax.numpy as jnp
from jax import lax
from jax.experimental import pallas as pl
from jax.experimental.pallas import tpu as pltpu
from jax.sharding import PartitionSpec as P

LIST = 144
PAIRS = 32 + LIST // 2
OFFSETS = (-2, -1, 1, 2)
SIDE = 4
BF16, F32 = jnp.bfloat16, jnp.float32


def params(mib=32):
    return pltpu.CompilerParams(vmem_limit_bytes=mib * 1024 * 1024)


def cost(flops, moved):
    return pl.CostEstimate(flops=flops, bytes_accessed=moved, transcendentals=0)


def along_dom(value, by):
    return lax.ppermute(value, "dom", [(i, (i + by) % 16) for i in range(16)])


def along_x(value, by):
    pairs = [(SIDE * x + y, SIDE * ((x + by) % SIDE) + y) for x in range(SIDE) for y in range(SIDE)]
    return lax.ppermute(value, "st", pairs)


def along_y(value, by):
    pairs = [(SIDE * x + y, SIDE * x + (y + by) % SIDE) for x in range(SIDE) for y in range(SIDE)]
    return lax.ppermute(value, "st", pairs)


def pick_waves(waves, send_list):
    def kernel(send_ref, waves_ref, *outs):
        for n in range(4):
            for j in range(16):
                block = send_ref[n, j]
                outs[n][j] = waves_ref[:, pl.ds(pl.multiple_of(block * 128, 128), 128)]

    piece = jax.ShapeDtypeStruct((16, 32, 128), BF16)
    return pl.pallas_call(
        kernel,
        out_shape=[piece] * 4,
        in_specs=[
            pl.BlockSpec(memory_space=pltpu.SMEM),
            pl.BlockSpec(memory_space=pltpu.VMEM),
        ],
        out_specs=[pl.BlockSpec(memory_space=pltpu.VMEM)] * 4,
        compiler_params=params(16),
        name="pick_waves",
    )(send_list, waves)


NT = (((1,), (1,)), ((), ()))
ROWS = 16
OWN_ROWS = 32


def coef_own(inv_sqrt_blocks, waves, block_ref):
    def kernel(ref_ref, blocks_ref, waves_ref, out_ref):
        step = pl.program_id(0)
        for b in range(OWN_ROWS):
            i = step * OWN_ROWS + b
            operand = jnp.concatenate(
                [
                    waves_ref[:, pl.ds(pl.multiple_of(ref_ref[i, k] * 128, 128), 128)]
                    for k in range(2)
                ],
                axis=1,
            )
            factor = jnp.concatenate([blocks_ref[b, 0], blocks_ref[b, 1]], axis=1)
            out_ref[b] = lax.dot_general(operand, factor, NT, preferred_element_type=F32)

    return pl.pallas_call(
        kernel,
        grid=(64 // OWN_ROWS,),
        out_shape=jax.ShapeDtypeStruct((64, 32, 128), F32),
        in_specs=[
            pl.BlockSpec(memory_space=pltpu.SMEM),
            pl.BlockSpec((OWN_ROWS, 2, 128, 128), lambda i: (i, 0, 0, 0)),
            pl.BlockSpec((32, 8192), lambda i: (0, 0)),
        ],
        out_specs=pl.BlockSpec((OWN_ROWS, 32, 128), lambda i: (i, 0, 0)),
        compiler_params=params(48),
        cost_estimate=cost(2 * 64 * 2 * 32 * 128 * 128, 6 * 1024 * 1024),
        name="coef_own",
    )(block_ref, inv_sqrt_blocks, waves)


def coef_all(inv_sqrt_blocks, first, pieces, block_ref, row_count, send_list, occupation):
    def kernel(
        ref_ref, count_ref, send_ref, blocks_1, blocks_2, blocks_3, first_ref, occ_ref,
        p0, p1, p2, p3, coef_ref, sent_y, sent_x, o0, o1, o2, o3, table,
    ):
        step = pl.program_id(0)

        @pl.when(step == 0)
        def _():
            for n, piece in enumerate((p0, p1, p2, p3)):
                table[16 * n : 16 * n + 16] = piece[...]
            lane = lax.broadcasted_iota(jnp.int32, (32, 128), 1)
            occ = jnp.broadcast_to(occ_ref[...], (32, 128))
            high = occ.astype(BF16).astype(F32)
            middle = (occ - high).astype(BF16).astype(F32)
            low = occ - high - middle
            parts = jnp.where(lane == 0, high, jnp.where(lane == 1, middle, low))
            coef_ref[64] = jnp.where(lane < 3, parts, 0.0).astype(BF16)

        for b in range(ROWS):
            i = step * ROWS + b
            operands, factors = [], []
            for slot in range(2, 8):
                block = table[jnp.clip(ref_ref[i, slot] - 64, 0, 63)]
                operands.append(jnp.where(slot < count_ref[0, i], block, jnp.zeros_like(block)))
                factors.append((blocks_1, blocks_2, blocks_3)[slot // 2 - 1][b, slot % 2])
            term = lax.dot_general(
                jnp.concatenate(factors, axis=1),
                jnp.concatenate(operands, axis=1),
                NT,
                preferred_element_type=F32,
            )
            coef_ref[i] = (first_ref[b] + term.T).astype(BF16)

        @pl.when(step == 64 // ROWS - 1)
        def _():
            for n, out in enumerate((o0, o1, o2, o3)):
                for j in range(16):
                    out[j] = coef_ref[send_ref[n, j]]
            sent_y[0:65] = coef_ref[...]
            sent_x[0:65] = coef_ref[...]

    piece = jax.ShapeDtypeStruct((16, 32, 128), BF16)
    whole = pl.BlockSpec((16, 32, 128), lambda i: (0, 0, 0))
    smem = pl.BlockSpec(memory_space=pltpu.SMEM)
    return pl.pallas_call(
        kernel,
        grid=(64 // ROWS,),
        out_shape=[jax.ShapeDtypeStruct((n, 32, 128), BF16) for n in (65, 97, 97)] + [piece] * 4,
        in_specs=[smem, smem, smem]
        + [pl.BlockSpec((ROWS, 2, 128, 128), lambda i, k=k: (i, k, 0, 0)) for k in (1, 2, 3)]
        + [
            pl.BlockSpec((ROWS, 32, 128), lambda i: (i, 0, 0)),
            pl.BlockSpec((32, 1), lambda i: (0, 0)),
        ]
        + [whole] * 4,
        out_specs=[pl.BlockSpec((n, 32, 128), lambda i: (0, 0, 0)) for n in (65, 97, 97)] + [whole] * 4,
        scratch_shapes=[pltpu.VMEM((64, 32, 128), BF16)],
        compiler_params=params(48),
        cost_estimate=cost(2 * 64 * 6 * 32 * 128 * 128, 14 * 1024 * 1024),
        name="coef_all",
    )(
        block_ref, row_count, send_list, inv_sqrt_blocks, inv_sqrt_blocks, inv_sqrt_blocks,
        first, occupation, *pieces,
    )


def from_beside(value):
    return along_y(value, 1), along_y(value, -1), along_x(value, 1), along_x(value, -1)


def from_far(beside):
    lower_y, higher_y, lower_x, higher_x = beside
    far_y = along_y(lower_y[:32], 1), along_y(higher_y[32:], -1)
    far_x = along_x(lower_x[:32], 1), along_x(higher_x[32:], -1)
    return (lower_y, higher_y, *far_y), (lower_x, higher_x, *far_x)


def unite(table, pieces):
    own, lower, higher, far_0, far_1 = pieces
    for n, piece in enumerate((own, lower, higher)):
        table[:, 32 * n : 32 * n + 32] = piece[...]
    table[0:32, 96:128] = far_0[...]
    table[32 : table.shape[0], 96:128] = far_1[...]


HALF = jax.ShapeDtypeStruct((4, 32, 16, 128), BF16)
KEPT = jax.ShapeDtypeStruct((4, 32, 16, 128), F32)
PARTS = [KEPT, HALF, HALF, HALF]


def product(weighted, low, high):
    both = jnp.dot(weighted, jnp.concatenate([low, high], axis=1), preferred_element_type=F32)
    for t in range(4):
        rows = both[8 * t : 8 * t + 8]
        yield jnp.concatenate([rows[:, :128], rows[:, 128:]], axis=0)


def density_own(here, coef, gathered_y, gathered_x, block_ref):
    def kernel(here_ref, ref_ref, own, ly, hy, fy0, fy1, lx, hx, fx0, fx1, w_ref, *rest):
        outs, tables, turned = rest[:8], rest[8:10], rest[10]
        x, y = here_ref[0], here_ref[1]
        for v, pieces in enumerate(((own, ly, hy, fy0, fy1), (own, lx, hx, fx0, fx1))):
            table = tables[v]
            unite(table, pieces)
            split = table[64].astype(F32)
            occ = split[:, 0:1] + split[:, 1:2] + split[:, 2:3]

            for i in range(32):
                mine = table[32 * v + i]
                weighted = (occ * mine.astype(F32)).astype(BF16).astype(F32)
                turned[32 * v + i] = weighted.T

            for i in range(32):
                groups = []
                for t in range(4):
                    group = SIDE * lax.rem(x + t, SIDE) + y if v == 0 else SIDE * x + lax.rem(y + t, SIDE)
                    groups.append(turned[32 * v + i, pl.ds(pl.multiple_of(group * 8, 8), 8)])
                lhs = jnp.concatenate(groups, axis=0).astype(BF16)
                w_ref[32 * v + i] = lhs
                both = [table[jnp.clip(ref_ref[32 * v + i, k], 0, 63)] for k in range(2)]
                for t, part in enumerate(product(lhs, *both)):
                    outs[4 * v + t][0, i] = part.astype(outs[4 * v + t].dtype)

    smem, vmem = pl.BlockSpec(memory_space=pltpu.SMEM), pl.BlockSpec(memory_space=pltpu.VMEM)
    full = pl.BlockSpec((65, 32, 128), lambda i: (0, 0, 0))
    lower = pl.BlockSpec((32, 32, 128), lambda i: (0, 0, 0))
    upper = pl.BlockSpec((33, 32, 128), lambda i: (0, 0, 0))
    return pl.pallas_call(
        kernel,
        grid=(1,),
        out_shape=[jax.ShapeDtypeStruct((64, 32, 128), BF16)] + PARTS * 2,
        in_specs=[smem, smem, full] + [full, full, lower, upper] * 2,
        out_specs=[pl.BlockSpec((64, 32, 128), lambda i: (0, 0, 0))]
        + [pl.BlockSpec((1, 32, 16, 128), lambda i: (0, 0, 0, 0))] * 8,
        scratch_shapes=[
            pltpu.VMEM((65, 128, 128), BF16),
            pltpu.VMEM((65, 128, 128), BF16),
            pltpu.VMEM((64, 128, 128), F32),
        ],
        compiler_params=params(),
        cost_estimate=cost(2 * 64 * 2 * 128 * 32 * 128, 7 * 1024 * 1024),
        name="density_own",
    )(here, block_ref, coef, *gathered_y, *gathered_x)


def density_rest(weighted, halo, halo_y, halo_x, block_ref, begun):
    def kernel(ref_ref, w_ref, own, ly, hy, fy0, fy1, lx, hx, fx0, fx1, *rest):
        outs, tables = rest[8:16], rest[16:]
        pair = pl.program_id(0)

        @pl.when(pair == 0)
        def _():
            unite(tables[0], (own, ly, hy, fy0, fy1))
            unite(tables[1], (own, lx, hx, fx0, fx1))

        for v, table in enumerate(tables):
            for i in range(32):
                codes = [ref_ref[32 * v + i, 2 + 2 * pair + k] - 64 for k in range(2)]
                both = [table[jnp.clip(code, 0, 63)] for code in codes]
                for t, part in enumerate(product(w_ref[32 * v + i], *both)):
                    outs[4 * v + t][0, i] = part.astype(outs[4 * v + t].dtype)

    smem = pl.BlockSpec(memory_space=pltpu.SMEM)
    full = pl.BlockSpec((64, 32, 128), lambda i: (0, 0, 0))
    lower = pl.BlockSpec((32, 32, 128), lambda i: (0, 0, 0))
    return pl.pallas_call(
        kernel,
        grid=(3,),
        out_shape=PARTS * 2,
        in_specs=[smem, full, full] + [full, full, lower, lower] * 2 + [pl.BlockSpec(memory_space=pl.ANY)] * 8,
        out_specs=[pl.BlockSpec((1, 32, 16, 128), lambda i: (i + 1, 0, 0, 0))] * 8,
        scratch_shapes=[pltpu.VMEM((64, 128, 128), BF16)] * 2,
        input_output_aliases={11 + n: n for n in range(8)},
        compiler_params=params(),
        cost_estimate=cost(2 * 64 * 6 * 128 * 32 * 128, 10 * 1024 * 1024),
        name="density_rest",
    )(block_ref, weighted, halo, *halo_y, *halo_x, *begun)


def finish(parts, row_count):
    rows = 16

    def kernel(count_ref, *refs):
        ins, out_ref = refs[:8], refs[8]
        step = pl.program_id(0)
        for v in range(2):

            @pl.when(step // (32 // rows) == v)
            def _():
                for pair in range(4):
                    value = ins[4 * v][pair]
                    for t in range(1, 4):
                        value = value + ins[4 * v + t][pair].astype(F32)
                    for b in range(rows):
                        count = count_ref[0, step * rows + b]
                        for k in range(2):
                            part = value[b, 8 * k : 8 * k + 8]
                            out_ref[b, 2 * pair + k] = jnp.where(2 * pair + k < count, part, jnp.zeros_like(part))

    per = 32 // rows
    low = pl.BlockSpec((4, rows, 16, 128), lambda i: (0, jnp.minimum(i, per - 1), 0, 0))
    high = pl.BlockSpec((4, rows, 16, 128), lambda i: (0, jnp.maximum(i - per, 0), 0, 0))
    return pl.pallas_call(
        kernel,
        grid=(64 // rows,),
        out_shape=jax.ShapeDtypeStruct((64, 8, 8, 128), F32),
        in_specs=[pl.BlockSpec(memory_space=pltpu.SMEM)] + [low] * 4 + [high] * 4,
        out_specs=pl.BlockSpec((rows, 8, 8, 128), lambda i: (i, 0, 0, 0)),
        compiler_params=params(),
        cost_estimate=cost(0, 7 * 1024 * 1024),
        name="finish",
    )(row_count, *parts)


def plan(block_ref, row_count):
    room, none = 2 * PAIRS, 4 * PAIRS

    def kernel(ref_ref, count_ref, entry_ref, place_ref, over_ref):
        def clear(p, carry):
            entry_ref[0, p] = 0
            entry_ref[1, p] = 0
            return carry

        lax.fori_loop(0, LIST + 1, clear, 0, unroll=5)

        def row(i, lengths):
            count = count_ref[0, i]
            for k in range(2, 8):
                block = jnp.clip(ref_ref[i, k] - 64, 0, 63)
                which = block // 32
                long = jnp.where(which == 0, lengths[0], lengths[1])
                p = jnp.minimum(long, LIST)
                alive = (k < count).astype(jnp.int32)
                entry_ref[which, p] = i * 64 + block
                placed = (k < count) & (p < LIST)
                place_ref[i, k] = jnp.where(placed, which * room + 64 + p, none)
                lengths = (lengths[0] + alive * (1 - which), lengths[1] + alive * which)
            return lengths

        lengths = lax.fori_loop(0, 64, row, (jnp.int32(0), jnp.int32(0)), unroll=2)
        over_ref[0, 0] = (jnp.maximum(*lengths) > LIST).astype(jnp.int32)

    smem = pl.BlockSpec(memory_space=pltpu.SMEM)
    return pl.pallas_call(
        kernel,
        out_shape=[
            jax.ShapeDtypeStruct((2, LIST + 1), jnp.int32),
            jax.ShapeDtypeStruct((64, 8), jnp.int32),
            jax.ShapeDtypeStruct((1, 1), jnp.int32),
        ],
        in_specs=[smem, smem],
        out_specs=[smem] * 3,
        compiler_params=params(16),
        cost_estimate=cost(0, 24 * 1024 * 1024),
        name="plan",
    )(block_ref, row_count)


def targets(here_ref, v):
    x, y = here_ref[0], here_ref[1]
    for t in range(4):
        yield SIDE * lax.rem(x + t, SIDE) + y if v == 0 else SIDE * x + lax.rem(y + t, SIDE)


def weigh(v, here, shards, block_ref):
    def kernel(here_ref, ref_ref, own, lower, higher, far, w_ref, *rest):
        outs, table, turned = rest[:4], rest[4], rest[5]
        for n, piece in enumerate((own, lower, higher, far)):
            table[:, 32 * n : 32 * n + 32] = piece[0:65]
        split = table[64].astype(F32)
        occ = split[:, 0:1] + split[:, 1:2] + split[:, 2:3]
        for i in range(64):
            turned[i] = (occ * table[i].astype(F32)).astype(BF16).astype(F32).T
        starts = [pl.multiple_of(group * 8, 8) for group in targets(here_ref, v)]
        for i in range(64):
            groups = [turned[i, pl.ds(start, 8)] for start in starts]
            w_ref[i] = jnp.concatenate(groups, axis=0).astype(BF16)
        for i in range(32):
            both = [table[jnp.clip(ref_ref[32 * v + i, k], 0, 63)] for k in range(2)]
            for t, part in enumerate(product(w_ref[32 * v + i], *both)):
                outs[t][i] = part.astype(outs[t].dtype)

    smem, vmem = pl.BlockSpec(memory_space=pltpu.SMEM), pl.BlockSpec(memory_space=pltpu.VMEM)
    part = (32, 16, 128)
    return pl.pallas_call(
        kernel,
        out_shape=[jax.ShapeDtypeStruct((64, 32, 128), BF16), jax.ShapeDtypeStruct(part, F32)]
        + [jax.ShapeDtypeStruct(part, BF16)] * 3,
        in_specs=[smem, smem] + [vmem] * 4,
        out_specs=[vmem] * 5,
        scratch_shapes=[pltpu.VMEM((65, 128, 128), BF16), pltpu.VMEM((64, 128, 128), F32)],
        compiler_params=params(16),
        cost_estimate=cost(64 * 2 * 128 * 32 * 128, 4 * 1024 * 1024),
        name=f"weigh_{v}",
    )(here, block_ref, *shards)


def density_list(v, entries, weighted, shards, begun):
    def kernel(entry_ref, w_ref, own, lower, higher, far, *rest):
        begun_refs, outs, table = rest[:4], rest[4:8], rest[8]
        for n, piece in enumerate((own, lower, higher, far)):
            table[:, 32 * n : 32 * n + 32] = piece[piece.shape[0] - 32 :]
        for begun_ref, out in zip(begun_refs, outs):
            out[0:32] = begun_ref[...]
        for p in range(0, LIST, 2):
            halves = []
            for q in range(2):
                entry = entry_ref[v, p + q]
                weight, block = w_ref[lax.shift_right_logical(entry, 6)], table[entry & 31]
                halves.append(jnp.dot(weight, block, preferred_element_type=F32))
            for t, out in enumerate(outs):
                pair = jnp.concatenate([half[8 * t : 8 * t + 8] for half in halves], axis=0)
                out[32 + p // 2] = pair.astype(out.dtype)

    smem, vmem = pl.BlockSpec(memory_space=pltpu.SMEM), pl.BlockSpec(memory_space=pltpu.VMEM)
    part = (PAIRS, 16, 128)
    return pl.pallas_call(
        kernel,
        out_shape=[jax.ShapeDtypeStruct(part, F32)] + [jax.ShapeDtypeStruct(part, BF16)] * 3,
        in_specs=[smem] + [vmem] * 9,
        out_specs=[vmem] * 4,
        scratch_shapes=[pltpu.VMEM((32, 128, 128), BF16)],
        compiler_params=params(16),
        cost_estimate=cost(LIST * 2 * 128 * 32 * 128, 4 * 1024 * 1024),
        name=f"density_list_{v}",
    )(entries, weighted, *shards, *begun)


def gather_up(parts, places):
    def kernel(place_ref, *refs):
        ins, out_ref, sums = refs[:8], refs[8], refs[9]
        for v in range(2):
            value = ins[4 * v][...]
            for t in range(1, 4):
                value = value + ins[4 * v + t][...].astype(F32)
            sums[2 * PAIRS * v : 2 * PAIRS * v + 2 * PAIRS] = value.reshape(2 * PAIRS, 8, 128)
        sums[4 * PAIRS] = jnp.zeros((8, 128), F32)
        for i in range(64):
            for k in range(2):
                out_ref[i, k] = sums[2 * PAIRS * (i // 32) + 2 * (i % 32) + k]
            for k in range(2, 8):
                out_ref[i, k] = sums[place_ref[i, k]]

    smem, vmem = pl.BlockSpec(memory_space=pltpu.SMEM), pl.BlockSpec(memory_space=pltpu.VMEM)
    return pl.pallas_call(
        kernel,
        out_shape=jax.ShapeDtypeStruct((64, 8, 8, 128), F32),
        in_specs=[smem] + [vmem] * 8,
        out_specs=vmem,
        scratch_shapes=[pltpu.VMEM((4 * PAIRS + 1, 8, 128), F32)],
        compiler_params=params(16),
        cost_estimate=cost(0, 7 * 1024 * 1024),
        name="gather_up",
    )(places, *parts)


def scattered(parts_x, parts_y):
    arrived = []
    for parts, along in ((parts_x, along_x), (parts_y, along_y)):
        arrived.append(parts[0])
        arrived += [along(parts[t], t) for t in range(1, 4)]
    return arrived


def any_way(coef, halo, here, block_ref, count):
    own_y, own_x = from_far(from_beside(coef))
    halo_y, halo_x = from_far(from_beside(halo))
    weighted, *begun = density_own(here, coef, own_y, own_x, block_ref)
    parts = density_rest(weighted, halo, halo_y, halo_x, block_ref, begun)
    return finish(scattered(parts[:4], parts[4:]), count)


def body(inv_sqrt_blocks, waves, occupation, block_ref, row_count, send_list):
    send = send_list[0]
    count = row_count.reshape(1, 64)
    st = lax.axis_index("st")
    here = jnp.stack([st // SIDE, st % SIDE]).astype(jnp.int32)

    picked = pick_waves(waves, send)
    pieces = [along_dom(p, offset) for p, offset in zip(picked, OFFSETS)]
    first = coef_own(inv_sqrt_blocks, waves, block_ref)
    entries, places, over = plan(block_ref, count)
    coef, sent_y, sent_x, *outgoing = coef_all(
        inv_sqrt_blocks, first, pieces, block_ref, count, send, occupation.reshape(32, 1)
    )
    halos = [along_dom(p, offset) for p, offset in zip(outgoing, OFFSETS)]
    far_x, far_y = along_x(coef, 2), along_y(coef, 2)
    sent_y = sent_y.at[65:81].set(halos[0]).at[81:97].set(halos[1])
    sent_x = sent_x.at[65:81].set(halos[2]).at[81:97].set(halos[3])
    sent_y, sent_x, far_x, far_y = lax.optimization_barrier((sent_y, sent_x, far_x, far_y))
    beside = [along_y(sent_y, 1), along_y(sent_y, -1), along_x(sent_x, 1), along_x(sent_x, -1)]
    half_y, half_x = jnp.concatenate(halos[:2], axis=0), jnp.concatenate(halos[2:], axis=0)
    half_y, half_x, entries = lax.optimization_barrier((half_y, half_x, entries))
    half_far_y, half_far_x = along_y(half_y, 2), along_x(half_x, 2)
    weighted_y, *begun_y = weigh(0, here, [coef, *beside[:2], far_y], block_ref)
    weighted_x, *begun_x = weigh(1, here, [coef, *beside[2:], far_x], block_ref)
    half_far_y, half_far_x, weighted_y, weighted_x = lax.optimization_barrier(
        (half_far_y, half_far_x, weighted_y, weighted_x)
    )
    parts_x = density_list(0, entries, weighted_y, [half_y, *beside[:2], half_far_y], begun_y)
    parts_y = density_list(1, entries, weighted_x, [half_x, *beside[2:], half_far_x], begun_x)
    density = gather_up(scattered(parts_x, parts_y), places)

    def again(density, coef, halo, *rest):
        return any_way(coef, halo, *rest)

    def keep(density, *rest):
        return density

    halo = jnp.concatenate([half_y, half_x], axis=0)
    return lax.cond(over[0, 0] > 0, again, keep, density, coef, halo, here, block_ref, count)


def solution(mesh):
    in_specs = (
        P("dom", None, None, None),
        P("st", "dom"),
        P("st"),
        P("dom", None),
        P("dom"),
        P("dom", None, None),
    )
    out_specs = P("dom", None, "st", None)
    return jax.shard_map(body, mesh=mesh, in_specs=in_specs, out_specs=out_specs, check_vma=False)
```

```python
import jax
import jax.numpy as jnp
from jax import lax
from jax.experimental import pallas as pl
from jax.experimental.pallas import tpu as pltpu
from jax.sharding import PartitionSpec as P

LIST = 144
PAIRS = 32 + LIST // 2
OFFSETS = (-2, -1, 1, 2)
SIDE = 4
BF16, F32 = jnp.bfloat16, jnp.float32


def params(mib=32):
    return pltpu.CompilerParams(vmem_limit_bytes=mib * 1024 * 1024)


def cost(flops, moved):
    return pl.CostEstimate(flops=flops, bytes_accessed=moved, transcendentals=0)


def along_dom(value, by):
    return lax.ppermute(value, "dom", [(i, (i + by) % 16) for i in range(16)])


def along_x(value, by):
    pairs = [(SIDE * x + y, SIDE * ((x + by) % SIDE) + y) for x in range(SIDE) for y in range(SIDE)]
    return lax.ppermute(value, "st", pairs)


def along_y(value, by):
    pairs = [(SIDE * x + y, SIDE * x + (y + by) % SIDE) for x in range(SIDE) for y in range(SIDE)]
    return lax.ppermute(value, "st", pairs)


def pick_waves(waves, send_list):
    def kernel(send_ref, waves_ref, *outs):
        for n in range(4):
            for j in range(16):
                block = send_ref[n, j]
                outs[n][j] = waves_ref[:, pl.ds(pl.multiple_of(block * 128, 128), 128)]

    piece = jax.ShapeDtypeStruct((16, 32, 128), BF16)
    return pl.pallas_call(
        kernel,
        out_shape=[piece] * 4,
        in_specs=[
            pl.BlockSpec(memory_space=pltpu.SMEM),
            pl.BlockSpec(memory_space=pltpu.VMEM),
        ],
        out_specs=[pl.BlockSpec(memory_space=pltpu.VMEM)] * 4,
        compiler_params=params(16),
        name="pick_waves",
    )(send_list, waves)


NT = (((1,), (1,)), ((), ()))
ROWS = 16
OWN_ROWS = 32


def coef_own(inv_sqrt_blocks, waves, block_ref):
    def kernel(ref_ref, blocks_ref, waves_ref, out_ref):
        step = pl.program_id(0)
        for b in range(OWN_ROWS):
            i = step * OWN_ROWS + b
            operand = jnp.concatenate(
                [
                    waves_ref[:, pl.ds(pl.multiple_of(ref_ref[i, k] * 128, 128), 128)]
                    for k in range(2)
                ],
                axis=1,
            )
            factor = jnp.concatenate([blocks_ref[b, 0], blocks_ref[b, 1]], axis=1)
            out_ref[b] = lax.dot_general(operand, factor, NT, preferred_element_type=F32)

    return pl.pallas_call(
        kernel,
        grid=(64 // OWN_ROWS,),
        out_shape=jax.ShapeDtypeStruct((64, 32, 128), F32),
        in_specs=[
            pl.BlockSpec(memory_space=pltpu.SMEM),
            pl.BlockSpec((OWN_ROWS, 2, 128, 128), lambda i: (i, 0, 0, 0)),
            pl.BlockSpec((32, 8192), lambda i: (0, 0)),
        ],
        out_specs=pl.BlockSpec((OWN_ROWS, 32, 128), lambda i: (i, 0, 0)),
        compiler_params=params(48),
        cost_estimate=cost(2 * 64 * 2 * 32 * 128 * 128, 6 * 1024 * 1024),
        name="coef_own",
    )(block_ref, inv_sqrt_blocks, waves)


def coef_all(inv_sqrt_blocks, first, pieces, block_ref, row_count, send_list, occupation):
    def kernel(
        ref_ref, count_ref, send_ref, blocks_1, blocks_2, blocks_3, first_ref, occ_ref,
        p0, p1, p2, p3, coef_ref, sent_y, sent_x, o0, o1, o2, o3, table,
    ):
        step = pl.program_id(0)

        @pl.when(step == 0)
        def _():
            for n, piece in enumerate((p0, p1, p2, p3)):
                table[16 * n : 16 * n + 16] = piece[...]
            lane = lax.broadcasted_iota(jnp.int32, (32, 128), 1)
            occ = jnp.broadcast_to(occ_ref[...], (32, 128))
            high = occ.astype(BF16).astype(F32)
            middle = (occ - high).astype(BF16).astype(F32)
            low = occ - high - middle
            parts = jnp.where(lane == 0, high, jnp.where(lane == 1, middle, low))
            coef_ref[64] = jnp.where(lane < 3, parts, 0.0).astype(BF16)

        for b in range(ROWS):
            i = step * ROWS + b
            operands, factors = [], []
            for slot in range(2, 8):
                block = table[jnp.clip(ref_ref[i, slot] - 64, 0, 63)]
                operands.append(jnp.where(slot < count_ref[0, i], block, jnp.zeros_like(block)))
                factors.append((blocks_1, blocks_2, blocks_3)[slot // 2 - 1][b, slot % 2])
            term = lax.dot_general(
                jnp.concatenate(factors, axis=1),
                jnp.concatenate(operands, axis=1),
                NT,
                preferred_element_type=F32,
            )
            coef_ref[i] = (first_ref[b] + term.T).astype(BF16)

        @pl.when(step == 64 // ROWS - 1)
        def _():
            for n, out in enumerate((o0, o1, o2, o3)):
                for j in range(16):
                    out[j] = coef_ref[send_ref[n, j]]
            sent_y[0:65] = coef_ref[...]
            sent_x[0:65] = coef_ref[...]

    piece = jax.ShapeDtypeStruct((16, 32, 128), BF16)
    whole = pl.BlockSpec((16, 32, 128), lambda i: (0, 0, 0))
    smem = pl.BlockSpec(memory_space=pltpu.SMEM)
    return pl.pallas_call(
        kernel,
        grid=(64 // ROWS,),
        out_shape=[jax.ShapeDtypeStruct((n, 32, 128), BF16) for n in (65, 97, 97)] + [piece] * 4,
        in_specs=[smem, smem, smem]
        + [pl.BlockSpec((ROWS, 2, 128, 128), lambda i, k=k: (i, k, 0, 0)) for k in (1, 2, 3)]
        + [
            pl.BlockSpec((ROWS, 32, 128), lambda i: (i, 0, 0)),
            pl.BlockSpec((32, 1), lambda i: (0, 0)),
        ]
        + [whole] * 4,
        out_specs=[pl.BlockSpec((n, 32, 128), lambda i: (0, 0, 0)) for n in (65, 97, 97)] + [whole] * 4,
        scratch_shapes=[pltpu.VMEM((64, 32, 128), BF16)],
        compiler_params=params(48),
        cost_estimate=cost(2 * 64 * 6 * 32 * 128 * 128, 14 * 1024 * 1024),
        name="coef_all",
    )(
        block_ref, row_count, send_list, inv_sqrt_blocks, inv_sqrt_blocks, inv_sqrt_blocks,
        first, occupation, *pieces,
    )


def from_beside(value):
    return along_y(value, 1), along_y(value, -1), along_x(value, 1), along_x(value, -1)


def from_far(beside):
    lower_y, higher_y, lower_x, higher_x = beside
    far_y = along_y(lower_y[:32], 1), along_y(higher_y[32:], -1)
    far_x = along_x(lower_x[:32], 1), along_x(higher_x[32:], -1)
    return (lower_y, higher_y, *far_y), (lower_x, higher_x, *far_x)


def unite(table, pieces):
    own, lower, higher, far_0, far_1 = pieces
    for n, piece in enumerate((own, lower, higher)):
        table[:, 32 * n : 32 * n + 32] = piece[...]
    table[0:32, 96:128] = far_0[...]
    table[32 : table.shape[0], 96:128] = far_1[...]


HALF = jax.ShapeDtypeStruct((4, 32, 16, 128), BF16)
KEPT = jax.ShapeDtypeStruct((4, 32, 16, 128), F32)
PARTS = [KEPT, HALF, HALF, HALF]


def product(weighted, low, high):
    both = jnp.dot(weighted, jnp.concatenate([low, high], axis=1), preferred_element_type=F32)
    for t in range(4):
        rows = both[8 * t : 8 * t + 8]
        yield jnp.concatenate([rows[:, :128], rows[:, 128:]], axis=0)


def density_own(here, coef, gathered_y, gathered_x, block_ref):
    def kernel(here_ref, ref_ref, own, ly, hy, fy0, fy1, lx, hx, fx0, fx1, w_ref, *rest):
        outs, tables, turned = rest[:8], rest[8:10], rest[10]
        x, y = here_ref[0], here_ref[1]
        for v, pieces in enumerate(((own, ly, hy, fy0, fy1), (own, lx, hx, fx0, fx1))):
            table = tables[v]
            unite(table, pieces)
            split = table[64].astype(F32)
            occ = split[:, 0:1] + split[:, 1:2] + split[:, 2:3]

            for i in range(32):
                mine = table[32 * v + i]
                weighted = (occ * mine.astype(F32)).astype(BF16).astype(F32)
                turned[32 * v + i] = weighted.T

            for i in range(32):
                groups = []
                for t in range(4):
                    group = SIDE * lax.rem(x + t, SIDE) + y if v == 0 else SIDE * x + lax.rem(y + t, SIDE)
                    groups.append(turned[32 * v + i, pl.ds(pl.multiple_of(group * 8, 8), 8)])
                lhs = jnp.concatenate(groups, axis=0).astype(BF16)
                w_ref[32 * v + i] = lhs
                both = [table[jnp.clip(ref_ref[32 * v + i, k], 0, 63)] for k in range(2)]
                for t, part in enumerate(product(lhs, *both)):
                    outs[4 * v + t][0, i] = part.astype(outs[4 * v + t].dtype)

    smem, vmem = pl.BlockSpec(memory_space=pltpu.SMEM), pl.BlockSpec(memory_space=pltpu.VMEM)
    full = pl.BlockSpec((65, 32, 128), lambda i: (0, 0, 0))
    lower = pl.BlockSpec((32, 32, 128), lambda i: (0, 0, 0))
    upper = pl.BlockSpec((33, 32, 128), lambda i: (0, 0, 0))
    return pl.pallas_call(
        kernel,
        grid=(1,),
        out_shape=[jax.ShapeDtypeStruct((64, 32, 128), BF16)] + PARTS * 2,
        in_specs=[smem, smem, full] + [full, full, lower, upper] * 2,
        out_specs=[pl.BlockSpec((64, 32, 128), lambda i: (0, 0, 0))]
        + [pl.BlockSpec((1, 32, 16, 128), lambda i: (0, 0, 0, 0))] * 8,
        scratch_shapes=[
            pltpu.VMEM((65, 128, 128), BF16),
            pltpu.VMEM((65, 128, 128), BF16),
            pltpu.VMEM((64, 128, 128), F32),
        ],
        compiler_params=params(),
        cost_estimate=cost(2 * 64 * 2 * 128 * 32 * 128, 7 * 1024 * 1024),
        name="density_own",
    )(here, block_ref, coef, *gathered_y, *gathered_x)


def density_rest(weighted, halo, halo_y, halo_x, block_ref, begun):
    def kernel(ref_ref, w_ref, own, ly, hy, fy0, fy1, lx, hx, fx0, fx1, *rest):
        outs, tables = rest[8:16], rest[16:]
        pair = pl.program_id(0)

        @pl.when(pair == 0)
        def _():
            unite(tables[0], (own, ly, hy, fy0, fy1))
            unite(tables[1], (own, lx, hx, fx0, fx1))

        for v, table in enumerate(tables):
            for i in range(32):
                codes = [ref_ref[32 * v + i, 2 + 2 * pair + k] - 64 for k in range(2)]
                both = [table[jnp.clip(code, 0, 63)] for code in codes]
                for t, part in enumerate(product(w_ref[32 * v + i], *both)):
                    outs[4 * v + t][0, i] = part.astype(outs[4 * v + t].dtype)

    smem = pl.BlockSpec(memory_space=pltpu.SMEM)
    full = pl.BlockSpec((64, 32, 128), lambda i: (0, 0, 0))
    lower = pl.BlockSpec((32, 32, 128), lambda i: (0, 0, 0))
    return pl.pallas_call(
        kernel,
        grid=(3,),
        out_shape=PARTS * 2,
        in_specs=[smem, full, full] + [full, full, lower, lower] * 2 + [pl.BlockSpec(memory_space=pl.ANY)] * 8,
        out_specs=[pl.BlockSpec((1, 32, 16, 128), lambda i: (i + 1, 0, 0, 0))] * 8,
        scratch_shapes=[pltpu.VMEM((64, 128, 128), BF16)] * 2,
        input_output_aliases={11 + n: n for n in range(8)},
        compiler_params=params(),
        cost_estimate=cost(2 * 64 * 6 * 128 * 32 * 128, 10 * 1024 * 1024),
        name="density_rest",
    )(block_ref, weighted, halo, *halo_y, *halo_x, *begun)


def finish(parts, row_count):
    rows = 16

    def kernel(count_ref, *refs):
        ins, out_ref = refs[:8], refs[8]
        step = pl.program_id(0)
        for v in range(2):

            @pl.when(step // (32 // rows) == v)
            def _():
                for pair in range(4):
                    value = ins[4 * v][pair]
                    for t in range(1, 4):
                        value = value + ins[4 * v + t][pair].astype(F32)
                    for b in range(rows):
                        count = count_ref[0, step * rows + b]
                        for k in range(2):
                            part = value[b, 8 * k : 8 * k + 8]
                            out_ref[b, 2 * pair + k] = jnp.where(2 * pair + k < count, part, jnp.zeros_like(part))

    per = 32 // rows
    low = pl.BlockSpec((4, rows, 16, 128), lambda i: (0, jnp.minimum(i, per - 1), 0, 0))
    high = pl.BlockSpec((4, rows, 16, 128), lambda i: (0, jnp.maximum(i - per, 0), 0, 0))
    return pl.pallas_call(
        kernel,
        grid=(64 // rows,),
        out_shape=jax.ShapeDtypeStruct((64, 8, 8, 128), F32),
        in_specs=[pl.BlockSpec(memory_space=pltpu.SMEM)] + [low] * 4 + [high] * 4,
        out_specs=pl.BlockSpec((rows, 8, 8, 128), lambda i: (i, 0, 0, 0)),
        compiler_params=params(),
        cost_estimate=cost(0, 7 * 1024 * 1024),
        name="finish",
    )(row_count, *parts)


def plan(block_ref, row_count):
    room, none = 2 * PAIRS, 4 * PAIRS

    def kernel(ref_ref, count_ref, entry_ref, place_ref, over_ref):
        def clear(p, carry):
            entry_ref[0, p] = 0
            entry_ref[1, p] = 0
            return carry

        lax.fori_loop(0, LIST + 1, clear, 0, unroll=5)

        def row(i, lengths):
            count = count_ref[0, i]
            for k in range(2, 8):
                block = jnp.clip(ref_ref[i, k] - 64, 0, 63)
                which = block // 32
                long = jnp.where(which == 0, lengths[0], lengths[1])
                p = jnp.minimum(long, LIST)
                alive = (k < count).astype(jnp.int32)
                entry_ref[which, p] = i * 64 + block
                placed = (k < count) & (p < LIST)
                place_ref[i, k] = jnp.where(placed, which * room + 64 + p, none)
                lengths = (lengths[0] + alive * (1 - which), lengths[1] + alive * which)
            return lengths

        lengths = lax.fori_loop(0, 64, row, (jnp.int32(0), jnp.int32(0)), unroll=2)
        over_ref[0, 0] = (jnp.maximum(*lengths) > LIST).astype(jnp.int32)

    smem = pl.BlockSpec(memory_space=pltpu.SMEM)
    return pl.pallas_call(
        kernel,
        out_shape=[
            jax.ShapeDtypeStruct((2, LIST + 1), jnp.int32),
            jax.ShapeDtypeStruct((64, 8), jnp.int32),
            jax.ShapeDtypeStruct((1, 1), jnp.int32),
        ],
        in_specs=[smem, smem],
        out_specs=[smem] * 3,
        compiler_params=params(16),
        cost_estimate=cost(0, 24 * 1024 * 1024),
        name="plan",
    )(block_ref, row_count)


def targets(here_ref, v):
    x, y = here_ref[0], here_ref[1]
    for t in range(4):
        yield SIDE * lax.rem(x + t, SIDE) + y if v == 0 else SIDE * x + lax.rem(y + t, SIDE)


def weigh(v, here, shards, block_ref):
    def kernel(here_ref, ref_ref, own, lower, higher, far, w_ref, *rest):
        outs, table, turned = rest[:4], rest[4], rest[5]
        for n, piece in enumerate((own, lower, higher, far)):
            table[:, 32 * n : 32 * n + 32] = piece[0:65]
        split = table[64].astype(F32)
        occ = split[:, 0:1] + split[:, 1:2] + split[:, 2:3]
        for i in range(64):
            turned[i] = (occ * table[i].astype(F32)).astype(BF16).astype(F32).T
        starts = [pl.multiple_of(group * 8, 8) for group in targets(here_ref, v)]
        for i in range(64):
            groups = [turned[i, pl.ds(start, 8)] for start in starts]
            w_ref[i] = jnp.concatenate(groups, axis=0).astype(BF16)
        for i in range(32):
            both = [table[jnp.clip(ref_ref[32 * v + i, k], 0, 63)] for k in range(2)]
            for t, part in enumerate(product(w_ref[32 * v + i], *both)):
                outs[t][i] = part.astype(outs[t].dtype)

    smem, vmem = pl.BlockSpec(memory_space=pltpu.SMEM), pl.BlockSpec(memory_space=pltpu.VMEM)
    part = (32, 16, 128)
    return pl.pallas_call(
        kernel,
        out_shape=[jax.ShapeDtypeStruct((64, 32, 128), BF16), jax.ShapeDtypeStruct(part, F32)]
        + [jax.ShapeDtypeStruct(part, BF16)] * 3,
        in_specs=[smem, smem] + [vmem] * 4,
        out_specs=[vmem] * 5,
        scratch_shapes=[pltpu.VMEM((65, 128, 128), BF16), pltpu.VMEM((64, 128, 128), F32)],
        compiler_params=params(16),
        cost_estimate=cost(64 * 2 * 128 * 32 * 128, 4 * 1024 * 1024),
        name=f"weigh_{v}",
    )(here, block_ref, *shards)


def density_list(v, entries, weighted, shards, begun):
    def kernel(entry_ref, w_ref, own, lower, higher, far, *rest):
        begun_refs, outs, table = rest[:4], rest[4:8], rest[8]
        for n, piece in enumerate((own, lower, higher, far)):
            table[:, 32 * n : 32 * n + 32] = piece[piece.shape[0] - 32 :]
        for begun_ref, out in zip(begun_refs, outs):
            out[0:32] = begun_ref[...]
        for p in range(0, LIST, 2):
            halves = []
            for q in range(2):
                entry = entry_ref[v, p + q]
                weight, block = w_ref[lax.shift_right_logical(entry, 6)], table[entry & 31]
                halves.append(jnp.dot(weight, block, preferred_element_type=F32))
            for t, out in enumerate(outs):
                pair = jnp.concatenate([half[8 * t : 8 * t + 8] for half in halves], axis=0)
                out[32 + p // 2] = pair.astype(out.dtype)

    smem, vmem = pl.BlockSpec(memory_space=pltpu.SMEM), pl.BlockSpec(memory_space=pltpu.VMEM)
    part = (PAIRS, 16, 128)
    return pl.pallas_call(
        kernel,
        out_shape=[jax.ShapeDtypeStruct(part, F32)] + [jax.ShapeDtypeStruct(part, BF16)] * 3,
        in_specs=[smem] + [vmem] * 9,
        out_specs=[vmem] * 4,
        scratch_shapes=[pltpu.VMEM((32, 128, 128), BF16)],
        compiler_params=params(16),
        cost_estimate=cost(LIST * 2 * 128 * 32 * 128, 4 * 1024 * 1024),
        name=f"density_list_{v}",
    )(entries, weighted, *shards, *begun)


def total(v, parts):
    def kernel(kept, first, second, third, out_ref):
        value = kept[...]
        for part in (first, second, third):
            value = value + part[...].astype(F32)
        out_ref[...] = value.reshape(2 * PAIRS, 8, 128)

    vmem = pl.BlockSpec(memory_space=pltpu.VMEM)
    return pl.pallas_call(
        kernel,
        out_shape=jax.ShapeDtypeStruct((2 * PAIRS, 8, 128), F32),
        in_specs=[vmem] * 4,
        out_specs=vmem,
        compiler_params=params(16),
        cost_estimate=cost(0, 3 * 1024 * 1024),
        name=f"total_{v}",
    )(*parts)


def gather_up(total_0, parts, places):
    def kernel(place_ref, *refs):
        total_ref, ins, out_ref, sums = refs[0], refs[1:5], refs[5], refs[6]
        value = ins[0][...]
        for part in ins[1:]:
            value = value + part[...].astype(F32)
        sums[0 : 2 * PAIRS] = total_ref[...]
        sums[2 * PAIRS : 4 * PAIRS] = value.reshape(2 * PAIRS, 8, 128)
        sums[4 * PAIRS] = jnp.zeros((8, 128), F32)
        for i in range(64):
            for k in range(2):
                out_ref[i, k] = sums[2 * PAIRS * (i // 32) + 2 * (i % 32) + k]
            for k in range(2, 8):
                out_ref[i, k] = sums[place_ref[i, k]]

    smem, vmem = pl.BlockSpec(memory_space=pltpu.SMEM), pl.BlockSpec(memory_space=pltpu.VMEM)
    return pl.pallas_call(
        kernel,
        out_shape=jax.ShapeDtypeStruct((64, 8, 8, 128), F32),
        in_specs=[smem] + [vmem] * 5,
        out_specs=vmem,
        scratch_shapes=[pltpu.VMEM((4 * PAIRS + 1, 8, 128), F32)],
        compiler_params=params(16),
        cost_estimate=cost(0, 7 * 1024 * 1024),
        name="gather_up",
    )(places, total_0, *parts)


def scattered(parts_x, parts_y):
    arrived = []
    for parts, along in ((parts_x, along_x), (parts_y, along_y)):
        arrived.append(parts[0])
        arrived += [along(parts[t], t) for t in range(1, 4)]
    return arrived


def any_way(coef, halo, here, block_ref, count):
    own_y, own_x = from_far(from_beside(coef))
    halo_y, halo_x = from_far(from_beside(halo))
    weighted, *begun = density_own(here, coef, own_y, own_x, block_ref)
    parts = density_rest(weighted, halo, halo_y, halo_x, block_ref, begun)
    return finish(scattered(parts[:4], parts[4:]), count)


def body(inv_sqrt_blocks, waves, occupation, block_ref, row_count, send_list):
    send = send_list[0]
    count = row_count.reshape(1, 64)
    st = lax.axis_index("st")
    here = jnp.stack([st // SIDE, st % SIDE]).astype(jnp.int32)

    picked = pick_waves(waves, send)
    pieces = [along_dom(p, offset) for p, offset in zip(picked, OFFSETS)]
    first = coef_own(inv_sqrt_blocks, waves, block_ref)
    entries, places, over = plan(block_ref, count)
    coef, sent_y, sent_x, *outgoing = coef_all(
        inv_sqrt_blocks, first, pieces, block_ref, count, send, occupation.reshape(32, 1)
    )
    halos = [along_dom(p, offset) for p, offset in zip(outgoing, OFFSETS)]
    far_x, far_y = along_x(coef, 2), along_y(coef, 2)
    sent_y = sent_y.at[65:81].set(halos[0]).at[81:97].set(halos[1])
    sent_x = sent_x.at[65:81].set(halos[2]).at[81:97].set(halos[3])
    sent_y, sent_x, far_x, far_y = lax.optimization_barrier((sent_y, sent_x, far_x, far_y))
    beside = [along_y(sent_y, 1), along_y(sent_y, -1), along_x(sent_x, 1), along_x(sent_x, -1)]
    half_y, half_x = jnp.concatenate(halos[:2], axis=0), jnp.concatenate(halos[2:], axis=0)
    half_y, half_x, entries = lax.optimization_barrier((half_y, half_x, entries))
    half_far_y, half_far_x = along_y(half_y, 2), along_x(half_x, 2)
    weighted_y, *begun_y = weigh(0, here, [coef, *beside[:2], far_y], block_ref)
    weighted_x, *begun_x = weigh(1, here, [coef, *beside[2:], far_x], block_ref)
    half_far_y, half_far_x, weighted_y, weighted_x = lax.optimization_barrier(
        (half_far_y, half_far_x, weighted_y, weighted_x)
    )
    parts_x = density_list(0, entries, weighted_y, [half_y, *beside[:2], half_far_y], begun_y)
    parts_y = density_list(1, entries, weighted_x, [half_x, *beside[2:], half_far_x], begun_x)
    arrived = scattered(parts_x, parts_y)
    density = gather_up(total(0, arrived[:4]), arrived[4:], places)

    def again(density, coef, halo, *rest):
        return any_way(coef, halo, *rest)

    def keep(density, *rest):
        return density

    halo = jnp.concatenate([half_y, half_x], axis=0)
    return lax.cond(over[0, 0] > 0, again, keep, density, coef, halo, here, block_ref, count)


def solution(mesh):
    in_specs = (
        P("dom", None, None, None),
        P("st", "dom"),
        P("st"),
        P("dom", None),
        P("dom"),
        P("dom", None, None),
    )
    out_specs = P("dom", None, "st", None)
    return jax.shard_map(body, mesh=mesh, in_specs=in_specs, out_specs=out_specs, check_vma=False)
```

```python
import jax
import jax.numpy as jnp
from jax import lax
from jax.experimental import pallas as pl
from jax.experimental.pallas import tpu as pltpu
from jax.sharding import PartitionSpec as P

LIST = 144
PAIRS = 32 + LIST // 2
OFFSETS = (-2, -1, 1, 2)
SIDE = 4
BF16, F32 = jnp.bfloat16, jnp.float32


def params(mib=32):
    return pltpu.CompilerParams(vmem_limit_bytes=mib * 1024 * 1024)


def cost(flops, moved):
    return pl.CostEstimate(flops=flops, bytes_accessed=moved, transcendentals=0)


def along_dom(value, by):
    return lax.ppermute(value, "dom", [(i, (i + by) % 16) for i in range(16)])


def along_x(value, by):
    pairs = [(SIDE * x + y, SIDE * ((x + by) % SIDE) + y) for x in range(SIDE) for y in range(SIDE)]
    return lax.ppermute(value, "st", pairs)


def along_y(value, by):
    pairs = [(SIDE * x + y, SIDE * x + (y + by) % SIDE) for x in range(SIDE) for y in range(SIDE)]
    return lax.ppermute(value, "st", pairs)


def pick_waves(waves, send_list):
    def kernel(send_ref, waves_ref, *outs):
        for n in range(4):
            for j in range(16):
                block = send_ref[n, j]
                outs[n][j] = waves_ref[:, pl.ds(pl.multiple_of(block * 128, 128), 128)]

    piece = jax.ShapeDtypeStruct((16, 32, 128), BF16)
    return pl.pallas_call(
        kernel,
        out_shape=[piece] * 4,
        in_specs=[
            pl.BlockSpec(memory_space=pltpu.SMEM),
            pl.BlockSpec(memory_space=pltpu.VMEM),
        ],
        out_specs=[pl.BlockSpec(memory_space=pltpu.VMEM)] * 4,
        compiler_params=params(16),
        name="pick_waves",
    )(send_list, waves)


NT = (((1,), (1,)), ((), ()))
ROWS = 16
OWN_ROWS = 32


def coef_own(inv_sqrt_blocks, waves, block_ref):
    def kernel(ref_ref, blocks_ref, waves_ref, out_ref):
        step = pl.program_id(0)
        for b in range(OWN_ROWS):
            i = step * OWN_ROWS + b
            operand = jnp.concatenate(
                [
                    waves_ref[:, pl.ds(pl.multiple_of(ref_ref[i, k] * 128, 128), 128)]
                    for k in range(2)
                ],
                axis=1,
            )
            factor = jnp.concatenate([blocks_ref[b, 0], blocks_ref[b, 1]], axis=1)
            out_ref[b] = lax.dot_general(operand, factor, NT, preferred_element_type=F32)

    return pl.pallas_call(
        kernel,
        grid=(64 // OWN_ROWS,),
        out_shape=jax.ShapeDtypeStruct((64, 32, 128), F32),
        in_specs=[
            pl.BlockSpec(memory_space=pltpu.SMEM),
            pl.BlockSpec((OWN_ROWS, 2, 128, 128), lambda i: (i, 0, 0, 0)),
            pl.BlockSpec((32, 8192), lambda i: (0, 0)),
        ],
        out_specs=pl.BlockSpec((OWN_ROWS, 32, 128), lambda i: (i, 0, 0)),
        compiler_params=params(48),
        cost_estimate=cost(2 * 64 * 2 * 32 * 128 * 128, 6 * 1024 * 1024),
        name="coef_own",
    )(block_ref, inv_sqrt_blocks, waves)


def coef_all(inv_sqrt_blocks, first, pieces, block_ref, row_count, send_list, occupation):
    def kernel(
        ref_ref, count_ref, send_ref, blocks_1, blocks_2, blocks_3, first_ref, occ_ref,
        p0, p1, p2, p3, coef_ref, sent_y, sent_x, o0, o1, o2, o3, table,
    ):
        step = pl.program_id(0)

        @pl.when(step == 0)
        def _():
            for n, piece in enumerate((p0, p1, p2, p3)):
                table[16 * n : 16 * n + 16] = piece[...]
            lane = lax.broadcasted_iota(jnp.int32, (32, 128), 1)
            occ = jnp.broadcast_to(occ_ref[...], (32, 128))
            high = occ.astype(BF16).astype(F32)
            middle = (occ - high).astype(BF16).astype(F32)
            low = occ - high - middle
            parts = jnp.where(lane == 0, high, jnp.where(lane == 1, middle, low))
            coef_ref[64] = jnp.where(lane < 3, parts, 0.0).astype(BF16)

        for b in range(ROWS):
            i = step * ROWS + b
            operands, factors = [], []
            for slot in range(2, 8):
                block = table[jnp.clip(ref_ref[i, slot] - 64, 0, 63)]
                operands.append(jnp.where(slot < count_ref[0, i], block, jnp.zeros_like(block)))
                factors.append((blocks_1, blocks_2, blocks_3)[slot // 2 - 1][b, slot % 2])
            term = lax.dot_general(
                jnp.concatenate(factors, axis=1),
                jnp.concatenate(operands, axis=1),
                NT,
                preferred_element_type=F32,
            )
            coef_ref[i] = (first_ref[b] + term.T).astype(BF16)

        @pl.when(step == 64 // ROWS - 1)
        def _():
            for n, out in enumerate((o0, o1, o2, o3)):
                for j in range(16):
                    out[j] = coef_ref[send_ref[n, j]]
            sent_y[0:65] = coef_ref[...]
            sent_x[0:65] = coef_ref[...]

    piece = jax.ShapeDtypeStruct((16, 32, 128), BF16)
    whole = pl.BlockSpec((16, 32, 128), lambda i: (0, 0, 0))
    smem = pl.BlockSpec(memory_space=pltpu.SMEM)
    return pl.pallas_call(
        kernel,
        grid=(64 // ROWS,),
        out_shape=[jax.ShapeDtypeStruct((n, 32, 128), BF16) for n in (65, 97, 97)] + [piece] * 4,
        in_specs=[smem, smem, smem]
        + [pl.BlockSpec((ROWS, 2, 128, 128), lambda i, k=k: (i, k, 0, 0)) for k in (1, 2, 3)]
        + [
            pl.BlockSpec((ROWS, 32, 128), lambda i: (i, 0, 0)),
            pl.BlockSpec((32, 1), lambda i: (0, 0)),
        ]
        + [whole] * 4,
        out_specs=[pl.BlockSpec((n, 32, 128), lambda i: (0, 0, 0)) for n in (65, 97, 97)] + [whole] * 4,
        scratch_shapes=[pltpu.VMEM((64, 32, 128), BF16)],
        compiler_params=params(48),
        cost_estimate=cost(2 * 64 * 6 * 32 * 128 * 128, 14 * 1024 * 1024),
        name="coef_all",
    )(
        block_ref, row_count, send_list, inv_sqrt_blocks, inv_sqrt_blocks, inv_sqrt_blocks,
        first, occupation, *pieces,
    )


def from_beside(value):
    return along_y(value, 1), along_y(value, -1), along_x(value, 1), along_x(value, -1)


def from_far(beside):
    lower_y, higher_y, lower_x, higher_x = beside
    far_y = along_y(lower_y[:32], 1), along_y(higher_y[32:], -1)
    far_x = along_x(lower_x[:32], 1), along_x(higher_x[32:], -1)
    return (lower_y, higher_y, *far_y), (lower_x, higher_x, *far_x)


def unite(table, pieces):
    own, lower, higher, far_0, far_1 = pieces
    for n, piece in enumerate((own, lower, higher)):
        table[:, 32 * n : 32 * n + 32] = piece[...]
    table[0:32, 96:128] = far_0[...]
    table[32 : table.shape[0], 96:128] = far_1[...]


HALF = jax.ShapeDtypeStruct((4, 32, 16, 128), BF16)
KEPT = jax.ShapeDtypeStruct((4, 32, 16, 128), F32)
PARTS = [KEPT, HALF, HALF, HALF]


def product(weighted, low, high):
    both = jnp.dot(weighted, jnp.concatenate([low, high], axis=1), preferred_element_type=F32)
    for t in range(4):
        rows = both[8 * t : 8 * t + 8]
        yield jnp.concatenate([rows[:, :128], rows[:, 128:]], axis=0)


def density_own(here, coef, gathered_y, gathered_x, block_ref):
    def kernel(here_ref, ref_ref, own, ly, hy, fy0, fy1, lx, hx, fx0, fx1, w_ref, *rest):
        outs, tables, turned = rest[:8], rest[8:10], rest[10]
        x, y = here_ref[0], here_ref[1]
        for v, pieces in enumerate(((own, ly, hy, fy0, fy1), (own, lx, hx, fx0, fx1))):
            table = tables[v]
            unite(table, pieces)
            split = table[64].astype(F32)
            occ = split[:, 0:1] + split[:, 1:2] + split[:, 2:3]

            for i in range(32):
                mine = table[32 * v + i]
                weighted = (occ * mine.astype(F32)).astype(BF16).astype(F32)
                turned[32 * v + i] = weighted.T

            for i in range(32):
                groups = []
                for t in range(4):
                    group = SIDE * lax.rem(x + t, SIDE) + y if v == 0 else SIDE * x + lax.rem(y + t, SIDE)
                    groups.append(turned[32 * v + i, pl.ds(pl.multiple_of(group * 8, 8), 8)])
                lhs = jnp.concatenate(groups, axis=0).astype(BF16)
                w_ref[32 * v + i] = lhs
                both = [table[jnp.clip(ref_ref[32 * v + i, k], 0, 63)] for k in range(2)]
                for t, part in enumerate(product(lhs, *both)):
                    outs[4 * v + t][0, i] = part.astype(outs[4 * v + t].dtype)

    smem, vmem = pl.BlockSpec(memory_space=pltpu.SMEM), pl.BlockSpec(memory_space=pltpu.VMEM)
    full = pl.BlockSpec((65, 32, 128), lambda i: (0, 0, 0))
    lower = pl.BlockSpec((32, 32, 128), lambda i: (0, 0, 0))
    upper = pl.BlockSpec((33, 32, 128), lambda i: (0, 0, 0))
    return pl.pallas_call(
        kernel,
        grid=(1,),
        out_shape=[jax.ShapeDtypeStruct((64, 32, 128), BF16)] + PARTS * 2,
        in_specs=[smem, smem, full] + [full, full, lower, upper] * 2,
        out_specs=[pl.BlockSpec((64, 32, 128), lambda i: (0, 0, 0))]
        + [pl.BlockSpec((1, 32, 16, 128), lambda i: (0, 0, 0, 0))] * 8,
        scratch_shapes=[
            pltpu.VMEM((65, 128, 128), BF16),
            pltpu.VMEM((65, 128, 128), BF16),
            pltpu.VMEM((64, 128, 128), F32),
        ],
        compiler_params=params(),
        cost_estimate=cost(2 * 64 * 2 * 128 * 32 * 128, 7 * 1024 * 1024),
        name="density_own",
    )(here, block_ref, coef, *gathered_y, *gathered_x)


def density_rest(weighted, halo, halo_y, halo_x, block_ref, begun):
    def kernel(ref_ref, w_ref, own, ly, hy, fy0, fy1, lx, hx, fx0, fx1, *rest):
        outs, tables = rest[8:16], rest[16:]
        pair = pl.program_id(0)

        @pl.when(pair == 0)
        def _():
            unite(tables[0], (own, ly, hy, fy0, fy1))
            unite(tables[1], (own, lx, hx, fx0, fx1))

        for v, table in enumerate(tables):
            for i in range(32):
                codes = [ref_ref[32 * v + i, 2 + 2 * pair + k] - 64 for k in range(2)]
                both = [table[jnp.clip(code, 0, 63)] for code in codes]
                for t, part in enumerate(product(w_ref[32 * v + i], *both)):
                    outs[4 * v + t][0, i] = part.astype(outs[4 * v + t].dtype)

    smem = pl.BlockSpec(memory_space=pltpu.SMEM)
    full = pl.BlockSpec((64, 32, 128), lambda i: (0, 0, 0))
    lower = pl.BlockSpec((32, 32, 128), lambda i: (0, 0, 0))
    return pl.pallas_call(
        kernel,
        grid=(3,),
        out_shape=PARTS * 2,
        in_specs=[smem, full, full] + [full, full, lower, lower] * 2 + [pl.BlockSpec(memory_space=pl.ANY)] * 8,
        out_specs=[pl.BlockSpec((1, 32, 16, 128), lambda i: (i + 1, 0, 0, 0))] * 8,
        scratch_shapes=[pltpu.VMEM((64, 128, 128), BF16)] * 2,
        input_output_aliases={11 + n: n for n in range(8)},
        compiler_params=params(),
        cost_estimate=cost(2 * 64 * 6 * 128 * 32 * 128, 10 * 1024 * 1024),
        name="density_rest",
    )(block_ref, weighted, halo, *halo_y, *halo_x, *begun)


def finish(parts, row_count):
    rows = 16

    def kernel(count_ref, *refs):
        ins, out_ref = refs[:8], refs[8]
        step = pl.program_id(0)
        for v in range(2):

            @pl.when(step // (32 // rows) == v)
            def _():
                for pair in range(4):
                    value = ins[4 * v][pair]
                    for t in range(1, 4):
                        value = value + ins[4 * v + t][pair].astype(F32)
                    for b in range(rows):
                        count = count_ref[0, step * rows + b]
                        for k in range(2):
                            part = value[b, 8 * k : 8 * k + 8]
                            out_ref[b, 2 * pair + k] = jnp.where(2 * pair + k < count, part, jnp.zeros_like(part))

    per = 32 // rows
    low = pl.BlockSpec((4, rows, 16, 128), lambda i: (0, jnp.minimum(i, per - 1), 0, 0))
    high = pl.BlockSpec((4, rows, 16, 128), lambda i: (0, jnp.maximum(i - per, 0), 0, 0))
    return pl.pallas_call(
        kernel,
        grid=(64 // rows,),
        out_shape=jax.ShapeDtypeStruct((64, 8, 8, 128), F32),
        in_specs=[pl.BlockSpec(memory_space=pltpu.SMEM)] + [low] * 4 + [high] * 4,
        out_specs=pl.BlockSpec((rows, 8, 8, 128), lambda i: (i, 0, 0, 0)),
        compiler_params=params(),
        cost_estimate=cost(0, 7 * 1024 * 1024),
        name="finish",
    )(row_count, *parts)


def plan(block_ref, row_count):
    room, none = 2 * PAIRS, 4 * PAIRS

    def kernel(ref_ref, count_ref, entry_ref, place_ref, over_ref):
        def clear(p, carry):
            entry_ref[0, p] = 0
            entry_ref[1, p] = 0
            return carry

        lax.fori_loop(0, LIST + 1, clear, 0, unroll=5)

        def row(i, lengths):
            count = count_ref[0, i]
            for k in range(2, 8):
                block = jnp.clip(ref_ref[i, k] - 64, 0, 63)
                which = block // 32
                long = jnp.where(which == 0, lengths[0], lengths[1])
                p = jnp.minimum(long, LIST)
                alive = (k < count).astype(jnp.int32)
                entry_ref[which, p] = i * 64 + block
                placed = (k < count) & (p < LIST)
                place_ref[i, k] = jnp.where(placed, which * room + 64 + p, none)
                lengths = (lengths[0] + alive * (1 - which), lengths[1] + alive * which)
            return lengths

        lengths = lax.fori_loop(0, 64, row, (jnp.int32(0), jnp.int32(0)), unroll=2)
        over_ref[0, 0] = (jnp.maximum(*lengths) > LIST).astype(jnp.int32)

    smem = pl.BlockSpec(memory_space=pltpu.SMEM)
    return pl.pallas_call(
        kernel,
        out_shape=[
            jax.ShapeDtypeStruct((2, LIST + 1), jnp.int32),
            jax.ShapeDtypeStruct((64, 8), jnp.int32),
            jax.ShapeDtypeStruct((1, 1), jnp.int32),
        ],
        in_specs=[smem, smem],
        out_specs=[smem] * 3,
        compiler_params=params(16),
        cost_estimate=cost(0, 24 * 1024 * 1024),
        name="plan",
    )(block_ref, row_count)


def targets(here_ref, v):
    x, y = here_ref[0], here_ref[1]
    for t in range(4):
        yield SIDE * lax.rem(x + t, SIDE) + y if v == 0 else SIDE * x + lax.rem(y + t, SIDE)


def weigh(v, here, shards, block_ref):
    def kernel(here_ref, ref_ref, own, lower, higher, far, w_ref, *rest):
        outs, table, turned = rest[:4], rest[4], rest[5]
        for n, piece in enumerate((own, lower, higher, far)):
            table[:, 32 * n : 32 * n + 32] = piece[0:65]
        split = table[64].astype(F32)
        occ = split[:, 0:1] + split[:, 1:2] + split[:, 2:3]
        for i in range(64):
            turned[i] = (occ * table[i].astype(F32)).astype(BF16).astype(F32).T
        starts = [pl.multiple_of(group * 8, 8) for group in targets(here_ref, v)]
        for i in range(64):
            groups = [turned[i, pl.ds(start, 8)] for start in starts]
            w_ref[i] = jnp.concatenate(groups, axis=0).astype(BF16)
        for i in range(32):
            both = [table[jnp.clip(ref_ref[32 * v + i, k], 0, 63)] for k in range(2)]
            for t, part in enumerate(product(w_ref[32 * v + i], *both)):
                outs[t][i] = part.astype(outs[t].dtype)

    smem, vmem = pl.BlockSpec(memory_space=pltpu.SMEM), pl.BlockSpec(memory_space=pltpu.VMEM)
    part = (32, 16, 128)
    return pl.pallas_call(
        kernel,
        out_shape=[jax.ShapeDtypeStruct((64, 32, 128), BF16), jax.ShapeDtypeStruct(part, F32)]
        + [jax.ShapeDtypeStruct(part, BF16)] * 3,
        in_specs=[smem, smem] + [vmem] * 4,
        out_specs=[vmem] * 5,
        scratch_shapes=[pltpu.VMEM((65, 128, 128), BF16), pltpu.VMEM((64, 128, 128), F32)],
        compiler_params=params(16),
        cost_estimate=cost(64 * 2 * 128 * 32 * 128, 4 * 1024 * 1024),
        name=f"weigh_{v}",
    )(here, block_ref, *shards)


def density_list(v, entries, weighted, shards, begun):
    def kernel(entry_ref, w_ref, own, lower, higher, far, *rest):
        begun_refs, outs, table = rest[:4], rest[4:8], rest[8]
        for n, piece in enumerate((own, lower, higher, far)):
            table[:, 32 * n : 32 * n + 32] = piece[piece.shape[0] - 32 :]
        for begun_ref, out in zip(begun_refs, outs):
            out[0:32] = begun_ref[...]
        for p in range(0, LIST, 2):
            halves = []
            for q in range(2):
                entry = entry_ref[v, p + q]
                weight, block = w_ref[lax.shift_right_logical(entry, 6)], table[entry & 31]
                halves.append(jnp.dot(weight, block, preferred_element_type=F32))
            for t, out in enumerate(outs):
                pair = jnp.concatenate([half[8 * t : 8 * t + 8] for half in halves], axis=0)
                out[32 + p // 2] = pair.astype(out.dtype)

    smem, vmem = pl.BlockSpec(memory_space=pltpu.SMEM), pl.BlockSpec(memory_space=pltpu.VMEM)
    part = (PAIRS, 16, 128)
    return pl.pallas_call(
        kernel,
        out_shape=[jax.ShapeDtypeStruct(part, F32)] + [jax.ShapeDtypeStruct(part, BF16)] * 3,
        in_specs=[smem] + [vmem] * 9,
        out_specs=[vmem] * 4,
        scratch_shapes=[pltpu.VMEM((32, 128, 128), BF16)],
        compiler_params=params(16),
        cost_estimate=cost(LIST * 2 * 128 * 32 * 128, 4 * 1024 * 1024),
        name=f"density_list_{v}",
    )(entries, weighted, *shards, *begun)


def total(v, parts):
    def kernel(kept, first, second, third, out_ref):
        value = kept[...]
        for part in (first, second, third):
            value = value + part[...].astype(F32)
        out_ref[...] = value.reshape(2 * PAIRS, 8, 128)

    vmem = pl.BlockSpec(memory_space=pltpu.VMEM)
    return pl.pallas_call(
        kernel,
        out_shape=jax.ShapeDtypeStruct((2 * PAIRS, 8, 128), F32),
        in_specs=[vmem] * 4,
        out_specs=vmem,
        compiler_params=params(16),
        cost_estimate=cost(0, 3 * 1024 * 1024),
        name=f"total_{v}",
    )(*parts)


def gather_up(total_0, parts, places):
    def kernel(place_ref, *refs):
        total_ref, ins, out_ref, sums = refs[0], refs[1:5], refs[5], refs[6]
        value = ins[0][...]
        for part in ins[1:]:
            value = value + part[...].astype(F32)
        sums[0 : 2 * PAIRS] = total_ref[...]
        sums[2 * PAIRS : 4 * PAIRS] = value.reshape(2 * PAIRS, 8, 128)
        sums[4 * PAIRS] = jnp.zeros((8, 128), F32)
        for i in range(64):
            for k in range(2):
                out_ref[i, k] = sums[2 * PAIRS * (i // 32) + 2 * (i % 32) + k]
            for k in range(2, 8):
                out_ref[i, k] = sums[place_ref[i, k]]

    smem, vmem = pl.BlockSpec(memory_space=pltpu.SMEM), pl.BlockSpec(memory_space=pltpu.VMEM)
    return pl.pallas_call(
        kernel,
        out_shape=jax.ShapeDtypeStruct((64, 8, 8, 128), F32),
        in_specs=[smem] + [vmem] * 5,
        out_specs=vmem,
        scratch_shapes=[pltpu.VMEM((4 * PAIRS + 1, 8, 128), F32)],
        compiler_params=params(16),
        cost_estimate=cost(0, 7 * 1024 * 1024),
        name="gather_up",
    )(places, total_0, *parts)


def scattered(parts_x, parts_y):
    arrived = []
    for parts, along in ((parts_x, along_x), (parts_y, along_y)):
        arrived.append(parts[0])
        arrived += [along(parts[t], t) for t in range(1, 4)]
    return arrived


def any_way(coef, halo, here, block_ref, count):
    own_y, own_x = from_far(from_beside(coef))
    halo_y, halo_x = from_far(from_beside(halo))
    weighted, *begun = density_own(here, coef, own_y, own_x, block_ref)
    parts = density_rest(weighted, halo, halo_y, halo_x, block_ref, begun)
    return finish(scattered(parts[:4], parts[4:]), count)


def body(inv_sqrt_blocks, waves, occupation, block_ref, row_count, send_list):
    send = send_list[0]
    count = row_count.reshape(1, 64)
    st = lax.axis_index("st")
    here = jnp.stack([st // SIDE, st % SIDE]).astype(jnp.int32)

    picked = pick_waves(waves, send)
    pieces = [along_dom(p, offset) for p, offset in zip(picked, OFFSETS)]
    first = coef_own(inv_sqrt_blocks, waves, block_ref)
    entries, places, over = plan(block_ref, count)
    coef, sent_y, sent_x, *outgoing = coef_all(
        inv_sqrt_blocks, first, pieces, block_ref, count, send, occupation.reshape(32, 1)
    )
    halos = [along_dom(p, offset) for p, offset in zip(outgoing, OFFSETS)]
    far_x, far_y = along_x(coef, 2), along_y(coef, 2)
    sent_y = sent_y.at[65:81].set(halos[0]).at[81:97].set(halos[1])
    sent_x = sent_x.at[65:81].set(halos[2]).at[81:97].set(halos[3])
    sent_y, sent_x, far_x, far_y = lax.optimization_barrier((sent_y, sent_x, far_x, far_y))
    beside = [along_y(sent_y, 1), along_y(sent_y, -1), along_x(sent_x, 1), along_x(sent_x, -1)]
    half_y, half_x = jnp.concatenate(halos[:2], axis=0), jnp.concatenate(halos[2:], axis=0)
    half_y, half_x, entries = lax.optimization_barrier((half_y, half_x, entries))
    half_far_y, half_far_x = along_y(half_y, 2), along_x(half_x, 2)
    weighted_y, *begun_y = weigh(0, here, [coef, *beside[:2], far_y], block_ref)
    weighted_x, *begun_x = weigh(1, here, [coef, *beside[2:], far_x], block_ref)
    half_far_y, half_far_x, weighted_y, weighted_x = lax.optimization_barrier(
        (half_far_y, half_far_x, weighted_y, weighted_x)
    )
    parts_x = density_list(0, entries, weighted_y, [half_y, *beside[:2], half_far_y], begun_y)
    parts_y = density_list(1, entries, weighted_x, [half_x, *beside[2:], half_far_x], begun_x)
    arrived = scattered(parts_x, parts_y)
    density = gather_up(total(0, arrived[:4]), arrived[4:], places)

    def again(density, coef, low, high, *rest):
        return any_way(coef, jnp.concatenate([low, high], axis=0), *rest)

    def keep(density, *rest):
        return density

    return lax.cond(over[0, 0] > 0, again, keep, density, coef, half_y, half_x, here, block_ref, count)


def solution(mesh):
    in_specs = (
        P("dom", None, None, None),
        P("st", "dom"),
        P("st"),
        P("dom", None),
        P("dom"),
        P("dom", None, None),
    )
    out_specs = P("dom", None, "st", None)
    return jax.shard_map(body, mesh=mesh, in_specs=in_specs, out_specs=out_specs, check_vma=False)
```
